32 devices in a mesh: batch: 8 (over y, x, core), seq: 4 (over z).
Axes of the slice: x: 2, y: 2, z: 4, core: 2. Of those that a mesh axis runs over, the one named last changes fastest.
Arguments:
- states: bfloat16 [64, 512, 768], P('batch', 'seq'), may hold values from -6 to 6
- lengths: int32 [64], P('batch'), may hold values from 32 to 512, as said below
- labels: int32 [64], P('batch'), may hold values from 0 to 2
- cotangent: bfloat16 [64, 512, 768], P('batch', 'seq'), may hold values from -6 to 6
- query_proj: bfloat16 [768, 768], replicated, may hold values from -0.21875 to 0.21875
- key_proj: bfloat16 [768, 768], replicated, may hold values from -0.21875 to 0.21875
- value_proj: bfloat16 [768, 768], replicated, may hold values from -0.21875 to 0.21875
- output_proj: bfloat16 [768, 768], replicated, may hold values from -0.625 to 0.625
- query_bias: bfloat16 [768], replicated, may hold values from -3 to 3
- value_bias: bfloat16 [768], replicated, may hold values from -1.1953125 to 1.1953125
- output_bias: bfloat16 [768], replicated, may hold values from -1.1953125 to 1.1953125
- first_gain: bfloat16 [768], replicated, may hold values from 0.5 to 1.5
- first_bias: bfloat16 [768], replicated, may hold values from -1.796875 to 1.796875
- inner_proj: bfloat16 [768, 3072], replicated, may hold values from -0.21875 to 0.21875
- inner_bias: bfloat16 [3072], replicated, may hold values from -3 to 3
- outer_proj: bfloat16 [3072, 768], replicated, may hold values from -0.109375 to 0.109375
- outer_bias: bfloat16 [768], replicated, may hold values from -1.1953125 to 1.1953125
- second_gain: bfloat16 [768], replicated, may hold values from 0.5 to 1.5
- second_bias: bfloat16 [768], replicated, may hold values from -1.796875 to 1.796875
- pool_proj: bfloat16 [768, 768], replicated, may hold values from -0.21875 to 0.21875
- pool_bias: bfloat16 [768], replicated, may hold values from -1.796875 to 1.796875
- class_proj: bfloat16 [768, 3], replicated, may hold values from -1 to 1
- class_bias: bfloat16 [3], replicated, may hold values from -3 to 3
Outputs:
- layer_out: bfloat16 [64, 512, 768], P('batch', 'seq')
- losses: float32 [64], P('batch')
- states_grad: bfloat16 [64, 512, 768], P('batch', 'seq')
- query_proj_grad: float32 [768, 768], replicated
- key_proj_grad: float32 [768, 768], replicated
- value_proj_grad: float32 [768, 768], replicated
- output_proj_grad: float32 [768, 768], replicated
- query_bias_grad: float32 [768], replicated
- value_bias_grad: float32 [768], replicated
- output_bias_grad: float32 [768], replicated
- first_gain_grad: float32 [768], replicated
- first_bias_grad: float32 [768], replicated
- inner_proj_grad: float32 [768, 3072], replicated
- inner_bias_grad: float32 [3072], replicated
- outer_proj_grad: float32 [3072, 768], replicated
- outer_bias_grad: float32 [768], replicated
- second_gain_grad: float32 [768], replicated
- second_bias_grad: float32 [768], replicated
- pool_proj_grad: float32 [768, 768], replicated
- pool_bias_grad: float32 [768], replicated
- class_proj_grad: float32 [768, 3], replicated
- class_bias_grad: float32 [3], replicated
The draws below stay inside these ranges and needn't reach their ends.
Inputs may be any that keep to these rules, and one draw needn't show every extreme that they name: `lengths`: in each aligned group of 8 sequences (those of one index of batch) one sequence, drawn from the seed, has exactly 512 tokens.
All inputs are finite; a program needn't handle non-finite values.
Results may differ from the reference program's by a relative error of at most 0.015.
Values may be sent and summed in bfloat16 or wider, within the bound.
A program may use at most 192 MiB of HBM per device.

```python
import jax
import jax.numpy as jnp
from jax import lax

D = 768
HEADS = 12
HEAD_DIM = 64
FF = 3072
CLASSES = 3
LEN = 512
SEQ_DEV = 8
SEQS = 64


def draw_lengths(key, part):
    key = jax.random.fold_in(key, 11)
    group_count = SEQS // SEQ_DEV
    scale_key, jitter_key, pick_key = jax.random.split(key, 3)
    halvings = jax.random.randint(scale_key, (group_count, SEQ_DEV), 0, 4)
    ceiling = jnp.right_shift(jnp.int32(LEN), halvings)
    drawn = jax.random.randint(jitter_key, (group_count, SEQ_DEV), (ceiling + 1) // 2, ceiling + 1)
    chosen = jax.random.randint(pick_key, (group_count, 1), 0, SEQ_DEV)
    full_one = jnp.arange(SEQ_DEV, dtype=jnp.int32)[None, :] == chosen
    return jnp.where(full_one, LEN, drawn).reshape(SEQS).astype(jnp.int32)


def with_ends(entries, rng, smallest, largest):
    longest = entries.shape.index(max(entries.shape))
    spots = []
    for shift in (0, 1):
        where = [jax.random.randint(jax.random.fold_in(rng, axis), (), 0, length) for axis, length in enumerate(entries.shape)]
        where[longest] = (where[longest] + shift) % entries.shape[longest]
        spots.append(tuple(where))
    return entries.at[spots[0]].set(smallest).at[spots[1]].set(largest)


def level_of(key, shape, shards, low, high):
    loudness = 1.0
    for dim, parts in shards:
        draws = jax.random.uniform(jax.random.fold_in(jax.random.fold_in(key, 6), dim), (parts,), jnp.float32, low / len(shards), high / len(shards))
        loudness = loudness * jnp.repeat(jnp.exp(draws), shape[dim] // parts).reshape((-1,) + (1,) * (len(shape) - 1 - dim))
    return loudness


def noise(own_key, extent, width, bound, pieces=(), kind=jnp.bfloat16):
    gain = level_of(own_key, extent, pieces, -0.22, 0.18) if pieces else 1.0
    entries = jax.random.normal(own_key, extent, jnp.float32) * width * gain
    return jnp.minimum(jnp.maximum(entries, -bound), bound).astype(kind)


def setup_inputs(seed: int = 0) -> dict:
    key_of = jax.random.split(jax.random.key(seed), 24)
    states = noise(key_of[0], (SEQS, LEN, D), 1.0, 6.0, ((0, 8), (1, 4)))
    lengths = draw_lengths(jax.random.fold_in(key_of[23], 71), 0)
    labels = with_ends(jax.random.randint(key_of[2], (SEQS,), 0, CLASSES), jax.random.fold_in(key_of[2], 1), 0, CLASSES - 1).astype(jnp.int32)
    cotangent = noise(key_of[3], (SEQS, LEN, D), 1.0, 6.0, ((0, 8), (1, 4)))
    query_proj = noise(key_of[4], (D, D), D ** -0.5, 0.21875)
    key_proj = noise(key_of[5], (D, D), D ** -0.5, 0.21875)
    value_proj = noise(key_of[6], (D, D), D ** -0.5, 0.21875)
    output_proj = noise(key_of[7], (D, D), (D // 8) ** -0.5, 0.625)
    query_bias = noise(key_of[8], (D,), 0.5, 3.0)
    value_bias = noise(key_of[9], (D,), 0.2, 1.1953125)
    output_bias = noise(key_of[10], (D,), 0.2, 1.1953125)
    first_gain = jnp.clip(1.0 + 0.1 * jax.random.normal(key_of[11], (D,), jnp.float32), 0.5, 1.5).astype(jnp.bfloat16)
    first_bias = noise(key_of[12], (D,), 0.3, 1.796875)
    inner_proj = noise(key_of[13], (D, FF), D ** -0.5, 0.21875)
    inner_bias = noise(key_of[14], (FF,), 0.5, 3.0)
    outer_proj = noise(key_of[15], (FF, D), FF ** -0.5, 0.109375)
    outer_bias = noise(key_of[16], (D,), 0.2, 1.1953125)
    second_gain = jnp.clip(1.0 + 0.1 * jax.random.normal(key_of[17], (D,), jnp.float32), 0.5, 1.5).astype(jnp.bfloat16)
    second_bias = noise(key_of[18], (D,), 0.3, 1.796875)
    pool_proj = noise(key_of[19], (D, D), D ** -0.5, 0.21875)
    pool_bias = noise(key_of[20], (D,), 0.3, 1.796875)
    class_proj = noise(key_of[21], (D, CLASSES), (D // 20) ** -0.5, 1.0)
    class_bias = noise(key_of[22], (CLASSES,), 1.0, 3.0)
    return {"states": states, "lengths": lengths, "labels": labels, "cotangent": cotangent, "query_proj": query_proj, "key_proj": key_proj, "value_proj": value_proj, "output_proj": output_proj, "query_bias": query_bias, "value_bias": value_bias, "output_bias": output_bias, "first_gain": first_gain, "first_bias": first_bias, "inner_proj": inner_proj, "inner_bias": inner_bias, "outer_proj": outer_proj, "outer_bias": outer_bias, "second_gain": second_gain, "second_bias": second_bias, "pool_proj": pool_proj, "pool_bias": pool_bias, "class_proj": class_proj, "class_bias": class_bias}


@jax.custom_vjp
def low(v):
    return lax.optimization_barrier(v.astype(jnp.bfloat16)).astype(jnp.float32)

@jax.custom_vjp
def low_back(v):
    return v

def low_keep(v):
    return (low(v), None)

def low_pass(kept, grad):
    return (grad,)

def back_keep(v):
    return (v, None)

def back_low(kept, grad):
    return (low(grad),)
low.defvjp(low_keep, low_pass)
low_back.defvjp(back_keep, back_low)
highest = lax.Precision.HIGHEST
norm_eps = 1e-06
masked_fill = -1e+30

def matmul(left, right):
    return jnp.dot(left, right, precision=highest)

def layer_norm(values, norm_gain, norm_bias):
    average = lax.optimization_barrier(jnp.mean(values, axis=-1, keepdims=True))
    centered = values - average
    variance = lax.optimization_barrier(jnp.mean(centered * centered, axis=-1, keepdims=True))
    return centered * lax.rsqrt(variance + norm_eps) * norm_gain + norm_bias

def one_sequence(inputs):
    query_heads, key_heads, value_heads, length = inputs
    usable = (jnp.arange(LEN, dtype=jnp.int32) < length)[None, None, :]
    scores = low_back(jnp.einsum('qhd,khd->hqk', query_heads, key_heads, precision=highest) * HEAD_DIM ** (-0.5))
    masked = jnp.where(usable, scores, masked_fill)
    row_top = lax.optimization_barrier(jnp.max(masked, axis=-1, keepdims=True))
    weights_exp = jnp.where(usable, jnp.exp(masked - row_top), 0.0)
    row_total = lax.optimization_barrier(jnp.sum(weights_exp, axis=-1))
    mixture = jnp.einsum('hqk,khd->qhd', low(weights_exp), value_heads, precision=highest)
    return mixture / jnp.transpose(row_total)[:, :, None]

def layer(weights, states, lengths, labels):
    query_proj, key_proj, value_proj, output_proj, query_bias, value_bias, output_bias, first_gain, first_bias, inner_proj, inner_bias, outer_proj, outer_bias, second_gain, second_bias, pool_proj, pool_bias, class_proj, class_bias = weights
    seq_count = states.shape[0]
    token_rows = states.reshape(seq_count * LEN, D)
    query_rows = low_back(low(matmul(token_rows, query_proj) + query_bias))
    key_rows = low_back(low(matmul(token_rows, key_proj)))
    value_rows = low_back(low(matmul(token_rows, value_proj) + value_bias))

    def heads_of(rows_flat):
        return rows_flat.reshape(seq_count, LEN, HEADS, HEAD_DIM)
    mixture = lax.map(jax.checkpoint(one_sequence), (heads_of(query_rows), heads_of(key_rows), heads_of(value_rows), lengths))
    attended = low_back(low(mixture.reshape(seq_count * LEN, D)))
    attn_out = low_back(matmul(attended, output_proj) + output_bias)
    first_out = layer_norm(token_rows + attn_out, first_gain, first_bias)
    expanded = low_back(matmul(low(first_out), inner_proj) + inner_bias)
    hidden = low(jax.nn.gelu(expanded, approximate=False))
    projected = low_back(matmul(hidden, outer_proj) + outer_bias)
    result = low(layer_norm(first_out + projected, second_gain, second_bias)).reshape(seq_count, LEN, D)
    pooled = jnp.tanh(matmul(result[:, 0, :], pool_proj) + pool_bias)
    logits = matmul(pooled, class_proj) + class_bias
    logit_top = lax.optimization_barrier(jnp.max(logits, axis=-1, keepdims=True))
    log_norm = logit_top[:, 0] + jnp.log(lax.optimization_barrier(jnp.sum(jnp.exp(logits - logit_top), axis=-1)))
    chosen = jnp.arange(CLASSES, dtype=jnp.int32)[None, :] == labels[:, None]
    losses = log_norm - lax.optimization_barrier(jnp.sum(jnp.where(chosen, logits, 0.0), axis=-1))
    return (result, losses)

def reference(states, lengths, labels, cotangent, query_proj, key_proj, value_proj, output_proj, query_bias, value_bias, output_bias, first_gain, first_bias, inner_proj, inner_bias, outer_proj, outer_bias, second_gain, second_bias, pool_proj, pool_bias, class_proj, class_bias):
    weights = tuple((matrix.astype(jnp.float32) for matrix in (query_proj, key_proj, value_proj, output_proj, query_bias, value_bias, output_bias, first_gain, first_bias, inner_proj, inner_bias, outer_proj, outer_bias, second_gain, second_bias, pool_proj, pool_bias, class_proj, class_bias)))
    groups = SEQS // SEQ_DEV
    grouped = (states.reshape(groups, SEQ_DEV, LEN, D), lengths.reshape(groups, SEQ_DEV), labels.reshape(groups, SEQ_DEV), cotangent.reshape(groups, SEQ_DEV, LEN, D))

    def one_group(totals, inputs):
        group_states, group_lengths, group_labels, group_cotangent = inputs

        def apply_layer(weight_list, state_values):
            return layer(weight_list, state_values, group_lengths, group_labels)
        (result, losses), pullback = jax.vjp(apply_layer, weights, group_states.astype(jnp.float32))
        weight_grads, state_grads = pullback((group_cotangent.astype(jnp.float32), jnp.ones_like(losses)))
        totals = tuple((running + update for running, update in zip(totals, weight_grads)))
        return (totals, (result.astype(jnp.bfloat16), losses, state_grads.astype(jnp.bfloat16)))
    initial = tuple((jnp.zeros_like(matrix) for matrix in weights))
    totals, (results, losses, states_grads) = lax.scan(one_group, initial, grouped)
    query_proj_grad, key_proj_grad, value_proj_grad, output_proj_grad, query_bias_grad, value_bias_grad, output_bias_grad, first_gain_grad, first_bias_grad, inner_proj_grad, inner_bias_grad, outer_proj_grad, outer_bias_grad, second_gain_grad, second_bias_grad, pool_proj_grad, pool_bias_grad, class_proj_grad, class_bias_grad = totals
    return (results.reshape(SEQS, LEN, D), losses.reshape(SEQS), states_grads.reshape(SEQS, LEN, D), query_proj_grad, key_proj_grad, value_proj_grad, output_proj_grad, query_bias_grad, value_bias_grad, output_bias_grad, first_gain_grad, first_bias_grad, inner_proj_grad, inner_bias_grad, outer_proj_grad, outer_bias_grad, second_gain_grad, second_bias_grad, pool_proj_grad, pool_bias_grad, class_proj_grad, class_bias_grad)
```

```python
import functools

import jax
import jax.numpy as jnp
from jax import lax
from jax.experimental import pallas as pl
from jax.experimental.pallas import tpu as pltpu
from jax.sharding import PartitionSpec as P

HEADS = 12
HEAD_DIM = 64
WIDTH = 768
HALF = 384
CHUNK = 256
MESH = pl.DeviceIdType.MESH

bf16 = jnp.bfloat16
f32 = jnp.float32
highest = lax.Precision.HIGHEST
norm_eps = 1e-06
masked_fill = -1e30
inv_root_two = 0.7071067811865476
inv_root_tau = 0.3989422804014327


def pick(code, table):
    out = table[-1]
    for i in range(len(table) - 2, -1, -1):
        out = jnp.where(code == i, table[i], out)
    return out


def flipped(index, bit):
    return index + bit * (1 - 2 * ((index // bit) % 2))


def reduce_kernel(
    chunks, pattern, lags, g_ref, small_ref, out_ref, small_out,
    acc, res, r0, r1, r2, r3, r4, sgot,
    rs_send, rs_recv, ag_send, ag_recv, loc, sm_send, sm_recv,
):
    b = lax.axis_index("batch")
    z = lax.axis_index("seq")
    core = b % 2
    got = [r0, r1, r2, r3, r4]
    near_b = [flipped(b, 2), flipped(b, 4), b, b]
    near_z = [z, z, flipped(z, 1), flipped(z, 2)]
    mine = [(b // 2) % 2, (b // 4) % 2, z % 2, (z // 2) % 2]
    orders = {"x": (0, 1, 2, 3), "y": (1, 0, 2, 3)}
    period = len(pattern)

    def direction(c, level):
        code = c % period
        dirs = [orders[p][level] for p in pattern]
        return (
            pick(code, [near_b[d] for d in dirs]),
            pick(code, [near_z[d] for d in dirs]),
            pick(code, [mine[d] for d in dirs]),
        )

    core_partner = (flipped(b, 1), z)
    barrier = pltpu.get_barrier_semaphore()
    partners = [core_partner] + [(near_b[d], near_z[d]) for d in range(4)]
    for who in partners:
        pl.semaphore_signal(barrier, inc=1, device_id=who, device_id_type=MESH)
    pl.semaphore_wait(barrier, len(partners))

    def base(c, level):
        rows = 0
        size = CHUNK
        for l in range(level):
            size = size // 2
            rows = rows + direction(c, l)[2] * size
        return pl.multiple_of(rows, 16)

    def g_rows(c):
        return pl.ds(pl.multiple_of(c * CHUNK, CHUNK), CHUNK)

    my_cols = pl.ds(pl.multiple_of(core * HALF, HALF), HALF)
    other_cols = pl.ds(pl.multiple_of((1 - core) * HALF, HALF), HALF)

    def rs_copy(c, s):
        if s == 0:
            return pltpu.make_async_remote_copy(
                g_ref.at[g_rows(c), other_cols], r0.at[c], rs_send.at[0, c], rs_recv.at[0, c],
                device_id=core_partner, device_id_type=MESH,
            )
        size = CHUNK >> s
        nb, nz, m = direction(c, s - 1)
        start = pl.multiple_of(base(c, s - 1) + (1 - m) * size, 16)
        return pltpu.make_async_remote_copy(
            acc.at[c, pl.ds(start, size)], got[s].at[c], rs_send.at[s, c], rs_recv.at[s, c],
            device_id=(nb, nz), device_id_type=MESH,
        )

    def ag_copy(c, s):
        if s == 0:
            return pltpu.make_async_remote_copy(
                res.at[c], out_ref.at[g_rows(c), my_cols], ag_send.at[0, c], ag_recv.at[0, c],
                device_id=core_partner, device_id_type=MESH,
            )
        size = CHUNK >> s
        nb, nz, _ = direction(c, s - 1)
        start = base(c, s)
        return pltpu.make_async_remote_copy(
            res.at[c, pl.ds(start, size)], res.at[c, pl.ds(start, size)],
            ag_send.at[s, c], ag_recv.at[s, c], device_id=(nb, nz), device_id_type=MESH,
        )

    def loc_in(c):
        return pltpu.make_async_copy(g_ref.at[g_rows(c), my_cols], acc.at[c], loc.at[0, c])

    def loc_out(c):
        return pltpu.make_async_copy(res.at[c], out_ref.at[g_rows(c), my_cols], loc.at[1, c])

    def stage_first(c):
        rs_copy(c, 0).start()
        loc_in(c).start()

    def stage_scatter(s, c):
        rs_copy(c, s - 1).wait_recv()
        if s == 1:
            loc_in(c).wait()
        half = CHUNK >> s
        start = base(c, s - 1)
        m = direction(c, s - 1)[2]
        for which in (0, 1):
            off = pl.multiple_of(((1 - m) if which == 0 else m) * half, 16)
            rows = pl.ds(pl.multiple_of(start + off, 16), half)
            acc[c, rows] = acc[c, rows] + got[s - 1][c, pl.ds(off, half)]
            if which == 0:
                rs_copy(c, s).start()

    def stage_turn(c):
        rs_copy(c, 4).wait_recv()
        rows = pl.ds(base(c, 4), 16)
        res[c, rows] = acc[c, rows] + r4[c]
        ag_copy(c, 4).start()

    def stage_gather(s, c):
        ag_copy(c, s + 1).wait_recv()
        ag_copy(c, s).start()
        if s == 0:
            loc_out(c).start()

    def stage_last(c):
        ag_copy(c, 0).wait_recv()
        loc_out(c).wait()
        for s in range(5):
            rs_copy(c, s).wait_send()
            ag_copy(c, s).wait_send()

    stages = (
        [stage_first]
        + [functools.partial(stage_scatter, s) for s in (1, 2, 3, 4)]
        + [stage_turn]
        + [functools.partial(stage_gather, s) for s in (3, 2, 1, 0)]
        + [stage_last]
    )

    def small_copy(i):
        return pltpu.make_async_remote_copy(
            small_out, sgot.at[i], sm_send.at[i], sm_recv.at[i],
            device_id=partners[i], device_id_type=MESH,
        )

    small_out[...] = small_ref[...]

    def tick(t, carry):
        for i in range(len(partners) + 1):

            @pl.when(t == 3 * i)
            def _():
                if i > 0:
                    small_copy(i - 1).wait()
                    small_out[...] = small_out[...] + sgot[i - 1]
                if i < len(partners):
                    small_copy(i).start()

        for stage, lag in reversed(list(zip(stages, lags))):
            c = t - lag

            @pl.when((c >= 0) & (c < chunks))
            def _():
                stage(c)

        return carry

    lax.fori_loop(0, chunks + lags[-1], tick, 0)


def reduce_all(g, small):
    rows = g.shape[0]
    if lax.axis_size("batch") != 8 or lax.axis_size("seq") != 4:
        return lax.psum(g.astype(f32), ("batch", "seq")), lax.psum(small, ("batch", "seq"))
    chunks = rows // CHUNK
    dma = pltpu.SemaphoreType.DMA
    return pl.pallas_call(
        functools.partial(reduce_kernel, chunks, "xy", tuple(3 * i for i in range(11))),
        out_shape=(
            jax.ShapeDtypeStruct(g.shape, bf16),
            jax.ShapeDtypeStruct(small.shape, f32),
        ),
        in_specs=[pl.BlockSpec(memory_space=pl.ANY), pl.BlockSpec(memory_space=pltpu.VMEM)],
        out_specs=(pl.BlockSpec(memory_space=pl.ANY), pl.BlockSpec(memory_space=pltpu.VMEM)),
        scratch_shapes=[
            pltpu.VMEM((chunks, CHUNK, HALF), bf16),
            pltpu.VMEM((chunks, CHUNK, HALF), bf16),
            pltpu.VMEM((chunks, CHUNK, HALF), bf16),
            pltpu.VMEM((chunks, CHUNK // 2, HALF), bf16),
            pltpu.VMEM((chunks, CHUNK // 4, HALF), bf16),
            pltpu.VMEM((chunks, CHUNK // 8, HALF), bf16),
            pltpu.VMEM((chunks, CHUNK // 16, HALF), bf16),
            pltpu.VMEM((5,) + small.shape, f32),
            dma((5, chunks)),
            dma((5, chunks)),
            dma((5, chunks)),
            dma((5, chunks)),
            dma((2, chunks)),
            dma((5,)),
            dma((5,)),
        ],
        compiler_params=pltpu.CompilerParams(
            collective_id=0, has_side_effects=True, vmem_limit_bytes=56 * 2**20
        ),
    )(g, small)


def shifted(block, distance):
    count = lax.axis_size("seq")
    route = [(i, (i + distance) % count) for i in range(count)]
    return lax.ppermute(block, "seq", route)


def to_sequences(block):
    count = lax.axis_size("seq")
    position = lax.axis_index("seq")
    seqs, tokens, width = block.shape
    parts = block.reshape(count, seqs // count, tokens, width)
    out = jnp.zeros((seqs // count, count, tokens, width), block.dtype)
    for distance in range(count):
        part = lax.dynamic_index_in_dim(parts, (position + distance) % count, 0, keepdims=False)
        if distance:
            part = shifted(part, distance)
        out = lax.dynamic_update_slice(
            out, part[:, None], (0, (position - distance) % count, 0, 0)
        )
    return out.reshape(seqs // count, count * tokens, width)


def to_tokens(block):
    count = lax.axis_size("seq")
    position = lax.axis_index("seq")
    seqs, tokens, width = block.shape
    parts = block.reshape(seqs, count, tokens // count, width)
    out = jnp.zeros((count, seqs, tokens // count, width), block.dtype)
    for distance in range(count):
        part = lax.dynamic_index_in_dim(parts, (position + distance) % count, 1, keepdims=False)
        if distance:
            part = shifted(part, distance)
        out = lax.dynamic_update_slice(out, part[None], ((position - distance) % count, 0, 0, 0))
    return out.reshape(count * seqs, tokens // count, width)


def project(left, right):
    return jnp.dot(left, right, preferred_element_type=f32)


def project_left(left, right):
    return jnp.einsum("ti,to->io", left, right, preferred_element_type=f32)


def project_right(left, right):
    return jnp.einsum("to,io->ti", left, right, preferred_element_type=f32)


def normalize(values, norm_gain, norm_bias):
    average = jnp.mean(values, axis=-1, keepdims=True)
    centered = values - average
    variance = jnp.mean(centered * centered, axis=-1, keepdims=True)
    inv_root = lax.rsqrt(variance + norm_eps)
    normed = centered * inv_root
    return (normed * norm_gain + norm_bias, normed, inv_root)


def normalize_back(upstream, normed, inv_root, norm_gain):
    gain_grad = jnp.sum(upstream * normed, axis=0)
    bias_grad = jnp.sum(upstream, axis=0)
    scaled = upstream * norm_gain
    centred_part = scaled - jnp.mean(scaled, axis=-1, keepdims=True)
    input_grad = inv_root * (
        centred_part - normed * jnp.mean(scaled * normed, axis=-1, keepdims=True)
    )
    return (input_grad, gain_grad, bias_grad)


def gelu_pair(expanded):
    cumulative = 0.5 * (1.0 + lax.erf(expanded * inv_root_two))
    density = jnp.exp(-0.5 * expanded * expanded) * inv_root_tau
    return (expanded * cumulative, cumulative + expanded * density)


def exit_head(cls_state, labels, pool_proj, pool_bias, class_proj, class_bias):
    pool_full = pool_proj.astype(f32)
    class_full = class_proj.astype(f32)
    pooled = jnp.tanh(jnp.dot(cls_state, pool_full, precision=highest) + pool_bias.astype(f32))
    logits = jnp.dot(pooled, class_full, precision=highest) + class_bias.astype(f32)
    logit_top = jnp.max(logits, axis=-1, keepdims=True)
    log_norm = logit_top + jnp.log(jnp.sum(jnp.exp(logits - logit_top), axis=-1, keepdims=True))
    classes = jnp.arange(class_proj.shape[1], dtype=jnp.int32)
    chosen = (classes[None, :] == labels[:, None]).astype(f32)
    losses = log_norm[:, 0] - jnp.sum(chosen * logits, axis=-1)
    logit_grad = jnp.exp(logits - log_norm) - chosen
    pre_grad = jnp.dot(logit_grad, class_full.T, precision=highest) * (1.0 - pooled * pooled)
    return pooled, losses, logit_grad, pre_grad


def local(
    states, lengths, labels, cotangent,
    query_proj, key_proj, value_proj, output_proj,
    query_bias, value_bias, output_bias, first_gain, first_bias,
    inner_proj, inner_bias, outer_proj, outer_bias, second_gain, second_bias,
    pool_proj, pool_bias, class_proj, class_bias,
):
    group, block_len, width = states.shape
    count = lax.axis_size("seq")
    position = lax.axis_index("seq")
    lane = lax.axis_index("batch")
    seqs = group // count
    length = block_len * count
    rows = seqs * length
    x = to_sequences(states).reshape(rows, width)
    upstream = to_sequences(cotangent).reshape(rows, width)
    own_lengths = lax.dynamic_slice_in_dim(lengths, position * seqs, seqs)
    own_labels = lax.dynamic_slice_in_dim(labels, position * seqs, seqs)

    queries = (project(x, query_proj) + query_bias).astype(bf16)
    keys = project(x, key_proj).astype(bf16)
    values = (project(x, value_proj) + value_bias).astype(bf16)

    def heads_of(flat):
        return flat.reshape(seqs, length, HEADS, HEAD_DIM)

    scaling = HEAD_DIM ** (-0.5)
    scores = (
        jnp.einsum("sqhd,skhd->shqk", heads_of(queries), heads_of(keys), preferred_element_type=f32)
        * scaling
    )
    usable = (jnp.arange(length, dtype=jnp.int32)[None, :] < own_lengths[:, None])[:, None, None, :]
    masked = jnp.where(usable, scores, masked_fill)
    row_top = jnp.max(masked, axis=-1, keepdims=True)
    weights_exp = jnp.where(usable, jnp.exp(masked - row_top), 0.0)
    row_total = jnp.sum(weights_exp, axis=-1, keepdims=True)
    weights_low = weights_exp.astype(bf16)
    mixture = jnp.einsum(
        "shqk,skhd->shqd", weights_low, heads_of(values), preferred_element_type=f32
    )
    attended = jnp.transpose(mixture / row_total, (0, 2, 1, 3)).reshape(rows, width)
    attended_low = attended.astype(bf16)
    attn_out = project(attended_low, output_proj) + output_bias
    first_gain_f = first_gain.astype(f32)
    second_gain_f = second_gain.astype(f32)
    first_out, first_normed, first_inv = normalize(
        x.astype(f32) + attn_out, first_gain_f, first_bias.astype(f32)
    )
    first_low = first_out.astype(bf16)
    expanded = project(first_low, inner_proj) + inner_bias
    activated, gelu_slope = gelu_pair(expanded)
    hidden = activated.astype(bf16)
    projected = project(hidden, outer_proj) + outer_bias
    second_out, second_normed, second_inv = normalize(
        first_out + projected, second_gain_f, second_bias.astype(f32)
    )
    layer_rows = second_out.astype(bf16)
    layer_full = layer_rows.reshape(seqs, length, width)
    layer_out = to_tokens(layer_full)

    cls_own = layer_full[:, 0, :]
    pre_own = exit_head(
        cls_own.astype(f32), own_labels, pool_proj, pool_bias, class_proj, class_bias
    )[3]
    cls_grad = jnp.dot(pre_own, pool_proj.astype(f32).T, precision=highest)
    cls_all = lax.all_gather(cls_own, ("batch", "seq"), axis=0, tiled=True).astype(f32)
    labels_all = lax.all_gather(labels, "batch", axis=0, tiled=True)
    pooled, losses_all, logit_grad, pre_grad = exit_head(
        cls_all, labels_all, pool_proj, pool_bias, class_proj, class_bias
    )
    losses = lax.dynamic_slice_in_dim(losses_all, lane * group, group)
    class_bias_grad = jnp.sum(logit_grad, axis=0)
    class_proj_grad = jnp.dot(pooled.T, logit_grad, precision=highest)
    pool_bias_grad = jnp.sum(pre_grad, axis=0)
    pool_proj_grad = jnp.dot(cls_all.T, pre_grad, precision=highest)

    out_grad = (
        upstream.astype(f32).reshape(seqs, length, width).at[:, 0, :].add(cls_grad)
    ).reshape(rows, width)
    second_z_grad, second_gain_grad, second_bias_grad = normalize_back(
        out_grad, second_normed, second_inv, second_gain_f
    )
    projected_grad = second_z_grad.astype(bf16)
    outer_proj_grad = project_left(hidden, projected_grad)
    outer_bias_grad = jnp.sum(projected_grad.astype(f32), axis=0)
    expanded_grad = (project_right(projected_grad, outer_proj) * gelu_slope).astype(bf16)
    inner_proj_grad = project_left(first_low, expanded_grad)
    inner_bias_grad = jnp.sum(expanded_grad.astype(f32), axis=0)
    first_grad = second_z_grad + project_right(expanded_grad, inner_proj)
    first_z_grad, first_gain_grad, first_bias_grad = normalize_back(
        first_grad, first_normed, first_inv, first_gain_f
    )
    attn_grad = first_z_grad.astype(bf16)
    output_proj_grad = project_left(attended_low, attn_grad)
    output_bias_grad = jnp.sum(attn_grad.astype(f32), axis=0)
    attended_grad = project_right(attn_grad, output_proj).astype(bf16)
    delta = jnp.sum(
        heads_of(attended_grad).astype(f32) * heads_of(attended), axis=-1
    )
    delta = jnp.transpose(delta, (0, 2, 1))[..., None]
    probs = weights_exp / row_total
    prob_grad = jnp.einsum(
        "sqhd,skhd->shqk", heads_of(attended_grad), heads_of(values), preferred_element_type=f32
    )
    score_grad = (probs * (prob_grad - delta)).astype(bf16)
    value_rows = (
        jnp.einsum(
            "shqk,sqhd->skhd", probs.astype(bf16), heads_of(attended_grad),
            preferred_element_type=f32,
        )
        .astype(bf16)
        .reshape(rows, width)
    )
    query_rows = (
        (
            jnp.einsum("shqk,skhd->sqhd", score_grad, heads_of(keys), preferred_element_type=f32)
            * scaling
        )
        .astype(bf16)
        .reshape(rows, width)
    )
    key_rows = (
        (
            jnp.einsum("shqk,sqhd->skhd", score_grad, heads_of(queries), preferred_element_type=f32)
            * scaling
        )
        .astype(bf16)
        .reshape(rows, width)
    )
    query_bias_grad = jnp.sum(query_rows.astype(f32), axis=0)
    value_bias_grad = jnp.sum(value_rows.astype(f32), axis=0)
    states_grad = to_tokens(
        (
            first_z_grad
            + project_right(query_rows, query_proj)
            + project_right(key_rows, key_proj)
            + project_right(value_rows, value_proj)
        )
        .astype(bf16)
        .reshape(seqs, length, width)
    )
    outer_block = outer_proj_grad.astype(bf16)
    inner_block = (
        inner_proj_grad.astype(bf16).reshape(width, 4, width).transpose(1, 0, 2).reshape(-1, width)
    )
    g = jnp.concatenate(
        [outer_block, inner_block, output_proj_grad.astype(bf16)]
        + [project_left(x, r).astype(bf16) for r in (query_rows, key_rows, value_rows)]
    )
    small = jnp.concatenate(
        [
            query_bias_grad[None], value_bias_grad[None], output_bias_grad[None],
            first_gain_grad[None], first_bias_grad[None], outer_bias_grad[None],
            second_gain_grad[None], second_bias_grad[None],
            inner_bias_grad.reshape(4, width), jnp.zeros((4, width), f32),
        ]
    )
    total, small = reduce_all(g, small)
    total = total.astype(f32).reshape(12, width, width)
    outer_total = total[0:4].reshape(4 * width, width)
    inner_total = total[4:8].transpose(1, 0, 2).reshape(width, 4 * width)
    return (
        layer_out, losses, states_grad,
        total[9], total[10], total[11], total[8],
        small[0], small[1], small[2], small[3], small[4],
        inner_total, small[8:12].reshape(-1), outer_total, small[5], small[6], small[7],
        pool_proj_grad, pool_bias_grad, class_proj_grad, class_bias_grad,
    )


def solution(mesh):
    split = P("batch", "seq", None)
    in_specs = (split, P("batch"), P("batch"), split) + (P(),) * 19
    out_specs = (split, P("batch"), split) + (P(),) * 19
    return jax.shard_map(local, mesh=mesh, in_specs=in_specs, out_specs=out_specs, check_vma=False)
```

```python
import functools

import jax
import jax.numpy as jnp
from jax import lax
from jax.experimental import pallas as pl
from jax.experimental.pallas import tpu as pltpu
from jax.sharding import PartitionSpec as P

HEADS = 12
HEAD_DIM = 64
WIDTH = 768
HALF = 384
CHUNK = 256
MESH = pl.DeviceIdType.MESH

bf16 = jnp.bfloat16
f32 = jnp.float32
highest = lax.Precision.HIGHEST
norm_eps = 1e-06
masked_fill = -1e30
inv_root_two = 0.7071067811865476
inv_root_tau = 0.3989422804014327


def pick(code, table):
    out = table[-1]
    for i in range(len(table) - 2, -1, -1):
        out = jnp.where(code == i, table[i], out)
    return out


def flipped(index, bit):
    return index + bit * (1 - 2 * ((index // bit) % 2))


NT = (((1,), (1,)), ((), ()))
NN = (((1,), (0,)), ((), ()))
TN = (((0,), (0,)), ((), ()))
VECS = 24
QB, VB, OB, G1, B1, IB, UB, G2, B2, PB, CP, CB = 0, 1, 2, 3, 4, 5, 9, 10, 11, 12, 13, 16


def dot(left, right, dims=NN):
    return lax.dot_general(left, right, dims, preferred_element_type=f32)


def gelu_parts(u):
    t = 1.0 / (1.0 + (0.3275911 * inv_root_two) * jnp.abs(u))
    bell = jnp.exp(-0.5 * u * u)
    poly = 1.061405429
    for coefficient in (-1.453152027, 1.421413741, -0.284496736, 0.254829592):
        poly = poly * t + coefficient
    tail = (0.5 * t) * poly * bell
    cumulative = jnp.where(u >= 0.0, 1.0 - tail, tail)
    return u * cumulative, cumulative + u * (bell * inv_root_tau)


def norm_rows(z):
    average = jnp.mean(z, axis=-1, keepdims=True)
    centered = z - average
    inv_root = lax.rsqrt(jnp.mean(centered * centered, axis=-1, keepdims=True) + norm_eps)
    return centered * inv_root, inv_root


def norm_rows_back(upstream, normed, inv_root, gain):
    scaled = upstream * gain
    return inv_root * (
        scaled
        - jnp.mean(scaled, axis=-1, keepdims=True)
        - normed * jnp.mean(scaled * normed, axis=-1, keepdims=True)
    )


def tile(i, size):
    return pl.ds(pl.multiple_of(i * size, size), size)


def copies(pairs, sems):
    out = []
    for i, (src, dst) in enumerate(pairs):
        out.append(pltpu.make_async_copy(src, dst, sems.at[i]))
    return out


def head_lanes(which):
    lane = lax.broadcasted_iota(jnp.int32, (1, 128), 1)
    return (lane >= 64) if which else (lane < 64)


def only(mask, block):
    return jnp.where(mask, block, jnp.zeros_like(block))


def attend_pair(q2, k2, v2, length, keys):
    k2 = k2[:keys]
    v2 = v2[:keys]
    place = lax.broadcasted_iota(jnp.int32, (1, keys), 1)
    out = None
    logs = []
    for which in (0, 1):
        lanes = head_lanes(which)
        scores = dot(only(lanes, q2) * bf16(0.125), k2, NT)
        scores = jnp.where(place < length, scores, masked_fill)
        top = jnp.max(scores, axis=-1, keepdims=True)
        weights = jnp.exp(scores - top)
        total = jnp.sum(weights, axis=-1, keepdims=True)
        part = dot(weights.astype(bf16), only(lanes, v2)) * (1.0 / total)
        out = part if out is None else out + part
        logs.append(top + jnp.log(total))
    return out, logs


def spread(src, dst, seqs, tokens, to_rows, sends, recvs, base, s):
    count = lax.axis_size("seq")
    b = lax.axis_index("batch")
    z = lax.axis_index("seq")
    out = []
    for d in range(1, count):
        other = lax.rem(z + d, count)
        if to_rows:
            source = src.at[other * seqs + s]
            target = dst.at[pl.ds(pl.multiple_of((s * count + z) * tokens, tokens), tokens)]
        else:
            source = src.at[pl.ds(pl.multiple_of((s * count + other) * tokens, tokens), tokens)]
            target = dst.at[z * seqs + s]
        i = base + s * (count - 1) + d - 1
        out.append(
            pltpu.make_async_remote_copy(
                source, target, sends.at[i], recvs.at[i],
                device_id=(b, other), device_id_type=MESH,
            )
        )
    return out


def own_part(src, dst, seqs, tokens, to_rows, sem, s):
    count = lax.axis_size("seq")
    z = lax.axis_index("seq")
    block = z * seqs + s
    rows = pl.ds(pl.multiple_of((s * count + z) * tokens, tokens), tokens)
    if to_rows:
        return pltpu.make_async_copy(src.at[block], dst.at[rows], sem)
    return pltpu.make_async_copy(src.at[rows], dst.at[block], sem)


def greet_line():
    count = lax.axis_size("seq")
    z = lax.axis_index("seq")
    return [(lax.axis_index("batch"), lax.rem(z + d, count)) for d in range(1, count)]


def forward_kernel(
    seqs, len_ref, states, cot, wq, wk, wv, wo, w1, w2,
    query_bias, value_bias, output_bias, first_gain, first_bias, inner_bias, outer_bias,
    second_gain, second_bias, pool_bias, class_proj, class_bias,
    vec_ref, x_out, cot_out, q_out, k_out, v_out, att_out, n1_out, low_out, hid_out, slope_out,
    n2_out, stat_out, y_out,
    x_s, wq_s, wk_s, wv_s, wo_s, w1_s, w2_s,
    q_s, k_s, v_s, att_s, n1_s, low_s, hid_s, slope_s, n2_s, stat_s, y_s, z_s,
    in_sem, out_sem, own_sem, sends, recvs,
):
    rows = z_s.shape[0]
    tokens = states.shape[1]
    line = greet_line()
    barrier = pltpu.get_barrier_semaphore()
    for who in line:
        pl.semaphore_signal(barrier, inc=1, device_id=who, device_id_type=MESH)
    weights_in = copies(
        [(wq, wq_s), (wk, wk_s), (wv, wv_s), (wo, wo_s), (w1, w1_s), (w2, w2_s)], in_sem
    )
    own = []
    for s in range(seqs):
        own.append(own_part(states, x_s, seqs, tokens, True, own_sem.at[s], s))
        own.append(own_part(cot, cot_out, seqs, tokens, True, own_sem.at[seqs + s], s))
    for copy in own + weights_in:
        copy.start()
    pl.semaphore_wait(barrier, len(line))
    moves = [spread(states, x_s, seqs, tokens, True, sends, recvs, 0, s) for s in range(seqs)]
    late = [
        spread(cot, cot_out, seqs, tokens, True, sends, recvs, seqs * len(line), s)
        for s in range(seqs)
    ]
    for group in moves + late:
        for copy in group:
            copy.start()
    vec_ref[...] = jnp.zeros_like(vec_ref)
    for i, ref in (
        (QB, query_bias), (VB, value_bias), (OB, output_bias), (G1, first_gain), (B1, first_bias),
        (UB, outer_bias), (G2, second_gain), (B2, second_bias), (PB, pool_bias),
    ):
        vec_ref[i : i + 1, :] = ref[...].astype(f32).reshape(1, WIDTH)
    for i in range(4):
        vec_ref[IB + i : IB + i + 1, :] = (
            inner_bias[i * WIDTH : (i + 1) * WIDTH].astype(f32).reshape(1, WIDTH)
        )
    eye = (
        lax.broadcasted_iota(jnp.int32, (8, 3), 0) == lax.broadcasted_iota(jnp.int32, (8, 3), 1)
    ).astype(bf16)
    vec_ref[CP : CP + 3, :] = dot(eye, class_proj[...], NT)[0:3, :]
    vec_ref[CB : CB + 1, 0:3] = class_bias[...].astype(f32).reshape(1, 3)

    z = lax.axis_index("seq")
    waiting = []
    for s in range(seqs):
        for copy in moves[s]:
            copy.wait_recv()
        own[2 * s].wait()
        part = pl.ds(s * rows, rows)
        waiting += forward_rows(
            s, part, len_ref[z * seqs + s], rows, s == 0, vec_ref, weights_in,
            (x_s, wq_s, wk_s, wv_s, wo_s, w1_s, w2_s, q_s, k_s, v_s, att_s, n1_s, low_s, hid_s,
             slope_s, n2_s, stat_s, y_s, z_s),
            (x_out, q_out, k_out, v_out, att_out, n1_out, low_out, hid_out, slope_out, n2_out,
             stat_out, y_out),
            out_sem,
        )
    for group in moves:
        for copy in group:
            copy.wait_send()
    for group in late:
        for copy in group:
            copy.wait()
    for s in range(seqs):
        own[2 * s + 1].wait()
    for copy in waiting:
        copy.wait()


def forward_rows(s, part, length, rows, first_time, vec_ref, weights_in, scratch, outs, out_sem):
    (x_s, wq_s, wk_s, wv_s, wo_s, w1_s, w2_s, q_s, k_s, v_s, att_s, n1_s, low_s, hid_s,
     slope_s, n2_s, stat_s, y_s, z_s) = scratch
    start = s * rows
    out = [
        pltpu.make_async_copy(src.at[part], dst.at[part], out_sem.at[s, i])
        for i, (src, dst) in enumerate(
            zip((x_s, q_s, k_s, v_s, att_s, n1_s, low_s, hid_s, slope_s, n2_s, stat_s, y_s), outs)
        )
    ]
    out[0].start()
    for i, (w, dst, bias) in enumerate(((wq_s, q_s, QB), (wk_s, k_s, None), (wv_s, v_s, VB))):
        if first_time:
            weights_in[i].wait()

        @pl.loop(0, WIDTH // 256)
        def _(j):
            cols = tile(j, 256)
            grid = dot(x_s[part, :], w[:, cols])
            if bias is not None:
                grid = grid + vec_ref[bias : bias + 1, cols]
            dst[part, cols] = grid.astype(bf16)

        out[1 + i].start()

    stat_s[part, :] = jnp.zeros((rows, 128), f32)
    lane = lax.broadcasted_iota(jnp.int32, (1, 128), 1)

    @pl.loop(0, HEADS // 2)
    def _(p):
        cols = tile(p, 128)
        mix, logs = attend_pair(q_s[part, cols], k_s[part, cols], v_s[part, cols], length, rows)
        att_s[part, cols] = mix.astype(bf16)
        stat_s[part, :] = jnp.where(
            lane == 2 * p, logs[0], jnp.where(lane == 2 * p + 1, logs[1], stat_s[part, :])
        )

    out[4].start()
    if first_time:
        weights_in[3].wait()

    @pl.loop(0, WIDTH // 256)
    def _(j):
        cols = tile(j, 256)
        z_s[:, cols] = (
            x_s[part, cols].astype(f32)
            + dot(att_s[part, :], wo_s[:, cols])
            + vec_ref[OB : OB + 1, cols]
        )

    @pl.loop(0, rows // 128)
    def _(i):
        r = tile(i, 128)
        q = pl.ds(pl.multiple_of(start + i * 128, 128), 128)
        normed, inv_root = norm_rows(z_s[r, :])
        n1_s[q, :] = normed.astype(bf16)
        first = normed * vec_ref[G1 : G1 + 1, :] + vec_ref[B1 : B1 + 1, :]
        low_s[q, :] = first.astype(bf16)
        z_s[r, :] = first + vec_ref[UB : UB + 1, :]
        stat_s[q, :] = jnp.where(lane == 12, inv_root, stat_s[q, :])

    out[5].start()
    out[6].start()
    if first_time:
        weights_in[4].wait()
        weights_in[5].wait()
    ft = 256

    @pl.loop(0, 4 * WIDTH // ft)
    def _(j):
        cols = tile(j, ft)
        u = dot(low_s[part, :], w1_s[:, cols]) + vec_ref[pl.ds(IB + j // 3, 1), tile(j % 3, ft)]
        h, slope = gelu_parts(u)
        hid_s[part, cols] = h.astype(bf16)
        slope_s[part, cols] = slope.astype(bf16)

    out[7].start()
    out[8].start()

    @pl.loop(0, WIDTH // 256)
    def _(j):
        cols = tile(j, 256)
        z_s[:, cols] += dot(hid_s[part, :], w2_s[:, cols])

    @pl.loop(0, rows // 128)
    def _(i):
        r = tile(i, 128)
        q = pl.ds(pl.multiple_of(start + i * 128, 128), 128)
        normed, inv_root = norm_rows(z_s[r, :])
        n2_s[q, :] = normed.astype(bf16)
        y_s[q, :] = (normed * vec_ref[G2 : G2 + 1, :] + vec_ref[B2 : B2 + 1, :]).astype(bf16)
        stat_s[q, :] = jnp.where(lane == 13, inv_root, stat_s[q, :])

    for i in (9, 10, 11):
        out[i].start()
    return out


def forward(lengths, states, cotangent, weights, small):
    count = lax.axis_size("seq")
    group, tokens, width = states.shape
    seqs = group // count
    one = count * tokens
    rows = seqs * one
    ff = 4 * width
    anywhere = pl.BlockSpec(memory_space=pl.ANY)
    in_vmem = pl.BlockSpec(memory_space=pltpu.VMEM)
    saved = [((rows, width), bf16)] * 6 + [((rows, ff), bf16)] * 2 + [
        ((rows, width), bf16), ((rows, 128), f32), ((rows, width), bf16),
    ]
    outs = [((VECS, width), f32), ((rows, width), bf16), ((rows, width), bf16)] + saved
    moves = 2 * seqs * (count - 1)
    flops = 2 * rows * width * (4 * width + 2 * ff) + 4 * rows * one * width
    dma = pltpu.SemaphoreType.DMA
    return pl.pallas_call(
        functools.partial(forward_kernel, seqs),
        out_shape=tuple(jax.ShapeDtypeStruct(s, t) for s, t in outs),
        in_specs=[pl.BlockSpec(memory_space=pltpu.SMEM)] + [anywhere] * 8 + [in_vmem] * len(small),
        out_specs=(in_vmem,) + (anywhere,) * (len(outs) - 1),
        scratch_shapes=[pltpu.VMEM((rows, width), bf16)]
        + [pltpu.VMEM(w.shape, bf16) for w in weights]
        + [pltpu.VMEM(s, t) for s, t in saved]
        + [
            pltpu.VMEM((one, width), f32), dma((6,)), dma((seqs, 12)), dma((2 * seqs,)),
            dma((moves,)), dma((moves,)),
        ],
        compiler_params=pltpu.CompilerParams(
            collective_id=1, has_side_effects=True, vmem_limit_bytes=60 * 2**20
        ),
        cost_estimate=pl.CostEstimate(
            flops=flops, bytes_accessed=50 * 2**20, transcendentals=rows * (ff + 12 * one)
        ),
        name="forward",
    )(lengths, states, cotangent, *weights, *small)


def exit_back(cls_rows, labels, vec_ref, pool_s):
    pooled = jnp.tanh(dot(cls_rows, pool_s[...]) + vec_ref[PB : PB + 1, :])
    class_rows = vec_ref[CP : CP + 3, :]
    logits = [
        jnp.sum(pooled * class_rows[i : i + 1, :], axis=-1, keepdims=True)
        + vec_ref[CB : CB + 1, i : i + 1]
        for i in range(3)
    ]
    top = jnp.maximum(jnp.maximum(logits[0], logits[1]), logits[2])
    raised = [jnp.exp(l - top) for l in logits]
    total = raised[0] + raised[1] + raised[2]
    back = jnp.zeros_like(pooled)
    for i in range(3):
        back = back + (raised[i] / total - (labels == i).astype(f32)) * class_rows[i : i + 1, :]
    pre = back * (1.0 - pooled * pooled)
    high = pre.astype(bf16)
    rest = pre - high.astype(f32)
    mid = rest.astype(bf16)
    low = (rest - mid.astype(f32)).astype(bf16)
    return dot(high, pool_s[...], NT) + dot(mid, pool_s[...], NT) + dot(low, pool_s[...], NT)


def ffn_back_kernel(
    seqs, label_ref, vec_ref, cot, n2, hid, slope, low, n1, stat, y, w1, w2, pool,
    g_out, ag_out, sums_out, head_out,
    cot_s, n2_s, hid_s, slope_s, low_s, n1_s, stat_s, cls_s, w1_s, w2_s, pool_s,
    pg_s, fg_s, eg_s, gst, ag_s, row_s, in_sem, out_sem,
):
    rows = cot_s.shape[0]
    one = rows // seqs
    cls_in = [
        pltpu.make_async_copy(
            y.at[pl.ds(s * one, 16)], cls_s.at[pl.ds(s * 16, 16)], in_sem.at[10 + s]
        )
        for s in range(seqs)
    ]
    loads = copies(
        [
            (pool, pool_s), (cot, cot_s), (n2, n2_s), (stat, stat_s), (w2, w2_s), (hid, hid_s),
            (slope, slope_s), (low, low_s), (w1, w1_s), (n1, n1_s),
        ],
        in_sem,
    )
    for copy in cls_in + loads:
        copy.start()
    for copy in cls_in:
        copy.wait()
    loads[0].wait()
    z = lax.axis_index("seq")
    place = lax.broadcasted_iota(jnp.int32, (16 * seqs, 1), 0)
    labels = jnp.zeros((16 * seqs, 1), jnp.int32)
    label_row = jnp.zeros((1, 128), f32)
    lane = lax.broadcasted_iota(jnp.int32, (1, 128), 1)
    for s in range(seqs):
        label = label_ref[z * seqs + s]
        labels = jnp.where(place == 16 * s, label, labels)
        label_row = jnp.where(lane == s, label.astype(f32), label_row)
    cls_grad = exit_back(cls_s[...], labels, vec_ref, pool_s)
    row_s[...] = jnp.zeros_like(row_s)
    for s in range(seqs):
        first = cls_s[16 * s : 16 * (s + 1), :].astype(f32)
        for j in range(6):
            row_s[s * 6 + j : s * 6 + j + 1, :] = first[0:1, j * 128 : (j + 1) * 128]
    row_s[12:13, :] = label_row
    head_out[...] = row_s[...].astype(bf16)
    for copy in loads[1:4]:
        copy.wait()
    sums_out[...] = jnp.zeros_like(sums_out)
    ROW = 128

    def add_sum(index, block):
        sums_out[index : index + 1, :] += jnp.sum(block, axis=0, keepdims=True)

    @pl.loop(0, rows // ROW)
    def _(i):
        r = tile(i, ROW)
        upstream = cot_s[r, :].astype(f32)
        place = lax.broadcasted_iota(jnp.int32, (ROW, 1), 0) + i * ROW
        for s in range(seqs):
            upstream = upstream + jnp.where(place == s * one, cls_grad[16 * s : 16 * s + 1, :], 0.0)
        normed = n2_s[r, :].astype(f32)
        add_sum(G2, upstream * normed)
        add_sum(B2, upstream)
        zg = norm_rows_back(upstream, normed, stat_s[r, 13:14], vec_ref[G2 : G2 + 1, :])
        low = zg.astype(bf16)
        pg_s[r, :] = low
        add_sum(UB, low.astype(f32))
        fg_s[r, :] = zg

    for copy in loads[4:9]:
        copy.wait()

    def g_copy(slot, unit):
        return pltpu.make_async_copy(gst.at[slot], g_out.at[unit], out_sem.at[slot])

    for j in range(4):

        @pl.loop(0, WIDTH // 256)
        def _(t):
            cols = tile(t, 256)
            ff = pl.ds(pl.multiple_of(j * WIDTH + t * 256, 256), 256)
            grad = dot(pg_s[...], w2_s[ff, :], NT) * slope_s[:, ff].astype(f32)
            low = grad.astype(bf16)
            eg_s[:, cols] = low
            sums_out[IB + j : IB + j + 1, cols] = jnp.sum(low.astype(f32), axis=0, keepdims=True)

        if j > 0:
            g_copy(0, j - 1).wait()

        @pl.loop(0, WIDTH // 256)
        def _(t):
            ff = pl.ds(pl.multiple_of(j * WIDTH + t * 256, 256), 256)
            gst[0, tile(t, 256), :] = dot(hid_s[:, ff], pg_s[...], TN).astype(bf16)

        g_copy(0, j).start()
        if j > 0:
            g_copy(1, 4 + j - 1).wait()

        @pl.loop(0, WIDTH // 256)
        def _(t):
            gst[1, tile(t, 256), :] = dot(low_s[:, tile(t, 256)], eg_s[...], TN).astype(bf16)

        g_copy(1, 4 + j).start()

        @pl.loop(0, WIDTH // 256)
        def _(t):
            cols = tile(t, 256)
            fg_s[:, cols] += dot(eg_s[...], w1_s[cols, j * WIDTH : (j + 1) * WIDTH], NT)

    loads[9].wait()

    @pl.loop(0, rows // ROW)
    def _(i):
        r = tile(i, ROW)
        upstream = fg_s[r, :]
        normed = n1_s[r, :].astype(f32)
        add_sum(G1, upstream * normed)
        add_sum(B1, upstream)
        zg = norm_rows_back(upstream, normed, stat_s[r, 12:13], vec_ref[G1 : G1 + 1, :])
        low = zg.astype(bf16)
        ag_s[r, :] = low
        add_sum(OB, low.astype(f32))

    ag_copy = pltpu.make_async_copy(ag_s, ag_out, out_sem.at[2])
    ag_copy.start()
    g_copy(0, 3).wait()
    g_copy(1, 7).wait()
    ag_copy.wait()


def ffn_back(seqs, labels, vecs, saved, w1, w2, pool):
    rows, width = saved[0].shape
    ff = 4 * width
    anywhere = pl.BlockSpec(memory_space=pl.ANY)
    in_vmem = pl.BlockSpec(memory_space=pltpu.VMEM)
    wide = pltpu.VMEM((rows, width), bf16)
    return pl.pallas_call(
        functools.partial(ffn_back_kernel, seqs),
        out_shape=(
            jax.ShapeDtypeStruct((12, width, width), bf16),
            jax.ShapeDtypeStruct((rows, width), bf16),
            jax.ShapeDtypeStruct((16, width), f32),
            jax.ShapeDtypeStruct((16, 128), bf16),
        ),
        in_specs=[pl.BlockSpec(memory_space=pltpu.SMEM), in_vmem] + [anywhere] * (len(saved) + 3),
        out_specs=(anywhere, anywhere, in_vmem, in_vmem),
        scratch_shapes=[
            wide, wide, pltpu.VMEM((rows, ff), bf16), pltpu.VMEM((rows, ff), bf16), wide, wide,
            pltpu.VMEM((rows, 128), f32), pltpu.VMEM((16 * seqs, width), bf16),
            pltpu.VMEM(w1.shape, bf16), pltpu.VMEM(w2.shape, bf16), pltpu.VMEM(pool.shape, bf16),
            wide, pltpu.VMEM((rows, width), f32), wide, pltpu.VMEM((2, width, width), bf16), wide,
            pltpu.VMEM((16, 128), f32),
            pltpu.SemaphoreType.DMA((10 + seqs,)), pltpu.SemaphoreType.DMA((3,)),
        ],
        compiler_params=pltpu.CompilerParams(vmem_limit_bytes=58 * 2**20),
        cost_estimate=pl.CostEstimate(
            flops=8 * rows * width * ff, bytes_accessed=45 * 2**20, transcendentals=0
        ),
        name="ffn_back",
    )(labels, vecs, *saved, w1, w2, pool)


def attend_back_pair(q2, k2, v2, d2, logs, delta, length, keys):
    k2 = k2[:keys]
    v2 = v2[:keys]
    usable = lax.broadcasted_iota(jnp.int32, (keys, 1), 0) < length
    dq = dk = dv = None
    for which in (0, 1):
        lanes = head_lanes(which)
        qh = only(lanes, q2) * bf16(0.125)
        dh = only(lanes, d2)
        kh = only(lanes, k2) * bf16(0.125)
        scores = dot(k2, qh, NT)
        probs = jnp.where(usable, jnp.exp(scores - logs[which]), 0.0)
        prob_grad = dot(v2, dh, NT)
        score_grad = (probs * (prob_grad - delta[which])).astype(bf16)
        parts = (
            dot(score_grad, kh, TN),
            dot(score_grad, qh),
            dot(probs.astype(bf16), dh),
        )
        if dq is None:
            dq, dk, dv = parts
        else:
            dq, dk, dv = dq + parts[0], dk + parts[1], dv + parts[2]
    return dq, dk, dv


def attn_back_kernel(
    seqs, len_ref, ag_ref, g_in, q, k, v, att, x, stat, wq, wk, wv, wo,
    g_out, sg_out, sums_out,
    q_s, k_s, v_s, att_s, x_s, stat_s, wq_s, wk_s, wv_s, wo_s,
    dat_s, dq_s, dk_s, dv_s, rowt_s, gst, sg_s, in_sem, out_sem,
):
    rows = ag_ref.shape[0]
    one = rows // seqs
    z = lax.axis_index("seq")
    loads = copies(
        [
            (wo, wo_s), (att, att_s), (q, q_s), (k, k_s), (v, v_s), (stat, stat_s),
            (x, x_s), (wq, wq_s), (wk, wk_s), (wv, wv_s),
        ],
        in_sem,
    )
    for copy in loads:
        copy.start()
    loads[0].wait()

    @pl.loop(0, WIDTH // 256)
    def _(t):
        cols = tile(t, 256)
        dat_s[:, cols] = dot(ag_ref[...], wo_s[cols, :], NT).astype(bf16)

    def g_copy(unit):
        return pltpu.make_async_copy(gst.at[unit], g_out.at[8 + unit], out_sem.at[unit])

    loads[1].wait()

    @pl.loop(0, WIDTH // 256)
    def _(t):
        gst[0, tile(t, 256), :] = dot(att_s[:, tile(t, 256)], ag_ref[...], TN).astype(bf16)

    g_copy(0).start()
    for copy in loads[2:6]:
        copy.wait()
    head_of = lax.broadcasted_iota(jnp.int32, (16, WIDTH), 1) // HEAD_DIM
    picker = (head_of == lax.broadcasted_iota(jnp.int32, (16, WIDTH), 0)).astype(bf16)
    for s in range(seqs):
        part = pl.ds(s * one, one)
        product = dat_s[part, :].astype(f32) * att_s[part, :].astype(f32)
        high = product.astype(bf16)
        low = (product - high.astype(f32)).astype(bf16)
        rowt_s[s, 128:144, :] = dot(picker, high, NT) + dot(picker, low, NT)
        rowt_s[s, 0:128, :] = jnp.transpose(stat_s[part, :])
        length = len_ref[z * seqs + s]
        step = one // 4
        for n in range(4):
            keys = (n + 1) * step

            @pl.when((length > n * step) & (length <= (n + 1) * step))
            def _():
                @pl.loop(0, HEADS // 2)
                def _(p):
                    cols = tile(p, 128)
                    logs = [rowt_s[s, pl.ds(2 * p + w, 1), :] for w in (0, 1)]
                    delta = [rowt_s[s, pl.ds(128 + 2 * p + w, 1), :] for w in (0, 1)]
                    dq, dk, dv = attend_back_pair(
                        q_s[part, cols], k_s[part, cols], v_s[part, cols], dat_s[part, cols],
                        logs, delta, length, keys,
                    )
                    dq_s[part, cols] = dq.astype(bf16)
                    dk_s[pl.ds(s * one, keys), cols] = dk.astype(bf16)
                    dv_s[pl.ds(s * one, keys), cols] = dv.astype(bf16)
                    if keys < one:
                        rest = pl.ds(s * one + keys, one - keys)
                        dk_s[rest, cols] = jnp.zeros((one - keys, 128), bf16)
                        dv_s[rest, cols] = jnp.zeros((one - keys, 128), bf16)

    for copy in loads[6:]:
        copy.wait()

    @pl.loop(0, WIDTH // 256)
    def _(t):
        cols = tile(t, 256)
        total = ag_ref[:, cols].astype(f32)
        for d, w in ((dq_s, wq_s), (dk_s, wk_s), (dv_s, wv_s)):
            total = total + dot(d[...], w[cols, :], NT)
        sg_s[:, cols] = total.astype(bf16)
        sums_out[0:1, cols] = jnp.sum(dq_s[:, cols].astype(f32), axis=0, keepdims=True)
        sums_out[1:2, cols] = jnp.sum(dv_s[:, cols].astype(f32), axis=0, keepdims=True)
        sums_out[2:8, cols] = jnp.zeros((6, 256), f32)

    sg_copy = pltpu.make_async_copy(sg_s, sg_out, out_sem.at[4])
    sg_copy.start()
    for i, d in enumerate((dq_s, dk_s, dv_s)):

        @pl.loop(0, WIDTH // 256)
        def _(t):
            gst[1 + i, tile(t, 256), :] = dot(x_s[:, tile(t, 256)], d[...], TN).astype(bf16)

        g_copy(1 + i).start()
    for unit in range(4):
        g_copy(unit).wait()
    sg_copy.wait()


def attn_back(seqs, lengths, ag, g, saved, weights):
    rows, width = ag.shape
    one = rows // seqs
    anywhere = pl.BlockSpec(memory_space=pl.ANY)
    in_vmem = pl.BlockSpec(memory_space=pltpu.VMEM)
    wide = pltpu.VMEM((rows, width), bf16)
    square = pltpu.VMEM((width, width), bf16)
    return pl.pallas_call(
        functools.partial(attn_back_kernel, seqs),
        out_shape=(
            jax.ShapeDtypeStruct(g.shape, bf16),
            jax.ShapeDtypeStruct((rows, width), bf16),
            jax.ShapeDtypeStruct((8, width), f32),
        ),
        in_specs=[pl.BlockSpec(memory_space=pltpu.SMEM), in_vmem] + [anywhere] * (len(saved) + 5),
        out_specs=(anywhere, anywhere, in_vmem),
        input_output_aliases={2: 0},
        scratch_shapes=[wide] * 5
        + [pltpu.VMEM((rows, 128), f32)]
        + [square] * 4
        + [wide] * 4
        + [
            pltpu.VMEM((seqs, 144, one), f32), pltpu.VMEM((4, width, width), bf16), wide,
            pltpu.SemaphoreType.DMA((10,)), pltpu.SemaphoreType.DMA((5,)),
        ],
        compiler_params=pltpu.CompilerParams(vmem_limit_bytes=56 * 2**20),
        cost_estimate=pl.CostEstimate(
            flops=16 * rows * width * width + 10 * rows * one * width,
            bytes_accessed=25 * 2**20, transcendentals=12 * rows * one,
        ),
        name="attn_back",
    )(lengths, ag, g, *saved, *weights)


def place_of_block():
    return (lax.axis_index("batch") % 8) * 4 + lax.axis_index("seq")


def sum_kernel(
    seqs, chunks, pattern, lags, g_ref, small_ref, head_ref, y_ref, sg_ref,
    out_ref, small_out, head_out, lay_out, grad_out,
    acc, res, r0, r1, r2, r3, r4, sgot,
    rs_send, rs_recv, ag_send, ag_recv, loc, sm_send, sm_recv, hd_send, hd_recv,
    tok_send, tok_recv, tok_own,
):
    b = lax.axis_index("batch")
    z = lax.axis_index("seq")
    core = b % 2
    got = [r0, r1, r2, r3, r4]
    near_b = [flipped(b, 2), flipped(b, 4), b, b]
    near_z = [z, z, flipped(z, 1), flipped(z, 2)]
    mine = [(b // 2) % 2, (b // 4) % 2, z % 2, (z // 2) % 2]
    orders = {"x": (0, 1, 2, 3), "y": (1, 0, 2, 3)}
    period = len(pattern)

    def direction(c, level):
        code = c % period
        dirs = [orders[p][level] for p in pattern]
        return (
            pick(code, [near_b[d] for d in dirs]),
            pick(code, [near_z[d] for d in dirs]),
            pick(code, [mine[d] for d in dirs]),
        )

    core_partner = (flipped(b, 1), z)
    barrier = pltpu.get_barrier_semaphore()
    partners = [(near_b[2], near_z[2]), (near_b[3], near_z[3]), core_partner]
    partners += [(near_b[0], near_z[0]), (near_b[1], near_z[1])]
    greeted = [core_partner, (near_b[0], near_z[0]), (near_b[1], near_z[1])] + greet_line()
    for who in greeted:
        pl.semaphore_signal(barrier, inc=1, device_id=who, device_id_type=MESH)
    pl.semaphore_wait(barrier, len(greeted))

    tokens = lay_out.shape[1]
    count = lax.axis_size("seq")
    moves = []
    own = []
    for i, (src, dst) in enumerate(((y_ref, lay_out), (sg_ref, grad_out))):
        for s in range(seqs):
            base_sem = i * seqs * (count - 1)
            moves += spread(src, dst, seqs, tokens, False, tok_send, tok_recv, base_sem, s)
            own.append(own_part(src, dst, seqs, tokens, False, tok_own.at[i * seqs + s], s))
    for copy in own:
        copy.start()
    half_moves = len(moves) // 2
    move_ticks = [i for i in range(half_moves)] + [12 + 4 * i for i in range(half_moves)]

    def base(c, level):
        rows = 0
        size = CHUNK
        for l in range(level):
            size = size // 2
            rows = rows + direction(c, l)[2] * size
        return pl.multiple_of(rows, 16)

    def g_rows(c):
        return pl.ds(pl.multiple_of(c * CHUNK, CHUNK), CHUNK)

    my_cols = pl.ds(pl.multiple_of(core * HALF, HALF), HALF)
    other_cols = pl.ds(pl.multiple_of((1 - core) * HALF, HALF), HALF)

    def rs_copy(c, s):
        if s == 0:
            return pltpu.make_async_remote_copy(
                g_ref.at[g_rows(c), other_cols], r0.at[c], rs_send.at[0, c], rs_recv.at[0, c],
                device_id=core_partner, device_id_type=MESH,
            )
        size = CHUNK >> s
        nb, nz, m = direction(c, s - 1)
        start = pl.multiple_of(base(c, s - 1) + (1 - m) * size, 16)
        return pltpu.make_async_remote_copy(
            acc.at[c, pl.ds(start, size)], got[s].at[c], rs_send.at[s, c], rs_recv.at[s, c],
            device_id=(nb, nz), device_id_type=MESH,
        )

    def ag_copy(c, s):
        if s == 0:
            return pltpu.make_async_remote_copy(
                res.at[c], out_ref.at[g_rows(c), my_cols], ag_send.at[0, c], ag_recv.at[0, c],
                device_id=core_partner, device_id_type=MESH,
            )
        size = CHUNK >> s
        nb, nz, _ = direction(c, s - 1)
        start = base(c, s)
        return pltpu.make_async_remote_copy(
            res.at[c, pl.ds(start, size)], res.at[c, pl.ds(start, size)],
            ag_send.at[s, c], ag_recv.at[s, c], device_id=(nb, nz), device_id_type=MESH,
        )

    def loc_in(c):
        return pltpu.make_async_copy(g_ref.at[g_rows(c), my_cols], acc.at[c], loc.at[0, c])

    def loc_out(c):
        return pltpu.make_async_copy(res.at[c], out_ref.at[g_rows(c), my_cols], loc.at[1, c])

    def stage_first(c):
        rs_copy(c, 0).start()
        loc_in(c).start()

    def stage_scatter(s, c):
        rs_copy(c, s - 1).wait_recv()
        if s == 1:
            loc_in(c).wait()
        half = CHUNK >> s
        start = base(c, s - 1)
        m = direction(c, s - 1)[2]
        for which in (0, 1):
            off = pl.multiple_of(((1 - m) if which == 0 else m) * half, 16)
            rows = pl.ds(pl.multiple_of(start + off, 16), half)
            acc[c, rows] = acc[c, rows] + got[s - 1][c, pl.ds(off, half)]
            if which == 0:
                rs_copy(c, s).start()

    def stage_turn(c):
        rs_copy(c, 4).wait_recv()
        rows = pl.ds(base(c, 4), 16)
        res[c, rows] = acc[c, rows] + r4[c]
        ag_copy(c, 4).start()

    def stage_gather(s, c):
        ag_copy(c, s + 1).wait_recv()
        ag_copy(c, s).start()
        if s == 0:
            loc_out(c).start()

    def stage_last(c):
        ag_copy(c, 0).wait_recv()
        loc_out(c).wait()
        for s in range(5):
            rs_copy(c, s).wait_send()
            ag_copy(c, s).wait_send()

    stages = (
        [stage_first]
        + [functools.partial(stage_scatter, s) for s in (1, 2, 3, 4)]
        + [stage_turn]
        + [functools.partial(stage_gather, s) for s in (3, 2, 1, 0)]
        + [stage_last]
    )

    place = place_of_block()

    def small_copies(i):
        first = place - place % (1 << i)
        part = pl.ds(first, 1 << i)
        return (
            pltpu.make_async_remote_copy(
                small_out, sgot.at[i], sm_send.at[i], sm_recv.at[i],
                device_id=partners[i], device_id_type=MESH,
            ),
            pltpu.make_async_remote_copy(
                head_out.at[part], head_out.at[part], hd_send.at[i], hd_recv.at[i],
                device_id=partners[i], device_id_type=MESH,
            ),
        )

    small_out[...] = small_ref[...]
    head_out[place] = head_ref[...]

    def tick(t, carry):
        for when, copy in zip(move_ticks, moves):

            @pl.when(t == when)
            def _():
                copy.start()

        for i in range(len(partners) + 1):

            @pl.when(t == 3 * i)
            def _():
                if i > 0:
                    for copy in small_copies(i - 1):
                        copy.wait()
                    small_out[...] = small_out[...] + sgot[i - 1]
                if i < len(partners):
                    for copy in small_copies(i):
                        copy.start()

        for stage, lag in reversed(list(zip(stages, lags))):
            c = t - lag

            @pl.when((c >= 0) & (c < chunks))
            def _():
                stage(c)

        return carry

    lax.fori_loop(0, chunks + lags[-1], tick, 0)
    for copy in own + moves:
        copy.wait()


def sum_all(seqs, g, small, head, y, sg, tokens):
    width = g.shape[-1]
    flat = g.reshape(-1, width)
    chunks = flat.shape[0] // CHUNK
    count = lax.axis_size("seq")
    group = seqs * count
    moves = 2 * seqs * (count - 1)
    dma = pltpu.SemaphoreType.DMA
    anywhere = pl.BlockSpec(memory_space=pl.ANY)
    in_vmem = pl.BlockSpec(memory_space=pltpu.VMEM)
    block = jax.ShapeDtypeStruct((group, tokens, width), bf16)
    total, small, head, lay, grad = pl.pallas_call(
        functools.partial(sum_kernel, seqs, chunks, "xy", tuple(3 * i for i in range(11))),
        out_shape=(
            jax.ShapeDtypeStruct(flat.shape, bf16),
            jax.ShapeDtypeStruct(small.shape, f32),
            jax.ShapeDtypeStruct((32,) + head.shape, bf16),
            block,
            block,
        ),
        in_specs=[anywhere, in_vmem, in_vmem, anywhere, anywhere],
        out_specs=(anywhere, in_vmem, in_vmem, anywhere, anywhere),
        scratch_shapes=[
            pltpu.VMEM((chunks, CHUNK, HALF), bf16),
            pltpu.VMEM((chunks, CHUNK, HALF), bf16),
            pltpu.VMEM((chunks, CHUNK, HALF), bf16),
            pltpu.VMEM((chunks, CHUNK // 2, HALF), bf16),
            pltpu.VMEM((chunks, CHUNK // 4, HALF), bf16),
            pltpu.VMEM((chunks, CHUNK // 8, HALF), bf16),
            pltpu.VMEM((chunks, CHUNK // 16, HALF), bf16),
            pltpu.VMEM((5,) + small.shape, f32),
            dma((5, chunks)),
            dma((5, chunks)),
            dma((5, chunks)),
            dma((5, chunks)),
            dma((2, chunks)),
            dma((5,)),
            dma((5,)),
            dma((5,)),
            dma((5,)),
            dma((moves,)),
            dma((moves,)),
            dma((2 * seqs,)),
        ],
        compiler_params=pltpu.CompilerParams(
            collective_id=0, has_side_effects=True, vmem_limit_bytes=56 * 2**20
        ),
        name="sum_gradients",
    )(flat, small, head, y, sg)
    blocks = lax.axis_size("batch") // 8
    if blocks > 1:
        alike = [[i + 8 * j for j in range(blocks)] for i in range(8)]
        total = lax.psum(total, "batch", axis_index_groups=alike)
        small = lax.psum(small, "batch", axis_index_groups=alike)
        head = lax.all_gather(head, "batch", axis_index_groups=alike, axis=0, tiled=True)
    return total.reshape(g.shape), small, head, lay, grad


def finish_kernel(
    total, small_ref, cls_ref, label_ref, vec_ref, pool_ref, lay_in, grad_in,
    lay_out, loss_out, grad_out, gq, gk, gv, go, gqb, gvb, gob, gg1, gb1, gin, gib, gou, gub,
    gg2, gb2, gpool, gpb, gcp, gcb,
    low_s, full_s, pool_s, pass_s, in_sem, out_sem,
):
    units = low_s.shape[0]
    group = loss_out.shape[0]
    seqs = cls_ref.shape[0]
    loads = [pltpu.make_async_copy(total.at[u], low_s.at[u], in_sem.at[u]) for u in range(units)]
    for copy in loads:
        copy.start()
    places = (
        [gou.at[pl.ds(j * WIDTH, WIDTH)] for j in range(4)]
        + [gin.at[:, pl.ds(j * WIDTH, WIDTH)] for j in range(4)]
        + [go, gq, gk, gv]
    )
    stores = [
        pltpu.make_async_copy(full_s.at[u], places[u], out_sem.at[u]) for u in range(units)
    ]
    passed_in = [
        pltpu.make_async_copy(src, pass_s.at[i], in_sem.at[units + i])
        for i, src in enumerate((lay_in, grad_in))
    ]
    passed = [
        pltpu.make_async_copy(pass_s.at[i], dst, out_sem.at[units + i])
        for i, dst in enumerate((lay_out, grad_out))
    ]
    for copy in passed_in:
        copy.start()
    pool_store = pltpu.make_async_copy(pool_s, gpool, out_sem.at[units + 2])

    def widen(u):
        loads[u].wait()

        @pl.loop(0, WIDTH // 128)
        def _(i):
            r = tile(i, 128)
            full_s[u, r, :] = low_s[u, r, :].astype(f32)

        stores[u].start()

    for u in range(4):
        widen(u)
    for before, after in zip(passed_in, passed):
        before.wait()
        after.start()

    def exact(left, right, dims=NN):
        return lax.dot_general(left, right, dims, precision=highest, preferred_element_type=f32)

    pooled = jnp.tanh(dot(cls_ref[...], pool_ref[...]) + vec_ref[PB : PB + 1, :])
    row = lax.broadcasted_iota(jnp.int32, (8, 1), 0)
    class_rows = jnp.where(row < 3, vec_ref[CP : CP + 8, :], 0.0)
    picked = jnp.where(
        row == lax.broadcasted_iota(jnp.int32, (8, 128), 1), vec_ref[CB : CB + 1, 0:128], 0.0
    )
    logits = exact(class_rows, pooled, NT) + jnp.sum(picked, axis=-1, keepdims=True)
    logits = jnp.where(row < 3, logits, masked_fill)
    top = jnp.max(logits, axis=0, keepdims=True)
    raised = jnp.exp(logits - top)
    total_row = jnp.sum(raised, axis=0, keepdims=True)
    chosen = (row == label_ref[...]).astype(f32)
    losses = (top + jnp.log(total_row)) - jnp.sum(
        jnp.where(chosen > 0.0, logits, 0.0), axis=0, keepdims=True
    )
    logit_grad = raised / total_row - chosen
    first = lax.axis_index("batch") * group
    pickers = (
        lax.broadcasted_iota(jnp.int32, (seqs, 128), 0)
        == lax.broadcasted_iota(jnp.int32, (seqs, 128), 1) + first
    ).astype(f32)
    loss_out[...] = exact(losses, pickers)[0, 0:group]
    pre = exact(logit_grad, class_rows, TN) * (1.0 - pooled * pooled)
    ones = jnp.ones((1, seqs), f32)
    gcb[...] = exact(ones, logit_grad, NT)[0, 0:3]
    gpb[...] = jnp.sum(pre, axis=0)
    gcp[...] = exact(pooled, logit_grad, (((0,), (1,)), ((), ())))[:, 0:3]
    high = pre.astype(bf16)
    rest = pre - high.astype(f32)
    mid = rest.astype(bf16)
    low = (rest - mid.astype(f32)).astype(bf16)
    for j in range(3):
        cols = pl.ds(j * 256, 256)
        cls = cls_ref[:, cols]
        pool_s[cols, :] = dot(cls, high, TN) + dot(cls, mid, TN) + dot(cls, low, TN)
    pool_store.start()
    for i, ref in (
        (QB, gqb), (VB, gvb), (OB, gob), (G1, gg1), (B1, gb1), (UB, gub), (G2, gg2), (B2, gb2),
    ):
        ref[...] = small_ref[i, :]
    for j in range(4):
        gib[j * WIDTH : (j + 1) * WIDTH] = small_ref[IB + j, :]
    for u in range(4, units):
        widen(u)
    for copy in stores + passed + [pool_store]:
        copy.wait()


def finish(total, small, cls, labels, vecs, pool, lay, grad):
    group, tokens, width = lay.shape
    anywhere = pl.BlockSpec(memory_space=pl.ANY)
    in_vmem = pl.BlockSpec(memory_space=pltpu.VMEM)
    square = ((width, width), f32, anywhere)
    row = ((width,), f32, in_vmem)
    outs = (
        [(lay.shape, bf16, anywhere), ((group,), f32, in_vmem), (grad.shape, bf16, anywhere)]
        + [square] * 4
        + [row] * 5
        + [((width, 4 * width), f32, anywhere), ((4 * width,), f32, in_vmem)]
        + [((4 * width, width), f32, anywhere), row, row, row]
        + [square, row, ((width, 3), f32, in_vmem), ((3,), f32, in_vmem)]
    )
    units = total.shape[0]
    return pl.pallas_call(
        finish_kernel,
        out_shape=tuple(jax.ShapeDtypeStruct(s, t) for s, t, _ in outs),
        in_specs=[anywhere] + [in_vmem] * 5 + [anywhere, anywhere],
        out_specs=tuple(m for _, _, m in outs),
        scratch_shapes=[
            pltpu.VMEM((units, width, width), bf16), pltpu.VMEM((units, width, width), f32),
            pltpu.VMEM((width, width), f32), pltpu.VMEM((2,) + lay.shape, bf16),
            pltpu.SemaphoreType.DMA((units + 2,)), pltpu.SemaphoreType.DMA((units + 3,)),
        ],
        compiler_params=pltpu.CompilerParams(vmem_limit_bytes=60 * 2**20),
        name="finish",
    )(total, small, cls, labels, vecs, pool, lay, grad)


def local(
    states, lengths, labels, cotangent,
    query_proj, key_proj, value_proj, output_proj,
    query_bias, value_bias, output_bias, first_gain, first_bias,
    inner_proj, inner_bias, outer_proj, outer_bias, second_gain, second_bias,
    pool_proj, pool_bias, class_proj, class_bias,
):
    group, tokens, width = states.shape
    seqs = group // lax.axis_size("seq")
    (
        vecs, x, upstream, q, k, v, att, n1, low, hid, slope, n2, stat, y,
    ) = forward(
        lengths, states, cotangent,
        (query_proj, key_proj, value_proj, output_proj, inner_proj, outer_proj),
        (query_bias, value_bias, output_bias, first_gain, first_bias, inner_bias, outer_bias,
         second_gain, second_bias, pool_bias, class_proj, class_bias),
    )
    g, attn_grad, sums_ffn, head = ffn_back(
        seqs, labels, vecs, (upstream, n2, hid, slope, low, n1, stat, y),
        inner_proj, outer_proj, pool_proj,
    )
    g, states_rows, sums_attn = attn_back(
        seqs, lengths, attn_grad, g, (q, k, v, att, x, stat),
        (query_proj, key_proj, value_proj, output_proj),
    )
    small = jnp.concatenate([sums_attn[0:2], sums_ffn[2:12], jnp.zeros((4, width), f32)])
    total, small, head, lay, grad = sum_all(seqs, g, small, head, y, states_rows, tokens)
    cls = head[:, 0 : 6 * seqs].reshape(-1, width)
    label_row = head[:, 6 * seqs, 0:seqs].reshape(1, -1).astype(jnp.int32)
    return finish(total, small, cls, label_row, vecs, pool_proj, lay, grad)


def solution(mesh):
    split = P("batch", "seq", None)
    in_specs = (split, P("batch"), P("batch"), split) + (P(),) * 19
    out_specs = (split, P("batch"), split) + (P(),) * 19
    return jax.shard_map(local, mesh=mesh, in_specs=in_specs, out_specs=out_specs, check_vma=False)
```

```python
import functools

import jax
import jax.numpy as jnp
from jax import lax
from jax.experimental import pallas as pl
from jax.experimental.pallas import tpu as pltpu
from jax.sharding import PartitionSpec as P

HEADS = 12
HEAD_DIM = 64
WIDTH = 768
HALF = 384
CHUNK = 256
MESH = pl.DeviceIdType.MESH

bf16 = jnp.bfloat16
f32 = jnp.float32
highest = lax.Precision.HIGHEST
norm_eps = 1e-06
masked_fill = -1e30
inv_root_two = 0.7071067811865476
inv_root_tau = 0.3989422804014327


def pick(code, table):
    out = table[-1]
    for i in range(len(table) - 2, -1, -1):
        out = jnp.where(code == i, table[i], out)
    return out


def flipped(index, bit):
    return index + bit * (1 - 2 * ((index // bit) % 2))


NT = (((1,), (1,)), ((), ()))
NN = (((1,), (0,)), ((), ()))
TN = (((0,), (0,)), ((), ()))
VECS = 24
QB, VB, OB, G1, B1, IB, UB, G2, B2, PB, CP, CB = 0, 1, 2, 3, 4, 5, 9, 10, 11, 12, 13, 16


def dot(left, right, dims=NN):
    return lax.dot_general(left, right, dims, preferred_element_type=f32)


def gelu_parts(u):
    t = 1.0 / (1.0 + (0.3275911 * inv_root_two) * jnp.abs(u))
    bell = jnp.exp(-0.5 * u * u)
    poly = 1.061405429
    for coefficient in (-1.453152027, 1.421413741, -0.284496736, 0.254829592):
        poly = poly * t + coefficient
    tail = (0.5 * t) * poly * bell
    cumulative = jnp.where(u >= 0.0, 1.0 - tail, tail)
    return u * cumulative, cumulative + u * (bell * inv_root_tau)


def norm_rows(z):
    average = jnp.mean(z, axis=-1, keepdims=True)
    centered = z - average
    inv_root = lax.rsqrt(jnp.mean(centered * centered, axis=-1, keepdims=True) + norm_eps)
    return centered * inv_root, inv_root


def norm_rows_back(upstream, normed, inv_root, gain):
    scaled = upstream * gain
    return inv_root * (
        scaled
        - jnp.mean(scaled, axis=-1, keepdims=True)
        - normed * jnp.mean(scaled * normed, axis=-1, keepdims=True)
    )


def tile(i, size):
    return pl.ds(pl.multiple_of(i * size, size), size)


def copies(pairs, sems):
    out = []
    for i, (src, dst) in enumerate(pairs):
        out.append(pltpu.make_async_copy(src, dst, sems.at[i]))
    return out


def head_lanes(which):
    lane = lax.broadcasted_iota(jnp.int32, (1, 128), 1)
    return (lane >= 64) if which else (lane < 64)


def only(mask, block):
    return jnp.where(mask, block, jnp.zeros_like(block))


def attend_pair(q2, k2, v2, length, keys):
    k2 = k2[:keys]
    v2 = v2[:keys]
    place = lax.broadcasted_iota(jnp.int32, (1, keys), 1)
    out = None
    logs = []
    for which in (0, 1):
        lanes = head_lanes(which)
        scores = dot(only(lanes, q2) * bf16(0.125), k2, NT)
        scores = jnp.where(place < length, scores, masked_fill)
        top = jnp.max(scores, axis=-1, keepdims=True)
        weights = jnp.exp(scores - top)
        total = jnp.sum(weights, axis=-1, keepdims=True)
        part = dot(weights.astype(bf16), only(lanes, v2)) * (1.0 / total)
        out = part if out is None else out + part
        logs.append(top + jnp.log(total))
    return out, logs


def spread(src, dst, seqs, tokens, to_rows, sends, recvs, base, s):
    count = lax.axis_size("seq")
    b = lax.axis_index("batch")
    z = lax.axis_index("seq")
    out = []
    for d in range(1, count):
        other = lax.rem(z + d, count)
        if to_rows:
            source = src.at[other * seqs + s]
            target = dst.at[pl.ds(pl.multiple_of((s * count + z) * tokens, tokens), tokens)]
        else:
            source = src.at[pl.ds(pl.multiple_of((s * count + other) * tokens, tokens), tokens)]
            target = dst.at[z * seqs + s]
        i = base + s * (count - 1) + d - 1
        out.append(
            pltpu.make_async_remote_copy(
                source, target, sends.at[i], recvs.at[i],
                device_id=(b, other), device_id_type=MESH,
            )
        )
    return out


def own_part(src, dst, seqs, tokens, to_rows, sem, s):
    count = lax.axis_size("seq")
    z = lax.axis_index("seq")
    block = z * seqs + s
    rows = pl.ds(pl.multiple_of((s * count + z) * tokens, tokens), tokens)
    if to_rows:
        return pltpu.make_async_copy(src.at[block], dst.at[rows], sem)
    return pltpu.make_async_copy(src.at[rows], dst.at[block], sem)


def greet_line():
    count = lax.axis_size("seq")
    z = lax.axis_index("seq")
    return [(lax.axis_index("batch"), lax.rem(z + d, count)) for d in range(1, count)]


def forward_kernel(
    seqs, len_ref, states, cot, wq, wk, wv, wo, w1, w2,
    query_bias, value_bias, output_bias, first_gain, first_bias, inner_bias, outer_bias,
    second_gain, second_bias, pool_bias, class_proj, class_bias,
    vec_ref, x_out, cot_out, q_out, k_out, v_out, att_out, n1_out, low_out, hid_out, slope_out,
    n2_out, stat_out, y_out,
    x_s, wq_s, wk_s, wv_s, wo_s, w1_s, w2_s,
    q_s, k_s, v_s, att_s, n1_s, low_s, hid_s, slope_s, n2_s, stat_s, y_s, z_s,
    in_sem, out_sem, own_sem, sends, recvs,
):
    rows = z_s.shape[0]
    tokens = states.shape[1]
    line = greet_line()
    barrier = pltpu.get_barrier_semaphore()
    for who in line:
        pl.semaphore_signal(barrier, inc=1, device_id=who, device_id_type=MESH)
    weights_in = copies(
        [(wq, wq_s), (wk, wk_s), (wv, wv_s), (wo, wo_s), (w1, w1_s), (w2, w2_s)], in_sem
    )
    own = []
    for s in range(seqs):
        own.append(own_part(states, x_s, seqs, tokens, True, own_sem.at[s], s))
        own.append(own_part(cot, cot_out, seqs, tokens, True, own_sem.at[seqs + s], s))
    for copy in own + weights_in:
        copy.start()
    pl.semaphore_wait(barrier, len(line))
    moves = [spread(states, x_s, seqs, tokens, True, sends, recvs, 0, s) for s in range(seqs)]
    late = [
        spread(cot, cot_out, seqs, tokens, True, sends, recvs, seqs * len(line), s)
        for s in range(seqs)
    ]
    for group in moves + late:
        for copy in group:
            copy.start()
    vec_ref[...] = jnp.zeros_like(vec_ref)
    for i, ref in (
        (QB, query_bias), (VB, value_bias), (OB, output_bias), (G1, first_gain), (B1, first_bias),
        (UB, outer_bias), (G2, second_gain), (B2, second_bias), (PB, pool_bias),
    ):
        vec_ref[i : i + 1, :] = ref[...].astype(f32).reshape(1, WIDTH)
    for i in range(4):
        vec_ref[IB + i : IB + i + 1, :] = (
            inner_bias[i * WIDTH : (i + 1) * WIDTH].astype(f32).reshape(1, WIDTH)
        )
    eye = (
        lax.broadcasted_iota(jnp.int32, (8, 3), 0) == lax.broadcasted_iota(jnp.int32, (8, 3), 1)
    ).astype(bf16)
    vec_ref[CP : CP + 3, :] = dot(eye, class_proj[...], NT)[0:3, :]
    vec_ref[CB : CB + 1, 0:3] = class_bias[...].astype(f32).reshape(1, 3)

    z = lax.axis_index("seq")
    waiting = []
    for s in range(seqs):
        for copy in moves[s]:
            copy.wait_recv()
        own[2 * s].wait()
        part = pl.ds(s * rows, rows)
        waiting += forward_rows(
            s, part, len_ref[z * seqs + s], rows, s == 0, vec_ref, weights_in,
            (x_s, wq_s, wk_s, wv_s, wo_s, w1_s, w2_s, q_s, k_s, v_s, att_s, n1_s, low_s, hid_s,
             slope_s, n2_s, stat_s, y_s, z_s),
            (x_out, q_out, k_out, v_out, att_out, n1_out, low_out, hid_out, slope_out, n2_out,
             stat_out, y_out),
            out_sem,
        )
    for group in moves:
        for copy in group:
            copy.wait_send()
    for group in late:
        for copy in group:
            copy.wait()
    for s in range(seqs):
        own[2 * s + 1].wait()
    for copy in waiting:
        copy.wait()


def forward_rows(s, part, length, rows, first_time, vec_ref, weights_in, scratch, outs, out_sem):
    (x_s, wq_s, wk_s, wv_s, wo_s, w1_s, w2_s, q_s, k_s, v_s, att_s, n1_s, low_s, hid_s,
     slope_s, n2_s, stat_s, y_s, z_s) = scratch
    start = s * rows
    out = [
        pltpu.make_async_copy(src.at[part], dst.at[part], out_sem.at[s, i])
        for i, (src, dst) in enumerate(
            zip((x_s, q_s, k_s, v_s, att_s, n1_s, low_s, hid_s, slope_s, n2_s, stat_s, y_s), outs)
        )
    ]
    out[0].start()
    for i, (w, dst, bias) in enumerate(((wq_s, q_s, QB), (wk_s, k_s, None), (wv_s, v_s, VB))):
        if first_time:
            weights_in[i].wait()

        @pl.loop(0, WIDTH // 256)
        def _(j):
            cols = tile(j, 256)
            grid = dot(x_s[part, :], w[:, cols])
            if bias is not None:
                grid = grid + vec_ref[bias : bias + 1, cols]
            dst[part, cols] = grid.astype(bf16)

        out[1 + i].start()

    stat_s[part, :] = jnp.zeros((rows, 128), f32)
    lane = lax.broadcasted_iota(jnp.int32, (1, 128), 1)

    @pl.loop(0, HEADS // 2)
    def _(p):
        cols = tile(p, 128)
        mix, logs = attend_pair(q_s[part, cols], k_s[part, cols], v_s[part, cols], length, rows)
        att_s[part, cols] = mix.astype(bf16)
        stat_s[part, :] = jnp.where(
            lane == 2 * p, logs[0], jnp.where(lane == 2 * p + 1, logs[1], stat_s[part, :])
        )

    out[4].start()
    if first_time:
        weights_in[3].wait()

    @pl.loop(0, WIDTH // 256)
    def _(j):
        cols = tile(j, 256)
        z_s[:, cols] = (
            x_s[part, cols].astype(f32)
            + dot(att_s[part, :], wo_s[:, cols])
            + vec_ref[OB : OB + 1, cols]
        )

    @pl.loop(0, rows // 128)
    def _(i):
        r = tile(i, 128)
        q = pl.ds(pl.multiple_of(start + i * 128, 128), 128)
        normed, inv_root = norm_rows(z_s[r, :])
        n1_s[q, :] = normed.astype(bf16)
        first = normed * vec_ref[G1 : G1 + 1, :] + vec_ref[B1 : B1 + 1, :]
        low_s[q, :] = first.astype(bf16)
        z_s[r, :] = first + vec_ref[UB : UB + 1, :]
        stat_s[q, :] = jnp.where(lane == 12, inv_root, stat_s[q, :])

    out[5].start()
    out[6].start()
    if first_time:
        weights_in[4].wait()
        weights_in[5].wait()
    ft = 256

    @pl.loop(0, 4 * WIDTH // ft)
    def _(j):
        cols = tile(j, ft)
        u = dot(low_s[part, :], w1_s[:, cols]) + vec_ref[pl.ds(IB + j // 3, 1), tile(j % 3, ft)]
        h, slope = gelu_parts(u)
        hid_s[part, cols] = h.astype(bf16)
        slope_s[part, cols] = slope.astype(bf16)

    out[7].start()
    out[8].start()

    @pl.loop(0, WIDTH // 256)
    def _(j):
        cols = tile(j, 256)
        z_s[:, cols] += dot(hid_s[part, :], w2_s[:, cols])

    @pl.loop(0, rows // 128)
    def _(i):
        r = tile(i, 128)
        q = pl.ds(pl.multiple_of(start + i * 128, 128), 128)
        normed, inv_root = norm_rows(z_s[r, :])
        n2_s[q, :] = normed.astype(bf16)
        y_s[q, :] = (normed * vec_ref[G2 : G2 + 1, :] + vec_ref[B2 : B2 + 1, :]).astype(bf16)
        stat_s[q, :] = jnp.where(lane == 13, inv_root, stat_s[q, :])

    for i in (9, 10, 11):
        out[i].start()
    return out


def forward(lengths, states, cotangent, weights, small):
    count = lax.axis_size("seq")
    group, tokens, width = states.shape
    seqs = group // count
    one = count * tokens
    rows = seqs * one
    ff = 4 * width
    anywhere = pl.BlockSpec(memory_space=pl.ANY)
    in_vmem = pl.BlockSpec(memory_space=pltpu.VMEM)
    saved = [((rows, width), bf16)] * 6 + [((rows, ff), bf16)] * 2 + [
        ((rows, width), bf16), ((rows, 128), f32), ((rows, width), bf16),
    ]
    outs = [((VECS, width), f32), ((rows, width), bf16), ((rows, width), bf16)] + saved
    moves = 2 * seqs * (count - 1)
    flops = 2 * rows * width * (4 * width + 2 * ff) + 4 * rows * one * width
    dma = pltpu.SemaphoreType.DMA
    return pl.pallas_call(
        functools.partial(forward_kernel, seqs),
        out_shape=tuple(jax.ShapeDtypeStruct(s, t) for s, t in outs),
        in_specs=[pl.BlockSpec(memory_space=pltpu.SMEM)] + [anywhere] * 8 + [in_vmem] * len(small),
        out_specs=(in_vmem,) + (anywhere,) * (len(outs) - 1),
        scratch_shapes=[pltpu.VMEM((rows, width), bf16)]
        + [pltpu.VMEM(w.shape, bf16) for w in weights]
        + [pltpu.VMEM(s, t) for s, t in saved]
        + [
            pltpu.VMEM((one, width), f32), dma((6,)), dma((seqs, 12)), dma((2 * seqs,)),
            dma((moves,)), dma((moves,)),
        ],
        compiler_params=pltpu.CompilerParams(
            collective_id=1, has_side_effects=True, vmem_limit_bytes=60 * 2**20
        ),
        cost_estimate=pl.CostEstimate(
            flops=flops, bytes_accessed=50 * 2**20, transcendentals=rows * (ff + 12 * one)
        ),
        name="forward",
    )(lengths, states, cotangent, *weights, *small)


def exit_back(cls_rows, labels, vec_ref, pool_s):
    pooled = jnp.tanh(dot(cls_rows, pool_s[...]) + vec_ref[PB : PB + 1, :])
    class_rows = vec_ref[CP : CP + 3, :]
    logits = [
        jnp.sum(pooled * class_rows[i : i + 1, :], axis=-1, keepdims=True)
        + vec_ref[CB : CB + 1, i : i + 1]
        for i in range(3)
    ]
    top = jnp.maximum(jnp.maximum(logits[0], logits[1]), logits[2])
    raised = [jnp.exp(l - top) for l in logits]
    total = raised[0] + raised[1] + raised[2]
    back = jnp.zeros_like(pooled)
    for i in range(3):
        back = back + (raised[i] / total - (labels == i).astype(f32)) * class_rows[i : i + 1, :]
    pre = back * (1.0 - pooled * pooled)
    high = pre.astype(bf16)
    rest = pre - high.astype(f32)
    mid = rest.astype(bf16)
    low = (rest - mid.astype(f32)).astype(bf16)
    return dot(high, pool_s[...], NT) + dot(mid, pool_s[...], NT) + dot(low, pool_s[...], NT)


def attend_back_pair(q2, k2, v2, d2, logs, delta, length, keys):
    k2 = k2[:keys]
    v2 = v2[:keys]
    usable = lax.broadcasted_iota(jnp.int32, (keys, 1), 0) < length
    dq = dk = dv = None
    for which in (0, 1):
        lanes = head_lanes(which)
        qh = only(lanes, q2) * bf16(0.125)
        dh = only(lanes, d2)
        kh = only(lanes, k2) * bf16(0.125)
        scores = dot(k2, qh, NT)
        probs = jnp.where(usable, jnp.exp(scores - logs[which]), 0.0)
        prob_grad = dot(v2, dh, NT)
        score_grad = (probs * (prob_grad - delta[which])).astype(bf16)
        parts = (
            dot(score_grad, kh, TN),
            dot(score_grad, qh),
            dot(probs.astype(bf16), dh),
        )
        if dq is None:
            dq, dk, dv = parts
        else:
            dq, dk, dv = dq + parts[0], dk + parts[1], dv + parts[2]
    return dq, dk, dv


def place_of_block():
    return (lax.axis_index("batch") % 8) * 4 + lax.axis_index("seq")


def back_kernel(
    seqs, chunks, pattern, lags, len_ref, label_ref, vec_ref,
    cot, n2, hid, slope, low, n1, stat, y, q, k, v, att, x,
    w1, w2, pool, wq, wk, wv, wo,
    out_ref, small_out, head_out, lay_out, grad_out,
    wide, fg_s, stat_s, w1_s, w2_s, pool_s, cls_s, row_s, rowt_s,
    acc, staged, r0, r1, r2, r3, r4, sgot,
    in_sem, hid_sem, rs_send, rs_recv, ag_send, ag_recv, loc, sm_send, sm_recv, hd_send, hd_recv,
    tok_send, tok_recv, tok_own,
):
    rows = fg_s.shape[0]
    one = rows // seqs
    tokens = lay_out.shape[1]
    count = lax.axis_size("seq")
    b = lax.axis_index("batch")
    z = lax.axis_index("seq")
    core = b % 2

    got = [r0, r1, r2, r3, r4]
    res = r0
    near_b = [flipped(b, 2), flipped(b, 4), b, b]
    near_z = [z, z, flipped(z, 1), flipped(z, 2)]
    mine = [(b // 2) % 2, (b // 4) % 2, z % 2, (z // 2) % 2]
    orders = {"x": (0, 1, 2, 3), "y": (1, 0, 2, 3)}
    period = len(pattern)

    def direction(c, level):
        code = c % period
        dirs = [orders[p][level] for p in pattern]
        return (
            pick(code, [near_b[d] for d in dirs]),
            pick(code, [near_z[d] for d in dirs]),
            pick(code, [mine[d] for d in dirs]),
        )

    core_partner = (flipped(b, 1), z)
    barrier = pltpu.get_barrier_semaphore()
    partners = [(near_b[2], near_z[2]), (near_b[3], near_z[3]), core_partner]
    partners += [(near_b[0], near_z[0]), (near_b[1], near_z[1])]
    greeted = [core_partner, (near_b[0], near_z[0]), (near_b[1], near_z[1])] + greet_line()
    for who in greeted:
        pl.semaphore_signal(barrier, inc=1, device_id=who, device_id_type=MESH)

    def base(c, level):
        first = 0
        size = CHUNK
        for l in range(level):
            size = size // 2
            first = first + direction(c, l)[2] * size
        return pl.multiple_of(first, 16)

    slots = staged.shape[0]
    my_cols = pl.ds(pl.multiple_of(core * HALF, HALF), HALF)

    def rs_copy(c, s):
        if s == 0:
            return pltpu.make_async_remote_copy(
                staged.at[c % slots], r0.at[c], rs_send.at[0, c], rs_recv.at[0, c],
                device_id=core_partner, device_id_type=MESH,
            )
        size = CHUNK >> s
        nb, nz, m = direction(c, s - 1)
        start = pl.multiple_of(base(c, s - 1) + (1 - m) * size, 16)
        return pltpu.make_async_remote_copy(
            acc.at[c, pl.ds(start, size)], got[s].at[c], rs_send.at[s, c], rs_recv.at[s, c],
            device_id=(nb, nz), device_id_type=MESH,
        )

    def out_rows(c):
        return out_ref.at[pl.ds(pl.multiple_of(c * CHUNK, CHUNK), CHUNK), my_cols]

    def ag_copy(c, s):
        if s == 0:
            return pltpu.make_async_remote_copy(
                res.at[c], out_rows(c), ag_send.at[0, c], ag_recv.at[0, c],
                device_id=core_partner, device_id_type=MESH,
            )
        size = CHUNK >> s
        nb, nz, _ = direction(c, s - 1)
        start = base(c, s)
        return pltpu.make_async_remote_copy(
            res.at[c, pl.ds(start, size)], res.at[c, pl.ds(start, size)],
            ag_send.at[s, c], ag_recv.at[s, c], device_id=(nb, nz), device_id_type=MESH,
        )

    def loc_out(c):
        return pltpu.make_async_copy(res.at[c], out_rows(c), loc.at[c])

    def stage_scatter(s, c):
        rs_copy(c, s - 1).wait_recv()
        half = CHUNK >> s
        start = base(c, s - 1)
        m = direction(c, s - 1)[2]
        for which in (0, 1):
            off = pl.multiple_of(((1 - m) if which == 0 else m) * half, 16)
            part = pl.ds(pl.multiple_of(start + off, 16), half)
            acc[c, part] = acc[c, part] + got[s - 1][c, pl.ds(off, half)]
            if which == 0:
                rs_copy(c, s).start()

    def stage_turn(c):
        rs_copy(c, 4).wait_recv()
        part = pl.ds(base(c, 4), 16)
        res[c, part] = acc[c, part] + r4[c]
        ag_copy(c, 4).start()

    def stage_gather(s, c):
        ag_copy(c, s + 1).wait_recv()
        ag_copy(c, s).start()
        if s == 0:
            loc_out(c).start()

    def stage_last(c):
        ag_copy(c, 0).wait_recv()
        loc_out(c).wait()
        for s in range(1, 5):
            rs_copy(c, s).wait_send()
        for s in range(5):
            ag_copy(c, s).wait_send()

    stages = (
        [functools.partial(stage_scatter, s) for s in (1, 2, 3, 4)]
        + [stage_turn]
        + [functools.partial(stage_gather, s) for s in (3, 2, 1, 0)]
        + [stage_last]
    )

    def tick(t):
        for stage, lag in reversed(list(zip(stages, lags))):
            c = t - lag

            @pl.when((c >= 0) & (c < chunks))
            def _():
                stage(c)

    def give(c, left, right, fresh=False):
        grad = dot(left, right, TN).astype(bf16)
        first = grad[:, 0:HALF]
        second = grad[:, HALF:]

        @pl.when(c >= slots)
        def _():
            rs_copy(c - slots, 0).wait_send()

        staged[c % slots] = jnp.where(core == 0, second, first)
        acc[c] = jnp.where(core == 0, first, second)
        rs_copy(c, 0).start()

    (cot_s, n2_s, low_s, n1_s, pg_s, eg_s) = [wide.at[i] for i in range(6)]
    ag_s = wide.at[10]

    def chunk_load(j):
        cols = pl.ds(pl.multiple_of(j * WIDTH, WIDTH), WIDTH)
        return (
            pltpu.make_async_copy(hid.at[:, cols], wide.at[6 + j % 2], hid_sem.at[0, j]),
            pltpu.make_async_copy(slope.at[:, cols], wide.at[8 + j % 2], hid_sem.at[1, j]),
        )

    cls_in = [
        pltpu.make_async_copy(
            y.at[pl.ds(s * one, 16)], cls_s.at[pl.ds(s * 16, 16)], in_sem.at[20 + s]
        )
        for s in range(seqs)
    ]
    loads = copies(
        [
            (pool, pool_s), (cot, cot_s), (n2, n2_s), (stat, stat_s), (w2, w2_s),
            (low, low_s), (w1, w1_s), (n1, n1_s),
        ],
        in_sem,
    )
    for copy in cls_in + loads[:5]:
        copy.start()
    for copy in chunk_load(0):
        copy.start()
    for copy in loads[5:]:
        copy.start()
    later = copies([(q, wide.at[0]), (k, wide.at[1])], in_sem.at[pl.ds(8, 2)])
    middle = copies([(v, wide.at[6]), (att, wide.at[8])], in_sem.at[pl.ds(10, 2)])
    (x_load,) = copies([(x, wide.at[7])], in_sem.at[pl.ds(12, 1)])
    attn_weights = [
        pltpu.make_async_copy(w, w2_s.at[pl.ds(i * WIDTH, WIDTH)], in_sem.at[13 + i])
        for i, w in enumerate((wo, wq, wk, wv))
    ]

    pl.semaphore_wait(barrier, len(greeted))
    y_moves = []
    own = []
    for s in range(seqs):
        y_moves += spread(y, lay_out, seqs, tokens, False, tok_send, tok_recv, 0, s)
        own.append(own_part(y, lay_out, seqs, tokens, False, tok_own.at[s], s))
    for copy in own + y_moves:
        copy.start()

    for copy in cls_in:
        copy.wait()
    loads[0].wait()
    place = lax.broadcasted_iota(jnp.int32, (16 * seqs, 1), 0)
    labels = jnp.zeros((16 * seqs, 1), jnp.int32)
    label_row = jnp.zeros((1, 128), f32)
    lane = lax.broadcasted_iota(jnp.int32, (1, 128), 1)
    for s in range(seqs):
        label = label_ref[z * seqs + s]
        labels = jnp.where(place == 16 * s, label, labels)
        label_row = jnp.where(lane == s, label.astype(f32), label_row)
    cls_grad = exit_back(cls_s[...], labels, vec_ref, pool_s)
    row_s[...] = jnp.zeros_like(row_s)
    for s in range(seqs):
        first = cls_s[16 * s : 16 * (s + 1), :].astype(f32)
        for j in range(6):
            row_s[s * 6 + j : s * 6 + j + 1, :] = first[0:1, j * 128 : (j + 1) * 128]
    row_s[12:13, :] = label_row
    block = place_of_block()
    head_out[block] = row_s[...].astype(bf16)
    for copy in loads[1:4]:
        copy.wait()
    small_out[...] = jnp.zeros_like(small_out)
    ROW = 128

    def add_sum(index, values):
        small_out[index : index + 1, :] += jnp.sum(values, axis=0, keepdims=True)

    @pl.loop(0, rows // ROW)
    def _(i):
        r = tile(i, ROW)
        upstream = cot_s[r, :].astype(f32)
        place = lax.broadcasted_iota(jnp.int32, (ROW, 1), 0) + i * ROW
        for s in range(seqs):
            upstream = upstream + jnp.where(place == s * one, cls_grad[16 * s : 16 * s + 1, :], 0.0)
        normed = n2_s[r, :].astype(f32)
        add_sum(G2, upstream * normed)
        add_sum(B2, upstream)
        zg = norm_rows_back(upstream, normed, stat_s[r, 13:14], vec_ref[G2 : G2 + 1, :])
        rounded = zg.astype(bf16)
        pg_s[r, :] = rounded
        add_sum(UB, rounded.astype(f32))
        fg_s[r, :] = zg

    for copy in later:
        copy.start()
    for copy in loads[4:7]:
        copy.wait()

    @pl.loop(0, 4)
    def _(j):
        for copy in chunk_load(j):
            copy.wait()

        @pl.when(j < 3)
        def _():
            for copy in chunk_load(j + 1):
                copy.start()

        @pl.when(j == 3)
        def _():
            for copy in middle:
                copy.start()

        @pl.loop(0, WIDTH // 256)
        def _(t):
            cols = tile(t, 256)
            ff = pl.ds(pl.multiple_of(j * WIDTH + t * 256, 256), 256)
            grad = dot(pg_s[...], w2_s[ff, :], NT) * wide[8 + j % 2, :, cols].astype(f32)
            rounded = grad.astype(bf16)
            eg_s[:, cols] = rounded
            small_out[pl.ds(IB + j, 1), cols] = jnp.sum(
                rounded.astype(f32), axis=0, keepdims=True
            )

        for i in range(4):

            @pl.when(j == i)
            def _():
                attn_weights[i].start()

        @pl.loop(0, 3)
        def _(t):
            give(6 * j + t, wide[6 + j % 2, :, tile(t, 256)], pg_s[...])

        tick(3 * j)

        @pl.loop(0, 3)
        def _(t):
            give(6 * j + 3 + t, low_s[:, tile(t, 256)], eg_s[...])

        tick(3 * j + 1)
        ff_cols = pl.ds(pl.multiple_of(j * WIDTH, WIDTH), WIDTH)

        @pl.loop(0, WIDTH // 256)
        def _(t):
            cols = tile(t, 256)
            fg_s[:, cols] += dot(eg_s[...], w1_s[cols, ff_cols], NT)

        tick(3 * j + 2)

    x_load.start()
    loads[7].wait()

    @pl.loop(0, rows // ROW)
    def _(i):
        r = tile(i, ROW)
        upstream = fg_s[r, :]
        normed = n1_s[r, :].astype(f32)
        add_sum(G1, upstream * normed)
        add_sum(B1, upstream)
        zg = norm_rows_back(upstream, normed, stat_s[r, 12:13], vec_ref[G1 : G1 + 1, :])
        rounded = zg.astype(bf16)
        ag_s[r, :] = rounded
        add_sum(OB, rounded.astype(f32))

    tick(12)

    (q_s, k_s, dv_s, sg_s, dq_s, dk_s, v_s, x_s, att_s, dat_s) = [wide.at[i] for i in range(10)]
    wo_s, wq_s, wk_s, wv_s = [w2_s.at[pl.ds(i * WIDTH, WIDTH)] for i in range(4)]
    attn_weights[0].wait()

    @pl.loop(0, WIDTH // 256)
    def _(t):
        cols = tile(t, 256)
        dat_s[:, cols] = dot(ag_s[...], wo_s[cols, :], NT).astype(bf16)

    for copy in middle + later:
        copy.wait()

    @pl.loop(0, 3)
    def _(t):
        give(24 + t, att_s[:, tile(t, 256)], ag_s[...])

    tick(13)
    head_of = lax.broadcasted_iota(jnp.int32, (16, WIDTH), 1) // HEAD_DIM
    picker = (head_of == lax.broadcasted_iota(jnp.int32, (16, WIDTH), 0)).astype(bf16)
    for s in range(seqs):
        part = pl.ds(s * one, one)
        product = dat_s[part, :].astype(f32) * att_s[part, :].astype(f32)
        high = product.astype(bf16)
        rest = (product - high.astype(f32)).astype(bf16)
        rowt_s[s, 128:144, :] = dot(picker, high, NT) + dot(picker, rest, NT)
        rowt_s[s, 0:128, :] = jnp.transpose(stat_s[part, :])

    @pl.loop(0, seqs * 3)
    def _(i):
        s = i // 3
        part = pl.ds(pl.multiple_of(s * one, one), one)
        length = len_ref[z * seqs + s]
        for half in (0, 1):
            p = 2 * (i % 3) + half
            cols = tile(p, 128)
            logs = [rowt_s[s, pl.ds(2 * p + w, 1), :] for w in (0, 1)]
            delta = [rowt_s[s, pl.ds(128 + 2 * p + w, 1), :] for w in (0, 1)]
            dq, dk, dv = attend_back_pair(
                q_s[part, cols], k_s[part, cols], v_s[part, cols], dat_s[part, cols],
                logs, delta, length, one,
            )
            dq_s[part, cols] = dq.astype(bf16)
            dk_s[part, cols] = dk.astype(bf16)
            dv_s[part, cols] = dv.astype(bf16)
        tick(14 + i)

    for copy in attn_weights[1:]:
        copy.wait()
    x_load.wait()

    @pl.loop(0, WIDTH // 256)
    def _(t):
        cols = tile(t, 256)
        total = ag_s[:, cols].astype(f32)
        for d, w in ((dq_s, wq_s), (dk_s, wk_s), (dv_s, wv_s)):
            total = total + dot(d[...], w[cols, :], NT)
        sg_s[:, cols] = total.astype(bf16)
        small_out[QB : QB + 1, cols] = jnp.sum(dq_s[:, cols].astype(f32), axis=0, keepdims=True)
        small_out[VB : VB + 1, cols] = jnp.sum(dv_s[:, cols].astype(f32), axis=0, keepdims=True)

    moves = []
    for s in range(seqs):
        moves += spread(
            sg_s, grad_out, seqs, tokens, False, tok_send, tok_recv, seqs * (count - 1), s
        )
        own.append(own_part(sg_s, grad_out, seqs, tokens, False, tok_own.at[seqs + s], s))
        own[-1].start()
    done = 14 + 3 * seqs
    for i, d in enumerate((dq_s, dk_s, dv_s)):

        @pl.loop(0, 3)
        def _(t):
            give(27 + 3 * i + t, x_s[:, tile(t, 256)], d[...])

        tick(done + i)
    done += 3


    def small_copies(i):
        first = block - block % (1 << i)
        part = pl.ds(first, 1 << i)
        return (
            pltpu.make_async_remote_copy(
                small_out, sgot.at[i], sm_send.at[i], sm_recv.at[i],
                device_id=partners[i], device_id_type=MESH,
            ),
            pltpu.make_async_remote_copy(
                head_out.at[part], head_out.at[part], hd_send.at[i], hd_recv.at[i],
                device_id=partners[i], device_id_type=MESH,
            ),
        )

    move_ticks = [done + 2 * i for i in range(len(moves))]

    def late_tick(t, carry):
        for when, copy in zip(move_ticks, moves):

            @pl.when(t == when)
            def _():
                copy.start()

        for i in range(len(partners) + 1):

            @pl.when(t == done + 3 * i)
            def _():
                if i > 0:
                    for copy in small_copies(i - 1):
                        copy.wait()
                    small_out[...] = small_out[...] + sgot[i - 1]
                if i < len(partners):
                    for copy in small_copies(i):
                        copy.start()

        tick(t)
        return carry

    lax.fori_loop(done, chunks + lags[-1], late_tick, 0)
    for c in range(chunks - slots, chunks):
        rs_copy(c, 0).wait_send()
    for copy in own + y_moves + moves:
        copy.wait()


def back(seqs, tokens, lengths, labels, vecs, saved, weights):
    rows, width = saved[0].shape
    ff = 4 * width
    one = rows // seqs
    count = lax.axis_size("seq")
    chunks = 12 * width // CHUNK
    moves = 2 * seqs * (count - 1)
    dma = pltpu.SemaphoreType.DMA
    anywhere = pl.BlockSpec(memory_space=pl.ANY)
    in_vmem = pl.BlockSpec(memory_space=pltpu.VMEM)
    in_smem = pl.BlockSpec(memory_space=pltpu.SMEM)
    block = jax.ShapeDtypeStruct((seqs * count, tokens, width), bf16)
    small = (16, width)
    half = functools.partial(pltpu.VMEM, dtype=bf16)
    total, small, head, lay, grad = pl.pallas_call(
        functools.partial(back_kernel, seqs, chunks, "xy", tuple(3 * i for i in range(10))),
        out_shape=(
            jax.ShapeDtypeStruct((12 * width, width), bf16),
            jax.ShapeDtypeStruct(small, f32),
            jax.ShapeDtypeStruct((32, 16, 128), bf16),
            block,
            block,
        ),
        in_specs=[in_smem, in_smem, in_vmem] + [anywhere] * (len(saved) + len(weights)),
        out_specs=(anywhere, in_vmem, in_vmem, anywhere, anywhere),
        scratch_shapes=[
            pltpu.VMEM((11, rows, width), bf16), pltpu.VMEM((rows, width), f32),
            pltpu.VMEM((rows, 128), f32), pltpu.VMEM((width, ff), bf16),
            pltpu.VMEM((ff, width), bf16), pltpu.VMEM((width, width), bf16),
            pltpu.VMEM((16 * seqs, width), bf16), pltpu.VMEM((16, 128), f32),
            pltpu.VMEM((seqs, 144, one), f32),
            pltpu.VMEM((chunks, CHUNK, HALF), bf16),
            pltpu.VMEM((6, CHUNK, HALF), bf16),
            pltpu.VMEM((chunks, CHUNK, HALF), bf16),
            pltpu.VMEM((chunks, CHUNK // 2, HALF), bf16),
            pltpu.VMEM((chunks, CHUNK // 4, HALF), bf16),
            pltpu.VMEM((chunks, CHUNK // 8, HALF), bf16),
            pltpu.VMEM((chunks, CHUNK // 16, HALF), bf16),
            pltpu.VMEM((5,) + small, f32),
            dma((20 + seqs,)), dma((2, 4)),
            dma((5, chunks)), dma((5, chunks)), dma((5, chunks)), dma((5, chunks)),
            dma((chunks,)), dma((5,)), dma((5,)), dma((5,)), dma((5,)),
            dma((moves,)), dma((moves,)), dma((2 * seqs,)),
        ],
        compiler_params=pltpu.CompilerParams(
            collective_id=0, has_side_effects=True, vmem_limit_bytes=62 * 2**20
        ),
        cost_estimate=pl.CostEstimate(
            flops=8 * rows * width * ff + 16 * rows * width * width + 10 * rows * one * width,
            bytes_accessed=100 * 2**20, transcendentals=12 * rows * one,
        ),
        name="back",
    )(lengths, labels, vecs, *saved, *weights)
    blocks = lax.axis_size("batch") // 8
    if blocks > 1:
        alike = [[i + 8 * j for j in range(blocks)] for i in range(8)]
        total = lax.psum(total, "batch", axis_index_groups=alike)
        small = lax.psum(small, "batch", axis_index_groups=alike)
        head = lax.all_gather(head, "batch", axis_index_groups=alike, axis=0, tiled=True)
    return total.reshape(12, width, width), small, head, lay, grad


def finish_kernel(
    total, small_ref, cls_ref, label_ref, vec_ref, pool_ref, lay_in, grad_in,
    lay_out, loss_out, grad_out, gq, gk, gv, go, gqb, gvb, gob, gg1, gb1, gin, gib, gou, gub,
    gg2, gb2, gpool, gpb, gcp, gcb,
    low_s, full_s, pool_s, pass_s, in_sem, out_sem,
):
    units = low_s.shape[0]
    group = loss_out.shape[0]
    seqs = cls_ref.shape[0]
    loads = [pltpu.make_async_copy(total.at[u], low_s.at[u], in_sem.at[u]) for u in range(units)]
    for copy in loads:
        copy.start()
    places = []
    for j in range(4):
        part = pl.ds(j * WIDTH, WIDTH)
        places += [gou.at[part], gin.at[:, part]]
    places += [go, gq, gk, gv]
    stores = [
        pltpu.make_async_copy(full_s.at[u], places[u], out_sem.at[u]) for u in range(units)
    ]
    passed_in = [
        pltpu.make_async_copy(src, pass_s.at[i], in_sem.at[units + i])
        for i, src in enumerate((lay_in, grad_in))
    ]
    passed = [
        pltpu.make_async_copy(pass_s.at[i], dst, out_sem.at[units + i])
        for i, dst in enumerate((lay_out, grad_out))
    ]
    for copy in passed_in:
        copy.start()
    pool_store = pltpu.make_async_copy(pool_s, gpool, out_sem.at[units + 2])

    def widen(u):
        loads[u].wait()

        @pl.loop(0, WIDTH // 128)
        def _(i):
            r = tile(i, 128)
            full_s[u, r, :] = low_s[u, r, :].astype(f32)

        stores[u].start()

    for u in range(4):
        widen(u)
    for before, after in zip(passed_in, passed):
        before.wait()
        after.start()

    def exact(left, right, dims=NN):
        return lax.dot_general(left, right, dims, precision=highest, preferred_element_type=f32)

    pooled = jnp.tanh(dot(cls_ref[...], pool_ref[...]) + vec_ref[PB : PB + 1, :])
    row = lax.broadcasted_iota(jnp.int32, (8, 1), 0)
    class_rows = jnp.where(row < 3, vec_ref[CP : CP + 8, :], 0.0)
    picked = jnp.where(
        row == lax.broadcasted_iota(jnp.int32, (8, 128), 1), vec_ref[CB : CB + 1, 0:128], 0.0
    )
    logits = exact(class_rows, pooled, NT) + jnp.sum(picked, axis=-1, keepdims=True)
    logits = jnp.where(row < 3, logits, masked_fill)
    top = jnp.max(logits, axis=0, keepdims=True)
    raised = jnp.exp(logits - top)
    total_row = jnp.sum(raised, axis=0, keepdims=True)
    chosen = (row == label_ref[...]).astype(f32)
    losses = (top + jnp.log(total_row)) - jnp.sum(
        jnp.where(chosen > 0.0, logits, 0.0), axis=0, keepdims=True
    )
    logit_grad = raised / total_row - chosen
    first = lax.axis_index("batch") * group
    pickers = (
        lax.broadcasted_iota(jnp.int32, (seqs, 128), 0)
        == lax.broadcasted_iota(jnp.int32, (seqs, 128), 1) + first
    ).astype(f32)
    loss_out[...] = exact(losses, pickers)[0, 0:group]
    pre = exact(logit_grad, class_rows, TN) * (1.0 - pooled * pooled)
    ones = jnp.ones((1, seqs), f32)
    gcb[...] = exact(ones, logit_grad, NT)[0, 0:3]
    gpb[...] = jnp.sum(pre, axis=0)
    gcp[...] = exact(pooled, logit_grad, (((0,), (1,)), ((), ())))[:, 0:3]
    high = pre.astype(bf16)
    rest = pre - high.astype(f32)
    mid = rest.astype(bf16)
    low = (rest - mid.astype(f32)).astype(bf16)
    for j in range(3):
        cols = pl.ds(j * 256, 256)
        cls = cls_ref[:, cols]
        pool_s[cols, :] = dot(cls, high, TN) + dot(cls, mid, TN) + dot(cls, low, TN)
    pool_store.start()
    for i, ref in (
        (QB, gqb), (VB, gvb), (OB, gob), (G1, gg1), (B1, gb1), (UB, gub), (G2, gg2), (B2, gb2),
    ):
        ref[...] = small_ref[i, :]
    for j in range(4):
        gib[j * WIDTH : (j + 1) * WIDTH] = small_ref[IB + j, :]
    for u in range(4, units):
        widen(u)
    for copy in stores + passed + [pool_store]:
        copy.wait()


def finish(total, small, cls, labels, vecs, pool, lay, grad):
    group, tokens, width = lay.shape
    anywhere = pl.BlockSpec(memory_space=pl.ANY)
    in_vmem = pl.BlockSpec(memory_space=pltpu.VMEM)
    square = ((width, width), f32, anywhere)
    row = ((width,), f32, in_vmem)
    outs = (
        [(lay.shape, bf16, anywhere), ((group,), f32, in_vmem), (grad.shape, bf16, anywhere)]
        + [square] * 4
        + [row] * 5
        + [((width, 4 * width), f32, anywhere), ((4 * width,), f32, in_vmem)]
        + [((4 * width, width), f32, anywhere), row, row, row]
        + [square, row, ((width, 3), f32, in_vmem), ((3,), f32, in_vmem)]
    )
    units = total.shape[0]
    return pl.pallas_call(
        finish_kernel,
        out_shape=tuple(jax.ShapeDtypeStruct(s, t) for s, t, _ in outs),
        in_specs=[anywhere] + [in_vmem] * 5 + [anywhere, anywhere],
        out_specs=tuple(m for _, _, m in outs),
        scratch_shapes=[
            pltpu.VMEM((units, width, width), bf16), pltpu.VMEM((units, width, width), f32),
            pltpu.VMEM((width, width), f32), pltpu.VMEM((2,) + lay.shape, bf16),
            pltpu.SemaphoreType.DMA((units + 2,)), pltpu.SemaphoreType.DMA((units + 3,)),
        ],
        compiler_params=pltpu.CompilerParams(vmem_limit_bytes=60 * 2**20),
        name="finish",
    )(total, small, cls, labels, vecs, pool, lay, grad)


def local(
    states, lengths, labels, cotangent,
    query_proj, key_proj, value_proj, output_proj,
    query_bias, value_bias, output_bias, first_gain, first_bias,
    inner_proj, inner_bias, outer_proj, outer_bias, second_gain, second_bias,
    pool_proj, pool_bias, class_proj, class_bias,
):
    group, tokens, width = states.shape
    seqs = group // lax.axis_size("seq")
    (
        vecs, x, upstream, q, k, v, att, n1, low, hid, slope, n2, stat, y,
    ) = forward(
        lengths, states, cotangent,
        (query_proj, key_proj, value_proj, output_proj, inner_proj, outer_proj),
        (query_bias, value_bias, output_bias, first_gain, first_bias, inner_bias, outer_bias,
         second_gain, second_bias, pool_bias, class_proj, class_bias),
    )
    total, small, head, lay, grad = back(
        seqs, tokens, lengths, labels, vecs,
        (upstream, n2, hid, slope, low, n1, stat, y, q, k, v, att, x),
        (inner_proj, outer_proj, pool_proj, query_proj, key_proj, value_proj, output_proj),
    )
    cls = head[:, 0 : 6 * seqs].reshape(-1, width)
    label_row = head[:, 6 * seqs, 0:seqs].reshape(1, -1).astype(jnp.int32)
    return finish(total, small, cls, label_row, vecs, pool_proj, lay, grad)


def solution(mesh):
    split = P("batch", "seq", None)
    in_specs = (split, P("batch"), P("batch"), split) + (P(),) * 19
    out_specs = (split, P("batch"), split) + (P(),) * 19
    return jax.shard_map(local, mesh=mesh, in_specs=in_specs, out_specs=out_specs, check_vma=False)
```

```python
import functools

import jax
import jax.numpy as jnp
from jax import lax
from jax.experimental import pallas as pl
from jax.experimental.pallas import tpu as pltpu
from jax.sharding import PartitionSpec as P

HEADS = 12
HEAD_DIM = 64
WIDTH = 768
HALF = 384
CHUNK = 256
MESH = pl.DeviceIdType.MESH

bf16 = jnp.bfloat16
f32 = jnp.float32
highest = lax.Precision.HIGHEST
norm_eps = 1e-06
masked_fill = -1e30
inv_root_two = 0.7071067811865476
inv_root_tau = 0.3989422804014327


def pick(code, table):
    out = table[-1]
    for i in range(len(table) - 2, -1, -1):
        out = jnp.where(code == i, table[i], out)
    return out


def flipped(index, bit):
    return index + bit * (1 - 2 * ((index // bit) % 2))


NT = (((1,), (1,)), ((), ()))
NN = (((1,), (0,)), ((), ()))
TN = (((0,), (0,)), ((), ()))
VECS = 24
QB, VB, OB, G1, B1, IB, UB, G2, B2, PB, CP, CB = 0, 1, 2, 3, 4, 5, 9, 10, 11, 12, 13, 16


def dot(left, right, dims=NN):
    return lax.dot_general(left, right, dims, preferred_element_type=f32)


def gelu_parts(u):
    t = 1.0 / (1.0 + (0.3275911 * inv_root_two) * jnp.abs(u))
    bell = jnp.exp(-0.5 * u * u)
    poly = 1.061405429
    for coefficient in (-1.453152027, 1.421413741, -0.284496736, 0.254829592):
        poly = poly * t + coefficient
    tail = (0.5 * t) * poly * bell
    cumulative = jnp.where(u >= 0.0, 1.0 - tail, tail)
    return u * cumulative, cumulative + u * (bell * inv_root_tau)


def norm_rows(z):
    average = jnp.mean(z, axis=-1, keepdims=True)
    centered = z - average
    inv_root = lax.rsqrt(jnp.mean(centered * centered, axis=-1, keepdims=True) + norm_eps)
    return centered * inv_root, inv_root


def norm_rows_back(upstream, normed, inv_root, gain):
    scaled = upstream * gain
    return inv_root * (
        scaled
        - jnp.mean(scaled, axis=-1, keepdims=True)
        - normed * jnp.mean(scaled * normed, axis=-1, keepdims=True)
    )


def tile(i, size):
    return pl.ds(pl.multiple_of(i * size, size), size)


def copies(pairs, sems):
    out = []
    for i, (src, dst) in enumerate(pairs):
        out.append(pltpu.make_async_copy(src, dst, sems.at[i]))
    return out


def head_lanes(which):
    lane = lax.broadcasted_iota(jnp.int32, (1, 128), 1)
    return (lane >= 64) if which else (lane < 64)


def only(mask, block):
    return jnp.where(mask, block, jnp.zeros_like(block))


def attend_pair(q2, k2, v2, length, keys):
    k2 = k2[:keys]
    v2 = v2[:keys]
    place = lax.broadcasted_iota(jnp.int32, (1, keys), 1)
    out = None
    logs = []
    for which in (0, 1):
        lanes = head_lanes(which)
        scores = dot(only(lanes, q2) * bf16(0.125), k2, NT)
        scores = jnp.where(place < length, scores, masked_fill)
        top = jnp.max(scores, axis=-1, keepdims=True)
        weights = jnp.exp(scores - top)
        total = jnp.sum(weights, axis=-1, keepdims=True)
        part = dot(weights.astype(bf16), only(lanes, v2)) * (1.0 / total)
        out = part if out is None else out + part
        logs.append(top + jnp.log(total))
    return out, logs


def three_terms(values):
    high = values.astype(bf16).astype(f32)
    mid = (values - high).astype(bf16).astype(f32)
    return high, mid, values - high - mid


def attend_back_pair(q2, k2, v2, d2, a2, q_aux, key_aux, value_aux):
    lane = lax.broadcasted_iota(jnp.int32, (1, 128), 1)
    product = d2.astype(f32) * a2.astype(f32)
    d_aux = jnp.zeros_like(product)
    for which in (0, 1):
        delta = jnp.sum(only(head_lanes(which), product), axis=-1, keepdims=True)
        for i, piece in enumerate(three_terms(-delta)):
            d_aux = jnp.where(lane == 64 * (1 - which) + i, piece, d_aux)
    d_aux = d_aux.astype(bf16)
    q2 = q2 * bf16(0.125)
    heads = []
    for which in (0, 1):
        lanes = head_lanes(which)
        heads.append(
            [
                jnp.where(lanes, block, other)
                for block, other in ((q2, q_aux), (k2, key_aux), (v2, value_aux), (d2, d_aux))
            ]
        )
    scores = [dot(kh, qh, NT) for qh, kh, _, _ in heads]
    prob_grads = [dot(vh, dh, NT) for _, _, vh, dh in heads]
    probs = [jnp.exp(s) for s in scores]
    score_grads = [(p * g).astype(bf16) for p, g in zip(probs, prob_grads)]
    out = [
        (dot(g, kh, TN), dot(g, qh), dot(p.astype(bf16), dh))
        for g, p, (qh, kh, _, dh) in zip(score_grads, probs, heads)
    ]
    first = head_lanes(0)
    dq, dk, dv = [jnp.where(first, one, two) for one, two in zip(*out)]
    return dq * 0.125, dk, dv


def exit_back(cls_rows, labels, vec_ref, pool_s):
    pooled = jnp.tanh(dot(cls_rows, pool_s[...]) + vec_ref[PB : PB + 1, :])
    class_rows = vec_ref[CP : CP + 3, :]
    logits = [
        jnp.sum(pooled * class_rows[i : i + 1, :], axis=-1, keepdims=True)
        + vec_ref[CB : CB + 1, i : i + 1]
        for i in range(3)
    ]
    top = jnp.maximum(jnp.maximum(logits[0], logits[1]), logits[2])
    raised = [jnp.exp(l - top) for l in logits]
    total = raised[0] + raised[1] + raised[2]
    back = jnp.zeros_like(pooled)
    for i in range(3):
        back = back + (raised[i] / total - (labels == i).astype(f32)) * class_rows[i : i + 1, :]
    pre = back * (1.0 - pooled * pooled)
    high = pre.astype(bf16)
    rest = pre - high.astype(f32)
    mid = rest.astype(bf16)
    low = (rest - mid.astype(f32)).astype(bf16)
    return dot(high, pool_s[...], NT) + dot(mid, pool_s[...], NT) + dot(low, pool_s[...], NT)


def spread(src, dst, seqs, tokens, to_rows, sends, recvs, base, s, ordered=False):
    count = lax.axis_size("seq")
    b = lax.axis_index("batch")
    z = lax.axis_index("seq")
    out = []
    for d in range(1, count):
        if ordered and count == 4:
            d = jnp.where(z % 2 == 0, d % 3 + 1, d)
        other = lax.rem(z + d, count)
        if to_rows:
            source = src.at[other * seqs + s]
            target = dst.at[pl.ds(pl.multiple_of((s * count + z) * tokens, tokens), tokens)]
        else:
            source = src.at[pl.ds(pl.multiple_of((s * count + other) * tokens, tokens), tokens)]
            target = dst.at[z * seqs + s]
        i = base + s * (count - 1) + d - 1
        out.append(
            pltpu.make_async_remote_copy(
                source, target, sends.at[i], recvs.at[i],
                device_id=(b, other), device_id_type=MESH,
            )
        )
    return out


def own_part(src, dst, seqs, tokens, to_rows, sem, s):
    count = lax.axis_size("seq")
    z = lax.axis_index("seq")
    block = z * seqs + s
    rows = pl.ds(pl.multiple_of((s * count + z) * tokens, tokens), tokens)
    if to_rows:
        return pltpu.make_async_copy(src.at[block], dst.at[rows], sem)
    return pltpu.make_async_copy(src.at[rows], dst.at[block], sem)


def greet_line():
    count = lax.axis_size("seq")
    z = lax.axis_index("seq")
    return [(lax.axis_index("batch"), lax.rem(z + d, count)) for d in range(1, count)]


def forward_kernel(
    seqs, len_ref, label_ref, states, cot, wq, wk, wv, wo, w1, w2, pool,
    query_bias, value_bias, output_bias, first_gain, first_bias, inner_bias, outer_bias,
    second_gain, second_bias, pool_bias, class_proj, class_bias,
    vec_ref, small_out, head_out, x_out, q_out, k_out, v_out, att_out, n1_out, low_out, hid_out,
    slope_out, stat_out, y_out, aux_out, pg_out,
    x_s, wq_s, wk_s, wv_s, wo_s, w1_s, w2_s,
    q_s, k_s, v_s, att_s, n1_s, low_s, hid_s, slope_s, stat_s, y_s, aux_s, n2_s, z_s,
    cot_s, pool_s, row_s, in_sem, out_sem, own_sem, sends, recvs,
):
    rows = z_s.shape[0]
    tokens = states.shape[1]
    line = greet_line()
    barrier = pltpu.get_barrier_semaphore()
    for who in line:
        pl.semaphore_signal(barrier, inc=1, device_id=who, device_id_type=MESH)
    weights_in = copies(
        [(wq, wq_s), (wk, wk_s), (wv, wv_s), (wo, wo_s), (w1, w1_s), (w2, w2_s), (pool, pool_s)],
        in_sem,
    )
    z = lax.axis_index("seq")
    own = [own_part(states, x_s, seqs, tokens, True, own_sem.at[s], s) for s in range(seqs)]
    own_cot = [
        own_part(cot, cot_s, seqs, tokens, True, own_sem.at[seqs + s], s) for s in range(seqs)
    ]
    for copy in own + weights_in + own_cot:
        copy.start()
    pl.semaphore_wait(barrier, len(line))

    def move(first, s, ordered):
        src, dst, start = (states, x_s, 0) if first else (cot, cot_s, seqs * len(line))
        return spread(src, dst, seqs, tokens, True, sends, recvs, start, s, ordered)

    moves = [move(True, s, False) for s in range(seqs)]
    late = [move(False, s, False) for s in range(seqs)]
    for copy in move(True, 0, True):
        copy.start()
    vec_ref[...] = jnp.zeros_like(vec_ref)
    for i, ref in (
        (QB, query_bias), (VB, value_bias), (OB, output_bias), (G1, first_gain), (B1, first_bias),
        (UB, outer_bias), (G2, second_gain), (B2, second_bias), (PB, pool_bias),
    ):
        vec_ref[i : i + 1, :] = ref[...].astype(f32).reshape(1, WIDTH)
    for i in range(4):
        vec_ref[IB + i : IB + i + 1, :] = (
            inner_bias[i * WIDTH : (i + 1) * WIDTH].astype(f32).reshape(1, WIDTH)
        )
    vec_ref[CP : CP + 3, :] = class_proj[...].astype(f32)
    vec_ref[CB : CB + 1, 0:3] = class_bias[...].astype(f32).reshape(1, 3)

    waiting = []
    def send_late(s):
        for copy in move(False, s, True):
            copy.start()

    for s in range(seqs):
        for copy in moves[s]:
            copy.wait_recv()
        own[s].wait()
        if s == 0:
            for i in range(1, seqs):
                for copy in move(True, i, True):
                    copy.start()
        part = pl.ds(s * rows, rows)
        waiting += forward_rows(
            s, part, len_ref[z * seqs + s], rows, s == 0, vec_ref, weights_in,
            (lambda: send_late(0)) if s == 0 else None,
            (x_s, wq_s, wk_s, wv_s, wo_s, w1_s, w2_s, q_s, k_s, v_s, att_s, n1_s, low_s, hid_s,
             slope_s, stat_s, y_s, aux_s, n2_s, z_s),
            (x_out, q_out, k_out, v_out, att_out, n1_out, low_out, hid_out, slope_out,
             stat_out, y_out, aux_out),
            out_sem,
        )
        if s == 0:
            for i in range(1, seqs):
                send_late(i)

    place = lax.broadcasted_iota(jnp.int32, (16 * seqs, 1), 0)
    labels = jnp.zeros((16 * seqs, 1), jnp.int32)
    label_row = jnp.zeros((1, 128), f32)
    lane = lax.broadcasted_iota(jnp.int32, (1, 128), 1)
    for s in range(seqs):
        label = label_ref[z * seqs + s]
        labels = jnp.where(place == 16 * s, label, labels)
        label_row = jnp.where(lane == s, label.astype(f32), label_row)
    cls_rows = jnp.concatenate([y_s[s * rows : s * rows + 16, :] for s in range(seqs)])
    weights_in[6].wait()
    cls_grad = exit_back(cls_rows, labels, vec_ref, pool_s)
    row_s[...] = jnp.zeros_like(row_s)
    for s in range(seqs):
        first = y_s[s * rows : s * rows + 16, :].astype(f32)
        for j in range(6):
            row_s[s * 6 + j : s * 6 + j + 1, :] = first[0:1, j * 128 : (j + 1) * 128]
    row_s[6 * seqs : 6 * seqs + 1, :] = label_row
    head_out[...] = row_s[...].astype(bf16)
    small_out[...] = jnp.zeros_like(small_out)

    def add_sum(index, values):
        small_out[index : index + 1, :] += jnp.sum(values, axis=0, keepdims=True)

    for s in range(seqs):
        for copy in late[s]:
            copy.wait_recv()
        own_cot[s].wait()

        @pl.loop(0, rows // 128)
        def _(i):
            r = pl.ds(pl.multiple_of(s * rows + i * 128, 128), 128)
            place = lax.broadcasted_iota(jnp.int32, (128, 1), 0) + i * 128
            upstream = cot_s[r, :].astype(f32) + jnp.where(
                place == 0, cls_grad[16 * s : 16 * s + 1, :], 0.0
            )
            normed = n2_s[r, :].astype(f32)
            add_sum(G2, upstream * normed)
            add_sum(B2, upstream)
            grad = norm_rows_back(upstream, normed, stat_s[r, 13:14], vec_ref[G2 : G2 + 1, :])
            rounded = grad.astype(bf16)
            n2_s[r, :] = rounded
            add_sum(UB, rounded.astype(f32))

        part = pl.ds(s * rows, rows)
        waiting.append(pltpu.make_async_copy(n2_s.at[part], pg_out.at[part], out_sem.at[s, 12]))
        waiting[-1].start()
    for group in moves + late:
        for copy in group:
            copy.wait_send()
    for copy in waiting:
        copy.wait()


def forward_rows(
    s, part, length, rows, first_time, vec_ref, weights_in, halfway, scratch, outs, out_sem
):
    (x_s, wq_s, wk_s, wv_s, wo_s, w1_s, w2_s, q_s, k_s, v_s, att_s, n1_s, low_s, hid_s,
     slope_s, stat_s, y_s, aux_s, n2_s, z_s) = scratch
    start = s * rows
    out = [
        pltpu.make_async_copy(src.at[part], dst.at[part], out_sem.at[s, i])
        for i, (src, dst) in enumerate(
            zip(
                (x_s, q_s, k_s, v_s, att_s, n1_s, low_s, hid_s, slope_s, stat_s, y_s, aux_s), outs
            )
        )
    ]
    out[0].start()
    for i, (w, dst, bias) in enumerate(((wq_s, q_s, QB), (wk_s, k_s, None), (wv_s, v_s, VB))):
        if first_time:
            weights_in[i].wait()

        @pl.loop(0, WIDTH // 256)
        def _(j):
            cols = tile(j, 256)
            grid = dot(x_s[part, :], w[:, cols])
            if bias is not None:
                grid = grid + vec_ref[bias : bias + 1, cols]
            dst[part, cols] = grid.astype(bf16)

        out[1 + i].start()

    stat_s[part, :] = jnp.zeros((rows, 128), f32)
    lane = lax.broadcasted_iota(jnp.int32, (1, 128), 1)

    @pl.loop(0, HEADS // 2)
    def _(p):
        cols = tile(p, 128)
        mix, logs = attend_pair(q_s[part, cols], k_s[part, cols], v_s[part, cols], length, rows)
        att_s[part, cols] = mix.astype(bf16)
        aux = jnp.where((lane == 3) | (lane == 67), 1.0, jnp.zeros((rows, 128), f32))
        for which in (0, 1):
            for i, piece in enumerate(three_terms(-logs[which])):
                aux = jnp.where(lane == 64 * (1 - which) + i, piece, aux)
        aux_s[part, cols] = aux.astype(bf16)

    out[4].start()
    out[11].start()
    if halfway is not None:
        halfway()
    if first_time:
        weights_in[3].wait()

    @pl.loop(0, WIDTH // 256)
    def _(j):
        cols = tile(j, 256)
        z_s[:, cols] = (
            x_s[part, cols].astype(f32)
            + dot(att_s[part, :], wo_s[:, cols])
            + vec_ref[OB : OB + 1, cols]
        )

    @pl.loop(0, rows // 128)
    def _(i):
        r = tile(i, 128)
        q = pl.ds(pl.multiple_of(start + i * 128, 128), 128)
        normed, inv_root = norm_rows(z_s[r, :])
        n1_s[q, :] = normed.astype(bf16)
        first = normed * vec_ref[G1 : G1 + 1, :] + vec_ref[B1 : B1 + 1, :]
        low_s[q, :] = first.astype(bf16)
        z_s[r, :] = first + vec_ref[UB : UB + 1, :]
        stat_s[q, :] = jnp.where(lane == 12, inv_root, stat_s[q, :])

    out[5].start()
    out[6].start()
    if first_time:
        weights_in[4].wait()
        weights_in[5].wait()
    ft = 256

    @pl.loop(0, 4 * WIDTH // ft)
    def _(j):
        cols = tile(j, ft)
        u = dot(low_s[part, :], w1_s[:, cols]) + vec_ref[pl.ds(IB + j // 3, 1), tile(j % 3, ft)]
        h, slope = gelu_parts(u)
        hid_s[part, cols] = h.astype(bf16)
        slope_s[part, cols] = slope.astype(bf16)

    out[7].start()
    out[8].start()

    @pl.loop(0, WIDTH // 256)
    def _(j):
        cols = tile(j, 256)
        z_s[:, cols] += dot(hid_s[part, :], w2_s[:, cols])

    @pl.loop(0, rows // 128)
    def _(i):
        r = tile(i, 128)
        q = pl.ds(pl.multiple_of(start + i * 128, 128), 128)
        normed, inv_root = norm_rows(z_s[r, :])
        n2_s[q, :] = normed.astype(bf16)
        y_s[q, :] = (normed * vec_ref[G2 : G2 + 1, :] + vec_ref[B2 : B2 + 1, :]).astype(bf16)
        stat_s[q, :] = jnp.where(lane == 13, inv_root, stat_s[q, :])

    for i in (9, 10):
        out[i].start()
    return out


def forward(lengths, labels, states, cotangent, weights, small):
    count = lax.axis_size("seq")
    group, tokens, width = states.shape
    seqs = group // count
    one = count * tokens
    rows = seqs * one
    ff = 4 * width
    anywhere = pl.BlockSpec(memory_space=pl.ANY)
    in_vmem = pl.BlockSpec(memory_space=pltpu.VMEM)
    wide = ((rows, width), bf16)
    saved = [wide] * 6 + [((rows, ff), bf16)] * 2 + [((rows, 128), f32), wide, wide, wide]
    outs = [((VECS, width), f32), ((16, width), f32), ((16, 128), bf16), wide] + saved
    moves = 2 * seqs * (count - 1)
    flops = 2 * rows * width * (4 * width + 2 * ff) + 4 * rows * one * width
    dma = pltpu.SemaphoreType.DMA
    return pl.pallas_call(
        functools.partial(forward_kernel, seqs),
        out_shape=tuple(jax.ShapeDtypeStruct(s, t) for s, t in outs),
        in_specs=[pl.BlockSpec(memory_space=pltpu.SMEM)] * 2
        + [anywhere] * 9
        + [in_vmem] * len(small),
        out_specs=(in_vmem,) * 3 + (anywhere,) * (len(outs) - 3),
        scratch_shapes=[pltpu.VMEM((rows, width), bf16)]
        + [pltpu.VMEM(w.shape, bf16) for w in weights[:6]]
        + [pltpu.VMEM(s, t) for s, t in saved]
        + [
            pltpu.VMEM((one, width), f32), pltpu.VMEM((rows, width), bf16),
            pltpu.VMEM((width, width), bf16), pltpu.VMEM((16, 128), f32),
            dma((7,)), dma((seqs, 13)), dma((2 * seqs,)),
            dma((moves,)), dma((moves,)),
        ],
        compiler_params=pltpu.CompilerParams(
            collective_id=1, has_side_effects=True, vmem_limit_bytes=60 * 2**20
        ),
        cost_estimate=pl.CostEstimate(
            flops=flops, bytes_accessed=50 * 2**20, transcendentals=rows * (ff + 12 * one)
        ),
        name="forward",
    )(lengths, labels, states, cotangent, *weights, *small)


def place_of_block():
    return (lax.axis_index("batch") % 8) * 4 + lax.axis_index("seq")


def back_kernel(
    seqs, chunks, pattern, lags, len_ref, vec_ref, small_ref, head_ref,
    pg, hid, slope, low, n1, stat, y, q, k, v, att, x, aux,
    w1, w2, wq, wk, wv, wo,
    out_ref, small_out, head_out, lay_out, grad_out,
    wide, fg_s, stat_s, w1_s, w2_s,
    acc, staged, r0, r1, r2, r3, r4, sgot, own_s,
    in_sem, hid_sem, rs_send, rs_recv, ag_send, ag_recv, loc, sm_send, sm_recv, hd_send, hd_recv,
    tok_send, tok_recv, tok_own,
):
    rows = fg_s.shape[0]
    one = rows // seqs
    tokens = lay_out.shape[1]
    count = lax.axis_size("seq")
    b = lax.axis_index("batch")
    z = lax.axis_index("seq")
    core = b % 2

    got = [r0, r1, r2, r3, r4]
    res = r0
    near_b = [flipped(b, 2), flipped(b, 4), b, b]
    near_z = [z, z, flipped(z, 1), flipped(z, 2)]
    mine = [(b // 2) % 2, (b // 4) % 2, z % 2, (z // 2) % 2]
    orders = {"x": (0, 1, 2, 3), "y": (1, 0, 2, 3)}
    period = len(pattern)

    def direction(c, level):
        code = c % period
        dirs = [orders[p][level] for p in pattern]
        return (
            pick(code, [near_b[d] for d in dirs]),
            pick(code, [near_z[d] for d in dirs]),
            pick(code, [mine[d] for d in dirs]),
        )

    core_partner = (flipped(b, 1), z)
    barrier = pltpu.get_barrier_semaphore()
    partners = [(near_b[2], near_z[2]), (near_b[3], near_z[3]), core_partner]
    partners += [(near_b[0], near_z[0]), (near_b[1], near_z[1])]
    greeted = [core_partner, (near_b[0], near_z[0]), (near_b[1], near_z[1])] + greet_line()
    for who in greeted:
        pl.semaphore_signal(barrier, inc=1, device_id=who, device_id_type=MESH)

    def base(c, level):
        first = 0
        size = CHUNK
        for l in range(level):
            size = size // 2
            first = first + direction(c, l)[2] * size
        return pl.multiple_of(first, 16)

    slots = staged.shape[0]
    my_cols = pl.ds(pl.multiple_of(core * HALF, HALF), HALF)

    def rs_copy(c, s):
        if s == 0:
            return pltpu.make_async_remote_copy(
                staged.at[c % slots], r0.at[c], rs_send.at[0, c], rs_recv.at[0, c],
                device_id=core_partner, device_id_type=MESH,
            )
        size = CHUNK >> s
        nb, nz, m = direction(c, s - 1)
        start = pl.multiple_of(base(c, s - 1) + (1 - m) * size, 16)
        return pltpu.make_async_remote_copy(
            acc.at[c, pl.ds(start, size)], got[s].at[c], rs_send.at[s, c], rs_recv.at[s, c],
            device_id=(nb, nz), device_id_type=MESH,
        )

    def out_rows(c):
        return out_ref.at[pl.ds(pl.multiple_of(c * CHUNK, CHUNK), CHUNK), my_cols]

    def ag_copy(c, s):
        if s == 0:
            return pltpu.make_async_remote_copy(
                res.at[c], out_rows(c), ag_send.at[0, c], ag_recv.at[0, c],
                device_id=core_partner, device_id_type=MESH,
            )
        size = CHUNK >> s
        nb, nz, _ = direction(c, s - 1)
        start = base(c, s)
        return pltpu.make_async_remote_copy(
            res.at[c, pl.ds(start, size)], res.at[c, pl.ds(start, size)],
            ag_send.at[s, c], ag_recv.at[s, c], device_id=(nb, nz), device_id_type=MESH,
        )

    def loc_out(c):
        return pltpu.make_async_copy(res.at[c], out_rows(c), loc.at[c])

    def stage_scatter(s, c):
        rs_copy(c, s - 1).wait_recv()
        half = CHUNK >> s
        start = base(c, s - 1)
        m = direction(c, s - 1)[2]
        for which in (0, 1):
            off = pl.multiple_of(((1 - m) if which == 0 else m) * half, 16)
            part = pl.ds(pl.multiple_of(start + off, 16), half)
            acc[c, part] = acc[c, part] + got[s - 1][c, pl.ds(off, half)]
            if which == 0:
                rs_copy(c, s).start()

    def stage_turn(c):
        rs_copy(c, 4).wait_recv()
        part = pl.ds(base(c, 4), 16)
        res[c, part] = acc[c, part] + r4[c]
        ag_copy(c, 4).start()

    def stage_gather(s, c):
        ag_copy(c, s + 1).wait_recv()
        ag_copy(c, s).start()
        if s == 0:
            loc_out(c).start()

    def stage_last(c):
        ag_copy(c, 0).wait_recv()
        loc_out(c).wait()
        for s in range(1, 5):
            rs_copy(c, s).wait_send()
        for s in range(5):
            ag_copy(c, s).wait_send()

    stages = (
        [functools.partial(stage_scatter, s) for s in (1, 2, 3, 4)]
        + [stage_turn]
        + [functools.partial(stage_gather, s) for s in (3, 2, 1, 0)]
        + [stage_last]
    )

    piece = tokens // 4
    per_seq = 4 * (count - 1)

    def send_piece(src, dst, first_sem, number):
        s = number // per_seq
        part = (number // (count - 1)) % 4
        d = number % (count - 1)
        other = (z + d + 1) % count
        i = first_sem + s * (count - 1) + d
        start = pl.multiple_of((s * count + other) * tokens + part * piece, piece)
        pltpu.make_async_remote_copy(
            src.at[pl.ds(start, piece)],
            dst.at[z * seqs + s, pl.ds(pl.multiple_of(part * piece, piece), piece)],
            tok_send.at[i], tok_recv.at[i], device_id=(b, other), device_id_type=MESH,
        ).start()

    def tick(t):
        @pl.when(t < seqs * per_seq)
        def _():
            send_piece(y, lay_out, 0, t)

        @pl.when((t >= 22) & (t < 22 + seqs * per_seq))
        def _():
            send_piece(wide.at[3], grad_out, seqs * (count - 1), t - 22)

        for stage, lag in reversed(list(zip(stages, lags))):
            c = t - lag

            @pl.when((c >= 0) & (c < chunks))
            def _():
                stage(c)

    def give(c, left, right, fresh=False):
        grad = dot(left, right, TN).astype(bf16)
        first = grad[:, 0:HALF]
        second = grad[:, HALF:]

        @pl.when(c >= slots)
        def _():
            rs_copy(c - slots, 0).wait_send()

        staged[c % slots] = jnp.where(core == 0, second, first)
        acc[c] = jnp.where(core == 0, first, second)
        rs_copy(c, 0).start()

    (low_s, n1_s, pg_s, eg_s) = [wide.at[i] for i in range(2, 6)]
    ag_s = wide.at[10]

    def chunk_load(j):
        cols = pl.ds(pl.multiple_of(j * WIDTH, WIDTH), WIDTH)
        return (
            pltpu.make_async_copy(hid.at[:, cols], wide.at[6 + j % 2], hid_sem.at[0, j]),
            pltpu.make_async_copy(slope.at[:, cols], wide.at[8 + j % 2], hid_sem.at[1, j]),
        )

    pg_load, low_load, n1_load, stat_load = copies(
        [(pg, pg_s), (low, low_s), (n1, n1_s), (stat, stat_s)], in_sem
    )

    def weight_load(j):
        part = pl.ds(pl.multiple_of(j * WIDTH, WIDTH), WIDTH)
        return (
            pltpu.make_async_copy(w2.at[part], w2_s.at[part], hid_sem.at[2, j]),
            pltpu.make_async_copy(w1.at[:, part], w1_s.at[:, part], hid_sem.at[3, j]),
        )

    pg_load.start()
    for copy in chunk_load(0) + weight_load(0)[:1] + (low_load,) + weight_load(0)[1:]:
        copy.start()
    own_in = [
        pltpu.make_async_copy(
            y.at[pl.ds(pl.multiple_of(s * one + z * tokens, tokens), tokens)],
            own_s.at[s], tok_own.at[s],
        )
        for s in range(seqs)
    ]
    own_y = [
        pltpu.make_async_copy(own_s.at[s], lay_out.at[z * seqs + s], tok_own.at[2 * seqs + s])
        for s in range(seqs)
    ]
    for copy in own_in:
        copy.start()
    later = copies(
        [(q, wide.at[0]), (k, wide.at[1]), (aux, wide.at[11])], in_sem.at[pl.ds(7, 3)]
    )
    middle = copies([(v, wide.at[6]), (att, wide.at[8])], in_sem.at[pl.ds(10, 2)])
    (x_load,) = copies([(x, wide.at[7])], in_sem.at[pl.ds(12, 1)])
    attn_weights = [
        pltpu.make_async_copy(w, w2_s.at[pl.ds(i * WIDTH, WIDTH)], in_sem.at[13 + i])
        for i, w in enumerate((wo, wq, wk, wv))
    ]
    block = place_of_block()
    head_out[block] = head_ref[...]
    small_out[...] = small_ref[...]
    y_moves = []
    for s in range(seqs):
        y_moves += spread(y, lay_out, seqs, tokens, False, tok_send, tok_recv, 0, s)
    pl.semaphore_wait(barrier, len(greeted))
    ROW = 128

    def add_sum(index, values):
        small_out[index : index + 1, :] += jnp.sum(values, axis=0, keepdims=True)

    pg_load.wait()

    @pl.loop(0, 4)
    def _(j):
        chunk_load(j)[0].wait()

        @pl.loop(0, 3)
        def _(t):
            give(6 * j + t, wide[6 + j % 2, :, tile(t, 256)], pg_s[...])

            @pl.when(j < 2)
            def _():
                tick(6 * j + t)

        chunk_load(j)[1].wait()
        weight_load(j)[0].wait()

        @pl.when(j < 3)
        def _():
            for copy in chunk_load(j + 1) + weight_load(j + 1):
                copy.start()

        @pl.when(j == 0)
        def _():
            for before, after in zip(own_in, own_y):
                before.wait()
                after.start()
            fg_s[...] = pg_s[...].astype(f32)

        @pl.when(j == 1)
        def _():
            for copy in (n1_load, stat_load):
                copy.start()

        @pl.when(j == 2)
        def _():
            for copy in later:
                copy.start()

        @pl.when(j == 3)
        def _():
            for copy in middle:
                copy.start()

        @pl.loop(0, WIDTH // 256)
        def _(t):
            cols = tile(t, 256)
            ff = pl.ds(pl.multiple_of(j * WIDTH + t * 256, 256), 256)
            grad = dot(pg_s[...], w2_s[ff, :], NT) * wide[8 + j % 2, :, cols].astype(f32)
            rounded = grad.astype(bf16)
            eg_s[:, cols] = rounded
            small_out[pl.ds(IB + j, 1), cols] = jnp.sum(
                rounded.astype(f32), axis=0, keepdims=True
            )

        for i in range(4):

            @pl.when(j == i)
            def _():
                attn_weights[i].start()

        @pl.when(j == 0)
        def _():
            low_load.wait()

        @pl.loop(0, 3)
        def _(t):
            give(6 * j + 3 + t, low_s[:, tile(t, 256)], eg_s[...])

            @pl.when(j < 2)
            def _():
                tick(6 * j + 3 + t)

        @pl.when(j >= 2)
        def _():
            tick(8 + 2 * j)

        weight_load(j)[1].wait()
        ff_cols = pl.ds(pl.multiple_of(j * WIDTH, WIDTH), WIDTH)

        @pl.loop(0, WIDTH // 256)
        def _(t):
            cols = tile(t, 256)
            fg_s[:, cols] += dot(eg_s[...], w1_s[cols, ff_cols], NT)

        @pl.when(j >= 2)
        def _():
            tick(9 + 2 * j)

    x_load.start()
    n1_load.wait()
    stat_load.wait()

    @pl.loop(0, rows // ROW)
    def _(i):
        r = tile(i, ROW)
        upstream = fg_s[r, :]
        normed = n1_s[r, :].astype(f32)
        add_sum(G1, upstream * normed)
        add_sum(B1, upstream)
        zg = norm_rows_back(upstream, normed, stat_s[r, 12:13], vec_ref[G1 : G1 + 1, :])
        rounded = zg.astype(bf16)
        ag_s[r, :] = rounded
        add_sum(OB, rounded.astype(f32))

    tick(16)

    (q_s, k_s, dv_s, sg_s, dq_s, dk_s, v_s, x_s, att_s, dat_s) = [wide.at[i] for i in range(10)]
    wo_s, wq_s, wk_s, wv_s = [w2_s.at[pl.ds(i * WIDTH, WIDTH)] for i in range(4)]
    attn_weights[0].wait()

    @pl.loop(0, WIDTH // 256)
    def _(t):
        cols = tile(t, 256)
        dat_s[:, cols] = dot(ag_s[...], wo_s[cols, :], NT).astype(bf16)

    for copy in middle + later:
        copy.wait()

    @pl.loop(0, 3)
    def _(t):
        give(24 + t, att_s[:, tile(t, 256)], ag_s[...])

    tick(17)
    aux_s = wide.at[11]
    for copy in attn_weights[1:]:
        copy.wait()
    x_load.wait()
    lane = lax.broadcasted_iota(jnp.int32, (1, 128), 1)

    def move(s, ordered):
        return spread(
            sg_s, grad_out, seqs, tokens, False, tok_send, tok_recv, seqs * (count - 1), s, ordered
        )

    own_sg = [
        own_part(sg_s, grad_out, seqs, tokens, False, tok_own.at[seqs + s], s) for s in range(seqs)
    ]

    @pl.loop(0, seqs)
    def _(s):
        part = pl.ds(pl.multiple_of(s * one, one), one)
        hidden = lax.broadcasted_iota(jnp.int32, (one, 1), 0) >= len_ref[z * seqs + s]
        ones = jnp.where((lane % 64) < 3, 1.0, jnp.zeros((one, 128), f32))
        key_aux = jnp.where((lane % 64 == 3) & hidden, masked_fill, ones).astype(bf16)
        value_aux = ones.astype(bf16)

        @pl.loop(0, 2)
        def _(i):
            for turn in range(3):
                cols = tile(3 * i + turn, 128)
                dq, dk, dv = attend_back_pair(
                    q_s[part, cols], k_s[part, cols], v_s[part, cols], dat_s[part, cols],
                    att_s[part, cols], aux_s[part, cols], key_aux, value_aux,
                )
                dq_s[part, cols] = dq.astype(bf16)
                dk_s[part, cols] = dk.astype(bf16)
                dv_s[part, cols] = dv.astype(bf16)
            tick(18 + 5 * s + 2 * i)
            tick(19 + 5 * s + 2 * i)

        @pl.loop(0, WIDTH // 256)
        def _(t):
            cols = tile(t, 256)
            total = ag_s[part, cols].astype(f32)
            for d, w in ((dq_s, wq_s), (dk_s, wk_s), (dv_s, wv_s)):
                total = total + dot(d[part, :], w[cols, :], NT)
            sg_s[part, cols] = total.astype(bf16)
            for index, d in ((QB, dq_s), (VB, dv_s)):
                small_out[index : index + 1, cols] += jnp.sum(
                    d[part, cols].astype(f32), axis=0, keepdims=True
                )

        for i in range(seqs):

            @pl.when(s == i)
            def _():
                own_sg[i].start()

        tick(22 + 5 * s)

    moves = []
    for s in range(seqs):
        moves += move(s, False)
    done = 18 + 5 * seqs
    for i, d in enumerate((dq_s, dk_s, dv_s)):

        @pl.loop(0, 3)
        def _(t):
            give(27 + 3 * i + t, x_s[:, tile(t, 256)], d[...])
            tick(done + 3 * i + t)

    done += 9


    def small_copies(i):
        first = block - block % (1 << i)
        part = pl.ds(first, 1 << i)
        return (
            pltpu.make_async_remote_copy(
                small_out, sgot.at[i], sm_send.at[i], sm_recv.at[i],
                device_id=partners[i], device_id_type=MESH,
            ),
            pltpu.make_async_remote_copy(
                head_out.at[part], head_out.at[part], hd_send.at[i], hd_recv.at[i],
                device_id=partners[i], device_id_type=MESH,
            ),
        )


    def late_tick(t, carry):
        for i in range(len(partners) + 1):

            @pl.when(t == done + 3 * i)
            def _():
                if i > 0:
                    for copy in small_copies(i - 1):
                        copy.wait()
                    small_out[...] = small_out[...] + sgot[i - 1]
                if i < len(partners):
                    for copy in small_copies(i):
                        copy.start()

        tick(t)
        return carry

    lax.fori_loop(done, chunks + lags[-1], late_tick, 0)
    for c in range(chunks - slots, chunks):
        rs_copy(c, 0).wait_send()
    for copy in own_sg + own_y + y_moves + moves:
        copy.wait()


def back(seqs, tokens, lengths, vecs, small, head, saved, weights):
    rows, width = saved[0].shape
    ff = 4 * width
    one = rows // seqs
    count = lax.axis_size("seq")
    chunks = 12 * width // CHUNK
    moves = 2 * seqs * (count - 1)
    dma = pltpu.SemaphoreType.DMA
    anywhere = pl.BlockSpec(memory_space=pl.ANY)
    in_vmem = pl.BlockSpec(memory_space=pltpu.VMEM)
    in_smem = pl.BlockSpec(memory_space=pltpu.SMEM)
    block = jax.ShapeDtypeStruct((seqs * count, tokens, width), bf16)
    half = functools.partial(pltpu.VMEM, dtype=bf16)
    total, small, head, lay, grad = pl.pallas_call(
        functools.partial(back_kernel, seqs, chunks, "xy", tuple(1 + 3 * i for i in range(10))),
        out_shape=(
            jax.ShapeDtypeStruct((12 * width, width), bf16),
            jax.ShapeDtypeStruct(small.shape, f32),
            jax.ShapeDtypeStruct((32,) + head.shape, bf16),
            block,
            block,
        ),
        in_specs=[in_smem, in_vmem, in_vmem, in_vmem] + [anywhere] * (len(saved) + len(weights)),
        out_specs=(anywhere, in_vmem, in_vmem, anywhere, anywhere),
        scratch_shapes=[
            pltpu.VMEM((12, rows, width), bf16), pltpu.VMEM((rows, width), f32),
            pltpu.VMEM((rows, 128), f32), pltpu.VMEM((width, ff), bf16),
            pltpu.VMEM((ff, width), bf16),
            pltpu.VMEM((chunks, CHUNK, HALF), bf16),
            pltpu.VMEM((6, CHUNK, HALF), bf16),
            pltpu.VMEM((chunks, CHUNK, HALF), bf16),
            pltpu.VMEM((chunks, CHUNK // 2, HALF), bf16),
            pltpu.VMEM((chunks, CHUNK // 4, HALF), bf16),
            pltpu.VMEM((chunks, CHUNK // 8, HALF), bf16),
            pltpu.VMEM((chunks, CHUNK // 16, HALF), bf16),
            pltpu.VMEM((5,) + small.shape, f32), pltpu.VMEM((seqs, tokens, width), bf16),
            dma((17,)), dma((4, 4)),
            dma((5, chunks)), dma((5, chunks)), dma((5, chunks)), dma((5, chunks)),
            dma((chunks,)), dma((5,)), dma((5,)), dma((5,)), dma((5,)),
            dma((moves,)), dma((moves,)), dma((3 * seqs,)),
        ],
        compiler_params=pltpu.CompilerParams(
            collective_id=0, has_side_effects=True, vmem_limit_bytes=62 * 2**20
        ),
        cost_estimate=pl.CostEstimate(
            flops=8 * rows * width * ff + 16 * rows * width * width + 10 * rows * one * width,
            bytes_accessed=100 * 2**20, transcendentals=12 * rows * one,
        ),
        name="back",
    )(lengths, vecs, small, head, *saved, *weights)
    blocks = lax.axis_size("batch") // 8
    if blocks > 1:
        alike = [[i + 8 * j for j in range(blocks)] for i in range(8)]
        total = lax.psum(total, "batch", axis_index_groups=alike)
        small = lax.psum(small, "batch", axis_index_groups=alike)
        head = lax.all_gather(head, "batch", axis_index_groups=alike, axis=0, tiled=True)
    return total.reshape(12, width, width), small, head, lay, grad


def finish_kernel(
    total, small_ref, cls_ref, label_ref, vec_ref, pool_ref, lay_in, grad_in,
    lay_out, loss_out, grad_out, gq, gk, gv, go, gqb, gvb, gob, gg1, gb1, gin, gib, gou, gub,
    gg2, gb2, gpool, gpb, gcp, gcb,
    low_s, full_s, pool_s, pass_s, in_sem, out_sem,
):
    units = low_s.shape[0]
    group = loss_out.shape[0]
    seqs = cls_ref.shape[0]
    loads = [pltpu.make_async_copy(total.at[u], low_s.at[u], in_sem.at[u]) for u in range(units)]
    for copy in loads:
        copy.start()
    places = []
    for j in range(4):
        part = pl.ds(j * WIDTH, WIDTH)
        places += [gou.at[part], gin.at[:, part]]
    places += [go, gq, gk, gv]
    stores = [
        pltpu.make_async_copy(full_s.at[u], places[u], out_sem.at[u]) for u in range(units)
    ]
    passed_in = [
        pltpu.make_async_copy(src, pass_s.at[i], in_sem.at[units + i])
        for i, src in enumerate((lay_in, grad_in))
    ]
    passed = [
        pltpu.make_async_copy(pass_s.at[i], dst, out_sem.at[units + i])
        for i, dst in enumerate((lay_out, grad_out))
    ]
    for copy in passed_in:
        copy.start()
    pool_store = pltpu.make_async_copy(pool_s, gpool, out_sem.at[units + 2])

    def widen(u):
        loads[u].wait()

        @pl.loop(0, WIDTH // 128)
        def _(i):
            r = tile(i, 128)
            full_s[u, r, :] = low_s[u, r, :].astype(f32)

        stores[u].start()

    for u in range(4):
        widen(u)
    for before, after in zip(passed_in, passed):
        before.wait()
        after.start()

    def exact(left, right, dims=NN):
        return lax.dot_general(left, right, dims, precision=highest, preferred_element_type=f32)

    pooled = jnp.tanh(dot(cls_ref[...], pool_ref[...]) + vec_ref[PB : PB + 1, :])
    row = lax.broadcasted_iota(jnp.int32, (8, 1), 0)
    class_rows = jnp.where(row < 3, vec_ref[CP : CP + 8, :], 0.0)
    picked = jnp.where(
        row == lax.broadcasted_iota(jnp.int32, (8, 128), 1), vec_ref[CB : CB + 1, 0:128], 0.0
    )
    logits = exact(class_rows, pooled, NT) + jnp.sum(picked, axis=-1, keepdims=True)
    logits = jnp.where(row < 3, logits, masked_fill)
    top = jnp.max(logits, axis=0, keepdims=True)
    raised = jnp.exp(logits - top)
    total_row = jnp.sum(raised, axis=0, keepdims=True)
    chosen = (row == label_ref[...]).astype(f32)
    losses = (top + jnp.log(total_row)) - jnp.sum(
        jnp.where(chosen > 0.0, logits, 0.0), axis=0, keepdims=True
    )
    logit_grad = raised / total_row - chosen
    first = lax.axis_index("batch") * group
    pickers = (
        lax.broadcasted_iota(jnp.int32, (seqs, 128), 0)
        == lax.broadcasted_iota(jnp.int32, (seqs, 128), 1) + first
    ).astype(f32)
    loss_out[...] = exact(losses, pickers)[0, 0:group]
    pre = exact(logit_grad, class_rows, TN) * (1.0 - pooled * pooled)
    ones = jnp.ones((1, seqs), f32)
    gcb[...] = exact(ones, logit_grad, NT)[0, 0:3]
    gpb[...] = jnp.sum(pre, axis=0)
    gcp[...] = exact(logit_grad, pooled)[0:3, :]
    high = pre.astype(bf16)
    rest = pre - high.astype(f32)
    mid = rest.astype(bf16)
    low = (rest - mid.astype(f32)).astype(bf16)
    for j in range(3):
        cols = pl.ds(j * 256, 256)
        cls = cls_ref[:, cols]
        pool_s[cols, :] = dot(cls, high, TN) + dot(cls, mid, TN) + dot(cls, low, TN)
    pool_store.start()
    for i, ref in (
        (QB, gqb), (VB, gvb), (OB, gob), (G1, gg1), (B1, gb1), (UB, gub), (G2, gg2), (B2, gb2),
    ):
        ref[...] = small_ref[i, :]
    for j in range(4):
        gib[j * WIDTH : (j + 1) * WIDTH] = small_ref[IB + j, :]
    for u in range(4, units):
        widen(u)
    for copy in stores + passed + [pool_store]:
        copy.wait()


def finish(total, small, cls, labels, vecs, pool, lay, grad):
    group, tokens, width = lay.shape
    anywhere = pl.BlockSpec(memory_space=pl.ANY)
    in_vmem = pl.BlockSpec(memory_space=pltpu.VMEM)
    square = ((width, width), f32, anywhere)
    row = ((width,), f32, in_vmem)
    outs = (
        [(lay.shape, bf16, anywhere), ((group,), f32, in_vmem), (grad.shape, bf16, anywhere)]
        + [square] * 4
        + [row] * 5
        + [((width, 4 * width), f32, anywhere), ((4 * width,), f32, in_vmem)]
        + [((4 * width, width), f32, anywhere), row, row, row]
        + [square, row, ((3, width), f32, in_vmem), ((3,), f32, in_vmem)]
    )
    units = total.shape[0]
    return pl.pallas_call(
        finish_kernel,
        out_shape=tuple(jax.ShapeDtypeStruct(s, t) for s, t, _ in outs),
        in_specs=[anywhere] + [in_vmem] * 5 + [anywhere, anywhere],
        out_specs=tuple(m for _, _, m in outs),
        scratch_shapes=[
            pltpu.VMEM((units, width, width), bf16), pltpu.VMEM((units, width, width), f32),
            pltpu.VMEM((width, width), f32), pltpu.VMEM((2,) + lay.shape, bf16),
            pltpu.SemaphoreType.DMA((units + 2,)), pltpu.SemaphoreType.DMA((units + 3,)),
        ],
        compiler_params=pltpu.CompilerParams(vmem_limit_bytes=60 * 2**20),
        name="finish",
    )(total, small, cls, labels, vecs, pool, lay, grad)


def local(
    states, lengths, labels, cotangent,
    query_proj, key_proj, value_proj, output_proj,
    query_bias, value_bias, output_bias, first_gain, first_bias,
    inner_proj, inner_bias, outer_proj, outer_bias, second_gain, second_bias,
    pool_proj, pool_bias, class_proj, class_bias,
):
    group, tokens, width = states.shape
    seqs = group // lax.axis_size("seq")
    vecs, small, head, x, q, k, v, att, n1, low, hid, slope, stat, y, aux, pg = forward(
        lengths, labels, states, cotangent,
        (query_proj, key_proj, value_proj, output_proj, inner_proj, outer_proj, pool_proj),
        (query_bias, value_bias, output_bias, first_gain, first_bias, inner_bias, outer_bias,
         second_gain, second_bias, pool_bias, class_proj.T, class_bias),
    )
    total, small, head, lay, grad = back(
        seqs, tokens, lengths, vecs, small, head,
        (pg, hid, slope, low, n1, stat, y, q, k, v, att, x, aux),
        (inner_proj, outer_proj, query_proj, key_proj, value_proj, output_proj),
    )
    cls = head[:, 0 : 6 * seqs].reshape(-1, width)
    label_row = head[:, 6 * seqs, 0:seqs].reshape(1, -1).astype(jnp.int32)
    out = finish(total, small, cls, label_row, vecs, pool_proj, lay, grad)
    return out[:20] + (out[20].T,) + out[21:]


def solution(mesh):
    split = P("batch", "seq", None)
    in_specs = (split, P("batch"), P("batch"), split) + (P(),) * 19
    out_specs = (split, P("batch"), split) + (P(),) * 19
    return jax.shard_map(local, mesh=mesh, in_specs=in_specs, out_specs=out_specs, check_vma=False)
```

```python
import functools

import jax
import jax.numpy as jnp
from jax import lax
from jax.experimental import pallas as pl
from jax.experimental.pallas import tpu as pltpu
from jax.sharding import PartitionSpec as P

HEADS = 12
HEAD_DIM = 64
WIDTH = 768
HALF = 384
CHUNK = 256
MESH = pl.DeviceIdType.MESH

bf16 = jnp.bfloat16
f32 = jnp.float32
highest = lax.Precision.HIGHEST
norm_eps = 1e-06
masked_fill = -1e30
inv_root_two = 0.7071067811865476
inv_root_tau = 0.3989422804014327


def pick(code, table):
    out = table[-1]
    for i in range(len(table) - 2, -1, -1):
        out = jnp.where(code == i, table[i], out)
    return out


def flipped(index, bit):
    return index + bit * (1 - 2 * ((index // bit) % 2))


NT = (((1,), (1,)), ((), ()))
NN = (((1,), (0,)), ((), ()))
TN = (((0,), (0,)), ((), ()))
VECS = 24
QB, VB, OB, G1, B1, IB, UB, G2, B2, PB, CP, CB = 0, 1, 2, 3, 4, 5, 9, 10, 11, 12, 13, 16


def dot(left, right, dims=NN):
    return lax.dot_general(left, right, dims, preferred_element_type=f32)


def gelu_parts(u):
    t = 1.0 / (1.0 + (0.3275911 * inv_root_two) * jnp.abs(u))
    bell = jnp.exp(-0.5 * u * u)
    poly = 1.061405429
    for coefficient in (-1.453152027, 1.421413741, -0.284496736, 0.254829592):
        poly = poly * t + coefficient
    tail = (0.5 * t) * poly * bell
    cumulative = jnp.where(u >= 0.0, 1.0 - tail, tail)
    return u * cumulative, cumulative + u * (bell * inv_root_tau)


def norm_rows(z):
    average = jnp.mean(z, axis=-1, keepdims=True)
    centered = z - average
    inv_root = lax.rsqrt(jnp.mean(centered * centered, axis=-1, keepdims=True) + norm_eps)
    return centered * inv_root, inv_root


def norm_rows_back(upstream, normed, inv_root, gain):
    scaled = upstream * gain
    return inv_root * (
        scaled
        - jnp.mean(scaled, axis=-1, keepdims=True)
        - normed * jnp.mean(scaled * normed, axis=-1, keepdims=True)
    )


def tile(i, size):
    return pl.ds(pl.multiple_of(i * size, size), size)


def copies(pairs, sems):
    out = []
    for i, (src, dst) in enumerate(pairs):
        out.append(pltpu.make_async_copy(src, dst, sems.at[i]))
    return out


def head_lanes(which):
    lane = lax.broadcasted_iota(jnp.int32, (1, 128), 1)
    return (lane >= 64) if which else (lane < 64)


def only(mask, block):
    return jnp.where(mask, block, jnp.zeros_like(block))


def attend_pair(q2, k2, v2, length, keys):
    k2 = k2[:keys]
    v2 = v2[:keys]
    place = lax.broadcasted_iota(jnp.int32, (1, keys), 1)
    out = None
    logs = []
    for which in (0, 1):
        lanes = head_lanes(which)
        scores = dot(only(lanes, q2) * bf16(0.125), k2, NT)
        scores = jnp.where(place < length, scores, masked_fill)
        top = jnp.max(scores, axis=-1, keepdims=True)
        weights = jnp.exp(scores - top)
        total = jnp.sum(weights, axis=-1, keepdims=True)
        part = dot(weights.astype(bf16), only(lanes, v2)) * (1.0 / total)
        out = part if out is None else out + part
        logs.append(top + jnp.log(total))
    return out, logs


def three_terms(values):
    high = values.astype(bf16).astype(f32)
    mid = (values - high).astype(bf16).astype(f32)
    return high, mid, values - high - mid


def attend_back_pair(q2, k2, v2, d2, a2, q_aux, key_aux, value_aux):
    lane = lax.broadcasted_iota(jnp.int32, (1, 128), 1)
    product = d2.astype(f32) * a2.astype(f32)
    d_aux = jnp.zeros_like(product)
    for which in (0, 1):
        delta = jnp.sum(only(head_lanes(which), product), axis=-1, keepdims=True)
        for i, piece in enumerate(three_terms(-delta)):
            d_aux = jnp.where(lane == 64 * (1 - which) + i, piece, d_aux)
    d_aux = d_aux.astype(bf16)
    q2 = q2 * bf16(0.125)
    heads = []
    for which in (0, 1):
        lanes = head_lanes(which)
        heads.append(
            [
                jnp.where(lanes, block, other)
                for block, other in ((q2, q_aux), (k2, key_aux), (v2, value_aux), (d2, d_aux))
            ]
        )
    scores = [dot(kh, qh, NT) for qh, kh, _, _ in heads]
    prob_grads = [dot(vh, dh, NT) for _, _, vh, dh in heads]
    probs = [jnp.exp(s) for s in scores]
    score_grads = [(p * g).astype(bf16) for p, g in zip(probs, prob_grads)]
    out = [
        (dot(g, kh, TN), dot(g, qh), dot(p.astype(bf16), dh))
        for g, p, (qh, kh, _, dh) in zip(score_grads, probs, heads)
    ]
    first = head_lanes(0)
    dq, dk, dv = [jnp.where(first, one, two) for one, two in zip(*out)]
    return dq * 0.125, dk, dv


def exit_back(cls_rows, labels, vec_ref, pool_s):
    pooled = jnp.tanh(dot(cls_rows, pool_s[...]) + vec_ref[PB : PB + 1, :])
    class_rows = vec_ref[CP : CP + 3, :]
    logits = [
        jnp.sum(pooled * class_rows[i : i + 1, :], axis=-1, keepdims=True)
        + vec_ref[CB : CB + 1, i : i + 1]
        for i in range(3)
    ]
    top = jnp.maximum(jnp.maximum(logits[0], logits[1]), logits[2])
    raised = [jnp.exp(l - top) for l in logits]
    total = raised[0] + raised[1] + raised[2]
    back = jnp.zeros_like(pooled)
    for i in range(3):
        back = back + (raised[i] / total - (labels == i).astype(f32)) * class_rows[i : i + 1, :]
    pre = back * (1.0 - pooled * pooled)
    high = pre.astype(bf16)
    rest = pre - high.astype(f32)
    mid = rest.astype(bf16)
    low = (rest - mid.astype(f32)).astype(bf16)
    return dot(high, pool_s[...], NT) + dot(mid, pool_s[...], NT) + dot(low, pool_s[...], NT)


def spread(src, dst, seqs, tokens, to_rows, sends, recvs, base, s, ordered=False):
    count = lax.axis_size("seq")
    b = lax.axis_index("batch")
    z = lax.axis_index("seq")
    out = []
    for d in range(1, count):
        if ordered and count == 4:
            d = jnp.where(z % 2 == 0, d % 3 + 1, d)
        other = lax.rem(z + d, count)
        if to_rows:
            source = src.at[other * seqs + s]
            target = dst.at[pl.ds(pl.multiple_of((s * count + z) * tokens, tokens), tokens)]
        else:
            source = src.at[pl.ds(pl.multiple_of((s * count + other) * tokens, tokens), tokens)]
            target = dst.at[z * seqs + s]
        i = base + s * (count - 1) + d - 1
        out.append(
            pltpu.make_async_remote_copy(
                source, target, sends.at[i], recvs.at[i],
                device_id=(b, other), device_id_type=MESH,
            )
        )
    return out


def own_part(src, dst, seqs, tokens, to_rows, sem, s):
    count = lax.axis_size("seq")
    z = lax.axis_index("seq")
    block = z * seqs + s
    rows = pl.ds(pl.multiple_of((s * count + z) * tokens, tokens), tokens)
    if to_rows:
        return pltpu.make_async_copy(src.at[block], dst.at[rows], sem)
    return pltpu.make_async_copy(src.at[rows], dst.at[block], sem)


def greet_line():
    count = lax.axis_size("seq")
    z = lax.axis_index("seq")
    return [(lax.axis_index("batch"), lax.rem(z + d, count)) for d in range(1, count)]


def forward_kernel(
    seqs, len_ref, label_ref, states, cot, wq, wk, wv, wo, w1, w2, pool,
    query_bias, value_bias, output_bias, first_gain, first_bias, inner_bias, outer_bias,
    second_gain, second_bias, pool_bias, class_proj, class_bias,
    vec_ref, small_out, head_out, x_out, q_out, k_out, v_out, att_out, n1_out, low_out, hid_out,
    slope_out, stat_out, y_out, aux_out, pg_out,
    x_s, wq_s, wk_s, wv_s, wo_s, w1_s, w2_s,
    q_s, k_s, v_s, att_s, n1_s, low_s, hid_s, slope_s, stat_s, y_s, aux_s, n2_s, z_s,
    cot_s, pool_s, row_s, in_sem, out_sem, own_sem, sends, recvs,
):
    rows = z_s.shape[0]
    tokens = states.shape[1]
    line = greet_line()
    barrier = pltpu.get_barrier_semaphore()
    for who in line:
        pl.semaphore_signal(barrier, inc=1, device_id=who, device_id_type=MESH)
    weights_in = copies(
        [(wq, wq_s), (wk, wk_s), (wv, wv_s), (wo, wo_s), (w1, w1_s), (w2, w2_s), (pool, pool_s)],
        in_sem,
    )
    z = lax.axis_index("seq")
    own = [own_part(states, x_s, seqs, tokens, True, own_sem.at[s], s) for s in range(seqs)]
    own_cot = [
        own_part(cot, cot_s, seqs, tokens, True, own_sem.at[seqs + s], s) for s in range(seqs)
    ]
    for copy in own + weights_in + own_cot:
        copy.start()
    pl.semaphore_wait(barrier, len(line))

    def move(first, s, ordered):
        src, dst, start = (states, x_s, 0) if first else (cot, cot_s, seqs * len(line))
        return spread(src, dst, seqs, tokens, True, sends, recvs, start, s, ordered)

    moves = [move(True, s, False) for s in range(seqs)]
    late = [move(False, s, False) for s in range(seqs)]
    for copy in move(True, 0, False):
        copy.start()
    vec_ref[...] = jnp.zeros_like(vec_ref)
    for i, ref in (
        (QB, query_bias), (VB, value_bias), (OB, output_bias), (G1, first_gain), (B1, first_bias),
        (UB, outer_bias), (G2, second_gain), (B2, second_bias), (PB, pool_bias),
    ):
        vec_ref[i : i + 1, :] = ref[...].astype(f32).reshape(1, WIDTH)
    for i in range(4):
        vec_ref[IB + i : IB + i + 1, :] = (
            inner_bias[i * WIDTH : (i + 1) * WIDTH].astype(f32).reshape(1, WIDTH)
        )
    vec_ref[CP : CP + 3, :] = class_proj[...].astype(f32)
    vec_ref[CB : CB + 1, 0:3] = class_bias[...].astype(f32).reshape(1, 3)

    waiting = []
    def send_late(s):
        for copy in move(False, s, False):
            copy.start()

    for s in range(seqs):
        for copy in moves[s]:
            copy.wait_recv()
        own[s].wait()
        if s == 0:
            for i in range(1, seqs):
                for copy in move(True, i, False):
                    copy.start()
        part = pl.ds(s * rows, rows)
        waiting += forward_rows(
            s, part, len_ref[z * seqs + s], rows, s == 0, vec_ref, weights_in,
            (lambda: send_late(0)) if s == 0 else None,
            (x_s, wq_s, wk_s, wv_s, wo_s, w1_s, w2_s, q_s, k_s, v_s, att_s, n1_s, low_s, hid_s,
             slope_s, stat_s, y_s, aux_s, n2_s, z_s),
            (x_out, q_out, k_out, v_out, att_out, n1_out, low_out, hid_out, slope_out,
             stat_out, y_out, aux_out),
            out_sem,
        )
        if s == 0:
            for i in range(1, seqs):
                send_late(i)

    place = lax.broadcasted_iota(jnp.int32, (16 * seqs, 1), 0)
    labels = jnp.zeros((16 * seqs, 1), jnp.int32)
    label_row = jnp.zeros((1, 128), f32)
    lane = lax.broadcasted_iota(jnp.int32, (1, 128), 1)
    for s in range(seqs):
        label = label_ref[z * seqs + s]
        labels = jnp.where(place == 16 * s, label, labels)
        label_row = jnp.where(lane == s, label.astype(f32), label_row)
    cls_rows = jnp.concatenate([y_s[s * rows : s * rows + 16, :] for s in range(seqs)])
    weights_in[6].wait()
    cls_grad = exit_back(cls_rows, labels, vec_ref, pool_s)
    row_s[...] = jnp.zeros_like(row_s)
    for s in range(seqs):
        first = y_s[s * rows : s * rows + 16, :].astype(f32)
        for j in range(6):
            row_s[s * 6 + j : s * 6 + j + 1, :] = first[0:1, j * 128 : (j + 1) * 128]
    row_s[6 * seqs : 6 * seqs + 1, :] = label_row
    head_out[...] = row_s[...].astype(bf16)
    small_out[...] = jnp.zeros_like(small_out)

    def add_sum(index, values):
        small_out[index : index + 1, :] += jnp.sum(values, axis=0, keepdims=True)

    for s in range(seqs):
        for copy in late[s]:
            copy.wait_recv()
        own_cot[s].wait()

        @pl.loop(0, rows // 128)
        def _(i):
            r = pl.ds(pl.multiple_of(s * rows + i * 128, 128), 128)
            place = lax.broadcasted_iota(jnp.int32, (128, 1), 0) + i * 128
            upstream = cot_s[r, :].astype(f32) + jnp.where(
                place == 0, cls_grad[16 * s : 16 * s + 1, :], 0.0
            )
            normed = n2_s[r, :].astype(f32)
            add_sum(G2, upstream * normed)
            add_sum(B2, upstream)
            grad = norm_rows_back(upstream, normed, stat_s[r, 13:14], vec_ref[G2 : G2 + 1, :])
            rounded = grad.astype(bf16)
            n2_s[r, :] = rounded
            add_sum(UB, rounded.astype(f32))

        part = pl.ds(s * rows, rows)
        waiting.append(pltpu.make_async_copy(n2_s.at[part], pg_out.at[part], out_sem.at[s, 12]))
        waiting[-1].start()
    for group in moves + late:
        for copy in group:
            copy.wait_send()
    for copy in waiting:
        copy.wait()


def forward_rows(
    s, part, length, rows, first_time, vec_ref, weights_in, halfway, scratch, outs, out_sem
):
    (x_s, wq_s, wk_s, wv_s, wo_s, w1_s, w2_s, q_s, k_s, v_s, att_s, n1_s, low_s, hid_s,
     slope_s, stat_s, y_s, aux_s, n2_s, z_s) = scratch
    start = s * rows
    out = [
        pltpu.make_async_copy(src.at[part], dst.at[part], out_sem.at[s, i])
        for i, (src, dst) in enumerate(
            zip(
                (x_s, q_s, k_s, v_s, att_s, n1_s, low_s, hid_s, slope_s, stat_s, y_s, aux_s), outs
            )
        )
    ]
    out[0].start()
    for i, (w, dst, bias) in enumerate(((wq_s, q_s, QB), (wk_s, k_s, None), (wv_s, v_s, VB))):
        if first_time:
            weights_in[i].wait()

        @pl.loop(0, WIDTH // 256)
        def _(j):
            cols = tile(j, 256)
            grid = dot(x_s[part, :], w[:, cols])
            if bias is not None:
                grid = grid + vec_ref[bias : bias + 1, cols]
            dst[part, cols] = grid.astype(bf16)

        out[1 + i].start()

    stat_s[part, :] = jnp.zeros((rows, 128), f32)
    lane = lax.broadcasted_iota(jnp.int32, (1, 128), 1)

    @pl.loop(0, HEADS // 2)
    def _(p):
        cols = tile(p, 128)
        mix, logs = attend_pair(q_s[part, cols], k_s[part, cols], v_s[part, cols], length, rows)
        att_s[part, cols] = mix.astype(bf16)
        aux = jnp.where((lane == 3) | (lane == 67), 1.0, jnp.zeros((rows, 128), f32))
        for which in (0, 1):
            for i, piece in enumerate(three_terms(-logs[which])):
                aux = jnp.where(lane == 64 * (1 - which) + i, piece, aux)
        aux_s[part, cols] = aux.astype(bf16)

    out[4].start()
    out[11].start()
    if halfway is not None:
        halfway()
    if first_time:
        weights_in[3].wait()

    @pl.loop(0, WIDTH // 256)
    def _(j):
        cols = tile(j, 256)
        z_s[:, cols] = (
            x_s[part, cols].astype(f32)
            + dot(att_s[part, :], wo_s[:, cols])
            + vec_ref[OB : OB + 1, cols]
        )

    @pl.loop(0, rows // 128)
    def _(i):
        r = tile(i, 128)
        q = pl.ds(pl.multiple_of(start + i * 128, 128), 128)
        normed, inv_root = norm_rows(z_s[r, :])
        n1_s[q, :] = normed.astype(bf16)
        first = normed * vec_ref[G1 : G1 + 1, :] + vec_ref[B1 : B1 + 1, :]
        low_s[q, :] = first.astype(bf16)
        z_s[r, :] = first + vec_ref[UB : UB + 1, :]
        stat_s[q, :] = jnp.where(lane == 12, inv_root, stat_s[q, :])

    out[5].start()
    out[6].start()
    if first_time:
        weights_in[4].wait()
        weights_in[5].wait()
    ft = 256

    @pl.loop(0, 4 * WIDTH // ft)
    def _(j):
        cols = tile(j, ft)
        u = dot(low_s[part, :], w1_s[:, cols]) + vec_ref[pl.ds(IB + j // 3, 1), tile(j % 3, ft)]
        h, slope = gelu_parts(u)
        hid_s[part, cols] = h.astype(bf16)
        slope_s[part, cols] = slope.astype(bf16)

    out[7].start()
    out[8].start()

    @pl.loop(0, WIDTH // 256)
    def _(j):
        cols = tile(j, 256)
        z_s[:, cols] += dot(hid_s[part, :], w2_s[:, cols])

    @pl.loop(0, rows // 128)
    def _(i):
        r = tile(i, 128)
        q = pl.ds(pl.multiple_of(start + i * 128, 128), 128)
        normed, inv_root = norm_rows(z_s[r, :])
        n2_s[q, :] = normed.astype(bf16)
        y_s[q, :] = (normed * vec_ref[G2 : G2 + 1, :] + vec_ref[B2 : B2 + 1, :]).astype(bf16)
        stat_s[q, :] = jnp.where(lane == 13, inv_root, stat_s[q, :])

    for i in (9, 10):
        out[i].start()
    return out


def forward(lengths, labels, states, cotangent, weights, small):
    count = lax.axis_size("seq")
    group, tokens, width = states.shape
    seqs = group // count
    one = count * tokens
    rows = seqs * one
    ff = 4 * width
    anywhere = pl.BlockSpec(memory_space=pl.ANY)
    in_vmem = pl.BlockSpec(memory_space=pltpu.VMEM)
    wide = ((rows, width), bf16)
    saved = [wide] * 6 + [((rows, ff), bf16)] * 2 + [((rows, 128), f32), wide, wide, wide]
    outs = [((VECS, width), f32), ((16, width), f32), ((16, 128), bf16), wide] + saved
    moves = 2 * seqs * (count - 1)
    flops = 2 * rows * width * (4 * width + 2 * ff) + 4 * rows * one * width
    dma = pltpu.SemaphoreType.DMA
    return pl.pallas_call(
        functools.partial(forward_kernel, seqs),
        out_shape=tuple(jax.ShapeDtypeStruct(s, t) for s, t in outs),
        in_specs=[pl.BlockSpec(memory_space=pltpu.SMEM)] * 2
        + [anywhere] * 9
        + [in_vmem] * len(small),
        out_specs=(in_vmem,) * 3 + (anywhere,) * (len(outs) - 3),
        scratch_shapes=[pltpu.VMEM((rows, width), bf16)]
        + [pltpu.VMEM(w.shape, bf16) for w in weights[:6]]
        + [pltpu.VMEM(s, t) for s, t in saved]
        + [
            pltpu.VMEM((one, width), f32), pltpu.VMEM((rows, width), bf16),
            pltpu.VMEM((width, width), bf16), pltpu.VMEM((16, 128), f32),
            dma((7,)), dma((seqs, 13)), dma((2 * seqs,)),
            dma((moves,)), dma((moves,)),
        ],
        compiler_params=pltpu.CompilerParams(
            collective_id=1, has_side_effects=True, vmem_limit_bytes=60 * 2**20
        ),
        cost_estimate=pl.CostEstimate(
            flops=flops, bytes_accessed=50 * 2**20, transcendentals=rows * (ff + 12 * one)
        ),
        name="forward",
    )(lengths, labels, states, cotangent, *weights, *small)


def place_of_block():
    return (lax.axis_index("batch") % 8) * 4 + lax.axis_index("seq")


def back_kernel(
    seqs, chunks, pattern, lags, len_ref, vec_ref, small_ref, head_ref,
    pg, hid, slope, low, n1, stat, y, q, k, v, att, x, aux,
    w1, w2, wq, wk, wv, wo,
    out_ref, small_out, head_out, lay_out, grad_out,
    wide, fg_s, stat_s, w1_s, w2_s,
    acc, staged, r0, r1, r2, r3, r4, sgot, own_s,
    in_sem, hid_sem, rs_send, rs_recv, ag_send, ag_recv, loc, sm_send, sm_recv, hd_send, hd_recv,
    tok_send, tok_recv, tok_own,
):
    rows = fg_s.shape[0]
    one = rows // seqs
    tokens = lay_out.shape[1]
    count = lax.axis_size("seq")
    b = lax.axis_index("batch")
    z = lax.axis_index("seq")
    core = b % 2

    got = [r0, r1, r2, r3, r4]
    res = r0
    near_b = [flipped(b, 2), flipped(b, 4), b, b]
    near_z = [z, z, flipped(z, 1), flipped(z, 2)]
    mine = [(b // 2) % 2, (b // 4) % 2, z % 2, (z // 2) % 2]
    orders = {"x": (0, 1, 2, 3), "y": (1, 0, 2, 3)}
    period = len(pattern)

    def direction(c, level):
        code = c % period
        dirs = [orders[p][level] for p in pattern]
        return (
            pick(code, [near_b[d] for d in dirs]),
            pick(code, [near_z[d] for d in dirs]),
            pick(code, [mine[d] for d in dirs]),
        )

    core_partner = (flipped(b, 1), z)
    barrier = pltpu.get_barrier_semaphore()
    partners = [(near_b[2], near_z[2]), (near_b[3], near_z[3]), core_partner]
    partners += [(near_b[0], near_z[0]), (near_b[1], near_z[1])]
    greeted = [core_partner, (near_b[0], near_z[0]), (near_b[1], near_z[1])] + greet_line()
    for who in greeted:
        pl.semaphore_signal(barrier, inc=1, device_id=who, device_id_type=MESH)

    def base(c, level):
        first = 0
        size = CHUNK
        for l in range(level):
            size = size // 2
            first = first + direction(c, l)[2] * size
        return pl.multiple_of(first, 16)

    slots = staged.shape[0]
    my_cols = pl.ds(pl.multiple_of(core * HALF, HALF), HALF)

    def rs_copy(c, s):
        if s == 0:
            return pltpu.make_async_remote_copy(
                staged.at[c % slots], r0.at[c], rs_send.at[0, c], rs_recv.at[0, c],
                device_id=core_partner, device_id_type=MESH,
            )
        size = CHUNK >> s
        nb, nz, m = direction(c, s - 1)
        start = pl.multiple_of(base(c, s - 1) + (1 - m) * size, 16)
        return pltpu.make_async_remote_copy(
            acc.at[c, pl.ds(start, size)], got[s].at[c], rs_send.at[s, c], rs_recv.at[s, c],
            device_id=(nb, nz), device_id_type=MESH,
        )

    def out_rows(c):
        return out_ref.at[pl.ds(pl.multiple_of(c * CHUNK, CHUNK), CHUNK), my_cols]

    def ag_copy(c, s):
        if s == 0:
            return pltpu.make_async_remote_copy(
                res.at[c], out_rows(c), ag_send.at[0, c], ag_recv.at[0, c],
                device_id=core_partner, device_id_type=MESH,
            )
        size = CHUNK >> s
        nb, nz, _ = direction(c, s - 1)
        start = base(c, s)
        return pltpu.make_async_remote_copy(
            res.at[c, pl.ds(start, size)], res.at[c, pl.ds(start, size)],
            ag_send.at[s, c], ag_recv.at[s, c], device_id=(nb, nz), device_id_type=MESH,
        )

    def loc_out(c):
        return pltpu.make_async_copy(res.at[c], out_rows(c), loc.at[c])

    def stage_scatter(s, c):
        rs_copy(c, s - 1).wait_recv()
        half = CHUNK >> s
        start = base(c, s - 1)
        m = direction(c, s - 1)[2]
        for which in (0, 1):
            off = pl.multiple_of(((1 - m) if which == 0 else m) * half, 16)
            part = pl.ds(pl.multiple_of(start + off, 16), half)
            acc[c, part] = acc[c, part] + got[s - 1][c, pl.ds(off, half)]
            if which == 0:
                rs_copy(c, s).start()

    def stage_turn(c):
        rs_copy(c, 4).wait_recv()
        part = pl.ds(base(c, 4), 16)
        res[c, part] = acc[c, part] + r4[c]
        ag_copy(c, 4).start()

    def stage_gather(s, c):
        ag_copy(c, s + 1).wait_recv()
        ag_copy(c, s).start()
        if s == 0:
            loc_out(c).start()

    def stage_last(c):
        ag_copy(c, 0).wait_recv()
        loc_out(c).wait()
        for s in range(1, 5):
            rs_copy(c, s).wait_send()
        for s in range(5):
            ag_copy(c, s).wait_send()

    stages = (
        [functools.partial(stage_scatter, s) for s in (1, 2, 3, 4)]
        + [stage_turn]
        + [functools.partial(stage_gather, s) for s in (3, 2, 1, 0)]
        + [stage_last]
    )

    piece = tokens // 4
    per_seq = 4 * (count - 1)

    def send_piece(src, dst, first_sem, number):
        s = number // per_seq
        part = (number // (count - 1)) % 4
        d = number % (count - 1)
        other = (z + d + 1) % count
        i = first_sem + s * (count - 1) + d
        start = pl.multiple_of((s * count + other) * tokens + part * piece, piece)
        pltpu.make_async_remote_copy(
            src.at[pl.ds(start, piece)],
            dst.at[z * seqs + s, pl.ds(pl.multiple_of(part * piece, piece), piece)],
            tok_send.at[i], tok_recv.at[i], device_id=(b, other), device_id_type=MESH,
        ).start()

    def tick(t):
        @pl.when(t < seqs * per_seq)
        def _():
            send_piece(y, lay_out, 0, t)

        @pl.when((t >= 23) & (t < 23 + seqs * per_seq))
        def _():
            send_piece(wide.at[3], grad_out, seqs * (count - 1), t - 23)

        for stage, lag in reversed(list(zip(stages, lags))):
            c = t - lag

            @pl.when((c >= 0) & (c < chunks))
            def _():
                stage(c)

    def give(c, left, right, fresh=False):
        grad = dot(left, right, TN).astype(bf16)
        first = grad[:, 0:HALF]
        second = grad[:, HALF:]

        @pl.when(c >= slots)
        def _():
            rs_copy(c - slots, 0).wait_send()

        staged[c % slots] = jnp.where(core == 0, second, first)
        acc[c] = jnp.where(core == 0, first, second)
        rs_copy(c, 0).start()

    (low_s, n1_s, pg_s, eg_s) = [wide.at[i] for i in range(2, 6)]
    ag_s = wide.at[10]

    def chunk_load(j):
        cols = pl.ds(pl.multiple_of(j * WIDTH, WIDTH), WIDTH)
        return (
            pltpu.make_async_copy(hid.at[:, cols], wide.at[6 + j % 2], hid_sem.at[0, j]),
            pltpu.make_async_copy(slope.at[:, cols], wide.at[8 + j % 2], hid_sem.at[1, j]),
        )

    pg_load, low_load, n1_load, stat_load = copies(
        [(pg, pg_s), (low, low_s), (n1, n1_s), (stat, stat_s)], in_sem
    )

    def weight_load(j):
        part = pl.ds(pl.multiple_of(j * WIDTH, WIDTH), WIDTH)
        return (
            pltpu.make_async_copy(w2.at[part], w2_s.at[part], hid_sem.at[2, j]),
            pltpu.make_async_copy(w1.at[:, part], w1_s.at[:, part], hid_sem.at[3, j]),
        )

    pg_load.start()
    for copy in chunk_load(0) + weight_load(0)[:1] + (low_load,) + weight_load(0)[1:]:
        copy.start()
    own_in = [
        pltpu.make_async_copy(
            y.at[pl.ds(pl.multiple_of(s * one + z * tokens, tokens), tokens)],
            own_s.at[s], tok_own.at[s],
        )
        for s in range(seqs)
    ]
    own_y = [
        pltpu.make_async_copy(own_s.at[s], lay_out.at[z * seqs + s], tok_own.at[2 * seqs + s])
        for s in range(seqs)
    ]
    for copy in own_in:
        copy.start()
    later = copies(
        [(q, wide.at[0]), (k, wide.at[1]), (aux, wide.at[11])], in_sem.at[pl.ds(7, 3)]
    )
    middle = copies([(v, wide.at[6]), (att, wide.at[8])], in_sem.at[pl.ds(10, 2)])
    (x_load,) = copies([(x, wide.at[7])], in_sem.at[pl.ds(12, 1)])
    attn_weights = [
        pltpu.make_async_copy(w, w2_s.at[pl.ds(i * WIDTH, WIDTH)], in_sem.at[13 + i])
        for i, w in enumerate((wo, wq, wk, wv))
    ]
    block = place_of_block()
    head_out[block] = head_ref[...]
    small_out[...] = small_ref[...]
    y_moves = []
    for s in range(seqs):
        y_moves += spread(y, lay_out, seqs, tokens, False, tok_send, tok_recv, 0, s)
    pl.semaphore_wait(barrier, len(greeted))
    ROW = 128

    def add_sum(index, values):
        small_out[index : index + 1, :] += jnp.sum(values, axis=0, keepdims=True)

    pg_load.wait()

    @pl.loop(0, 4)
    def _(j):
        chunk_load(j)[0].wait()

        @pl.loop(0, 3)
        def _(t):
            give(6 * j + t, wide[6 + j % 2, :, tile(t, 256)], pg_s[...])

            @pl.when(j < 2)
            def _():
                tick(6 * j + t)

        chunk_load(j)[1].wait()
        weight_load(j)[0].wait()

        @pl.when(j < 3)
        def _():
            for copy in chunk_load(j + 1) + weight_load(j + 1):
                copy.start()

        @pl.when(j == 0)
        def _():
            for before, after in zip(own_in, own_y):
                before.wait()
                after.start()
            fg_s[...] = pg_s[...].astype(f32)

        @pl.when(j == 1)
        def _():
            for copy in (n1_load, stat_load):
                copy.start()

        @pl.when(j == 2)
        def _():
            for copy in later:
                copy.start()

        @pl.when(j == 3)
        def _():
            for copy in middle:
                copy.start()

        @pl.loop(0, WIDTH // 256)
        def _(t):
            cols = tile(t, 256)
            ff = pl.ds(pl.multiple_of(j * WIDTH + t * 256, 256), 256)
            grad = dot(pg_s[...], w2_s[ff, :], NT) * wide[8 + j % 2, :, cols].astype(f32)
            rounded = grad.astype(bf16)
            eg_s[:, cols] = rounded
            small_out[pl.ds(IB + j, 1), cols] = jnp.sum(
                rounded.astype(f32), axis=0, keepdims=True
            )

        for i in range(4):

            @pl.when(j == i)
            def _():
                attn_weights[i].start()

        @pl.when(j == 0)
        def _():
            low_load.wait()

        @pl.loop(0, 3)
        def _(t):
            give(6 * j + 3 + t, low_s[:, tile(t, 256)], eg_s[...])

            @pl.when(j < 2)
            def _():
                tick(6 * j + 3 + t)

        @pl.when(j >= 2)
        def _():
            tick(6 + 3 * j)

        weight_load(j)[1].wait()
        ff_cols = pl.ds(pl.multiple_of(j * WIDTH, WIDTH), WIDTH)

        @pl.loop(0, WIDTH // 256)
        def _(t):
            cols = tile(t, 256)
            fg_s[:, cols] += dot(eg_s[...], w1_s[cols, ff_cols], NT)

        @pl.when(j >= 2)
        def _():
            tick(7 + 3 * j)
            tick(8 + 3 * j)

    x_load.start()
    n1_load.wait()
    stat_load.wait()

    @pl.loop(0, rows // ROW)
    def _(i):
        r = tile(i, ROW)
        upstream = fg_s[r, :]
        normed = n1_s[r, :].astype(f32)
        add_sum(G1, upstream * normed)
        add_sum(B1, upstream)
        zg = norm_rows_back(upstream, normed, stat_s[r, 12:13], vec_ref[G1 : G1 + 1, :])
        rounded = zg.astype(bf16)
        ag_s[r, :] = rounded
        add_sum(OB, rounded.astype(f32))

    tick(18)

    (q_s, k_s, dv_s, sg_s, dq_s, dk_s, v_s, x_s, att_s, dat_s) = [wide.at[i] for i in range(10)]
    wo_s, wq_s, wk_s, wv_s = [w2_s.at[pl.ds(i * WIDTH, WIDTH)] for i in range(4)]
    attn_weights[0].wait()

    @pl.loop(0, WIDTH // 256)
    def _(t):
        cols = tile(t, 256)
        dat_s[:, cols] = dot(ag_s[...], wo_s[cols, :], NT).astype(bf16)

    for copy in middle + later:
        copy.wait()

    @pl.loop(0, 3)
    def _(t):
        give(24 + t, att_s[:, tile(t, 256)], ag_s[...])

    tick(19)
    aux_s = wide.at[11]
    for copy in attn_weights[1:]:
        copy.wait()
    x_load.wait()
    lane = lax.broadcasted_iota(jnp.int32, (1, 128), 1)

    def move(s, ordered):
        return spread(
            sg_s, grad_out, seqs, tokens, False, tok_send, tok_recv, seqs * (count - 1), s, ordered
        )

    own_sg = [
        own_part(sg_s, grad_out, seqs, tokens, False, tok_own.at[seqs + s], s) for s in range(seqs)
    ]

    @pl.loop(0, seqs)
    def _(s):
        part = pl.ds(pl.multiple_of(s * one, one), one)
        hidden = lax.broadcasted_iota(jnp.int32, (one, 1), 0) >= len_ref[z * seqs + s]
        ones = jnp.where((lane % 64) < 3, 1.0, jnp.zeros((one, 128), f32))
        key_aux = jnp.where((lane % 64 == 3) & hidden, masked_fill, ones).astype(bf16)
        value_aux = ones.astype(bf16)

        @pl.loop(0, 2)
        def _(i):
            for turn in range(3):
                cols = tile(3 * i + turn, 128)
                dq, dk, dv = attend_back_pair(
                    q_s[part, cols], k_s[part, cols], v_s[part, cols], dat_s[part, cols],
                    att_s[part, cols], aux_s[part, cols], key_aux, value_aux,
                )
                dq_s[part, cols] = dq.astype(bf16)
                dk_s[part, cols] = dk.astype(bf16)
                dv_s[part, cols] = dv.astype(bf16)
            tick(20 + 4 * s + 2 * i)

            @pl.when(i == 0)
            def _():
                tick(21 + 4 * s)

        @pl.loop(0, WIDTH // 256)
        def _(t):
            cols = tile(t, 256)
            total = ag_s[part, cols].astype(f32)
            for d, w in ((dq_s, wq_s), (dk_s, wk_s), (dv_s, wv_s)):
                total = total + dot(d[part, :], w[cols, :], NT)
            sg_s[part, cols] = total.astype(bf16)
            for index, d in ((QB, dq_s), (VB, dv_s)):
                small_out[index : index + 1, cols] += jnp.sum(
                    d[part, cols].astype(f32), axis=0, keepdims=True
                )

        for i in range(seqs):

            @pl.when(s == i)
            def _():
                own_sg[i].start()

        tick(23 + 4 * s)

    moves = []
    for s in range(seqs):
        moves += move(s, False)
    done = 18 + 5 * seqs
    for i, d in enumerate((dq_s, dk_s, dv_s)):

        @pl.loop(0, 3)
        def _(t):
            give(27 + 3 * i + t, x_s[:, tile(t, 256)], d[...])
            tick(done + 3 * i + t)

    done += 9


    def small_copies(i):
        first = block - block % (1 << i)
        part = pl.ds(first, 1 << i)
        return (
            pltpu.make_async_remote_copy(
                small_out, sgot.at[i], sm_send.at[i], sm_recv.at[i],
                device_id=partners[i], device_id_type=MESH,
            ),
            pltpu.make_async_remote_copy(
                head_out.at[part], head_out.at[part], hd_send.at[i], hd_recv.at[i],
                device_id=partners[i], device_id_type=MESH,
            ),
        )


    def late_tick(t, carry):
        for i in range(len(partners) + 1):

            @pl.when(t == done + 3 * i)
            def _():
                if i > 0:
                    for copy in small_copies(i - 1):
                        copy.wait()
                    small_out[...] = small_out[...] + sgot[i - 1]
                if i < len(partners):
                    for copy in small_copies(i):
                        copy.start()

        tick(t)
        return carry

    lax.fori_loop(done, chunks + lags[-1], late_tick, 0)
    for c in range(chunks - slots, chunks):
        rs_copy(c, 0).wait_send()
    for copy in own_sg + own_y + y_moves + moves:
        copy.wait()


def back(seqs, tokens, lengths, vecs, small, head, saved, weights):
    rows, width = saved[0].shape
    ff = 4 * width
    one = rows // seqs
    count = lax.axis_size("seq")
    chunks = 12 * width // CHUNK
    moves = 2 * seqs * (count - 1)
    dma = pltpu.SemaphoreType.DMA
    anywhere = pl.BlockSpec(memory_space=pl.ANY)
    in_vmem = pl.BlockSpec(memory_space=pltpu.VMEM)
    in_smem = pl.BlockSpec(memory_space=pltpu.SMEM)
    block = jax.ShapeDtypeStruct((seqs * count, tokens, width), bf16)
    half = functools.partial(pltpu.VMEM, dtype=bf16)
    total, small, head, lay, grad = pl.pallas_call(
        functools.partial(back_kernel, seqs, chunks, "xy", tuple(1 + 3 * i for i in range(10))),
        out_shape=(
            jax.ShapeDtypeStruct((12 * width, width), bf16),
            jax.ShapeDtypeStruct(small.shape, f32),
            jax.ShapeDtypeStruct((32,) + head.shape, bf16),
            block,
            block,
        ),
        in_specs=[in_smem, in_vmem, in_vmem, in_vmem] + [anywhere] * (len(saved) + len(weights)),
        out_specs=(anywhere, in_vmem, in_vmem, anywhere, anywhere),
        scratch_shapes=[
            pltpu.VMEM((12, rows, width), bf16), pltpu.VMEM((rows, width), f32),
            pltpu.VMEM((rows, 128), f32), pltpu.VMEM((width, ff), bf16),
            pltpu.VMEM((ff, width), bf16),
            pltpu.VMEM((chunks, CHUNK, HALF), bf16),
            pltpu.VMEM((6, CHUNK, HALF), bf16),
            pltpu.VMEM((chunks, CHUNK, HALF), bf16),
            pltpu.VMEM((chunks, CHUNK // 2, HALF), bf16),
            pltpu.VMEM((chunks, CHUNK // 4, HALF), bf16),
            pltpu.VMEM((chunks, CHUNK // 8, HALF), bf16),
            pltpu.VMEM((chunks, CHUNK // 16, HALF), bf16),
            pltpu.VMEM((5,) + small.shape, f32), pltpu.VMEM((seqs, tokens, width), bf16),
            dma((17,)), dma((4, 4)),
            dma((5, chunks)), dma((5, chunks)), dma((5, chunks)), dma((5, chunks)),
            dma((chunks,)), dma((5,)), dma((5,)), dma((5,)), dma((5,)),
            dma((moves,)), dma((moves,)), dma((3 * seqs,)),
        ],
        compiler_params=pltpu.CompilerParams(
            collective_id=0, has_side_effects=True, vmem_limit_bytes=62 * 2**20
        ),
        cost_estimate=pl.CostEstimate(
            flops=8 * rows * width * ff + 16 * rows * width * width + 10 * rows * one * width,
            bytes_accessed=100 * 2**20, transcendentals=12 * rows * one,
        ),
        name="back",
    )(lengths, vecs, small, head, *saved, *weights)
    blocks = lax.axis_size("batch") // 8
    if blocks > 1:
        alike = [[i + 8 * j for j in range(blocks)] for i in range(8)]
        total = lax.psum(total, "batch", axis_index_groups=alike)
        small = lax.psum(small, "batch", axis_index_groups=alike)
        head = lax.all_gather(head, "batch", axis_index_groups=alike, axis=0, tiled=True)
    return total.reshape(12, width, width), small, head, lay, grad


def finish_kernel(
    seqs, total, small_ref, head_ref, vec_ref, pool_ref, lay_in, grad_in,
    lay_out, loss_out, grad_out, gq, gk, gv, go, gqb, gvb, gob, gg1, gb1, gin, gib, gou, gub,
    gg2, gb2, gpool, gpb, gcp, gcb,
    low_s, full_s, pool_s, pass_s, head_s, cls_s, in_sem, out_sem,
):
    units = low_s.shape[0]
    group = loss_out.shape[0]
    places = head_ref.shape[0]
    every = seqs * places
    loads = [pltpu.make_async_copy(total.at[u], low_s.at[u], in_sem.at[u]) for u in range(units)]
    for copy in loads:
        copy.start()
    targets = []
    for j in range(4):
        part = pl.ds(j * WIDTH, WIDTH)
        targets += [gou.at[part], gin.at[:, part]]
    targets += [go, gq, gk, gv]
    stores = [
        pltpu.make_async_copy(full_s.at[u], targets[u], out_sem.at[u]) for u in range(units)
    ]
    passed_in = [
        pltpu.make_async_copy(src, pass_s.at[i], in_sem.at[units + i])
        for i, src in enumerate((lay_in, grad_in))
    ]
    passed = [
        pltpu.make_async_copy(pass_s.at[i], dst, out_sem.at[units + i])
        for i, dst in enumerate((lay_out, grad_out))
    ]
    for copy in passed_in:
        copy.start()
    pool_store = pltpu.make_async_copy(pool_s, gpool, out_sem.at[units + 2])

    def widen(u):
        loads[u].wait()

        @pl.loop(0, WIDTH // 128)
        def _(i):
            r = tile(i, 128)
            full_s[u, r, :] = low_s[u, r, :].astype(f32)

        stores[u].start()

    for u in range(units):
        widen(u)
    for before, after in zip(passed_in, passed):
        before.wait()
        after.start()

    def exact(left, right, dims=NN):
        return lax.dot_general(left, right, dims, precision=highest, preferred_element_type=f32)

    head_s[...] = head_ref[...].astype(f32)
    eye = lax.broadcasted_iota(jnp.int32, (places, places), 0) == lax.broadcasted_iota(
        jnp.int32, (places, places), 1
    )
    label_rows = []
    for s in range(seqs):
        for j in range(6):
            cls_s[s * places : (s + 1) * places, j * 128 : (j + 1) * 128] = head_s[:, s * 6 + j, :]
        column = head_s[:, 6 * seqs, s : s + 1]
        label_rows.append(jnp.sum(jnp.where(eye, column, 0.0), axis=0, keepdims=True))
    cls = cls_s[...].astype(bf16)
    pooled = jnp.tanh(dot(cls, pool_ref[...]) + vec_ref[PB : PB + 1, :])
    row = lax.broadcasted_iota(jnp.int32, (8, 1), 0)
    class_rows = jnp.where(row < 3, vec_ref[CP : CP + 8, :], 0.0)
    picked = jnp.where(
        row == lax.broadcasted_iota(jnp.int32, (8, 128), 1), vec_ref[CB : CB + 1, 0:128], 0.0
    )
    logits = exact(class_rows, pooled, NT) + jnp.sum(picked, axis=-1, keepdims=True)
    logits = jnp.where(row < 3, logits, masked_fill)
    top = jnp.max(logits, axis=0, keepdims=True)
    raised = jnp.exp(logits - top)
    total_row = jnp.sum(raised, axis=0, keepdims=True)
    chosen = jnp.concatenate(
        [(row.astype(f32) == labels).astype(f32) for labels in label_rows], axis=-1
    )
    losses = (top + jnp.log(total_row)) - jnp.sum(
        jnp.where(chosen > 0.0, logits, 0.0), axis=0, keepdims=True
    )
    logit_grad = raised / total_row - chosen
    first = lax.axis_index("batch") * (group // seqs)
    own = lax.broadcasted_iota(jnp.int32, (every, 128), 1)
    pickers = (
        lax.broadcasted_iota(jnp.int32, (every, 128), 0)
        == (own % seqs) * places + first + own // seqs
    ).astype(f32)
    loss_out[...] = exact(losses, pickers)[0, 0:group]
    pre = exact(logit_grad, class_rows, TN) * (1.0 - pooled * pooled)
    ones = jnp.ones((1, every), f32)
    gcb[...] = exact(ones, logit_grad, NT)[0, 0:3]
    gpb[...] = jnp.sum(pre, axis=0)
    gcp[...] = exact(logit_grad, pooled)[0:3, :]
    high = pre.astype(bf16)
    rest = pre - high.astype(f32)
    mid = rest.astype(bf16)
    low = (rest - mid.astype(f32)).astype(bf16)
    for j in range(3):
        cols = pl.ds(j * 256, 256)
        part = cls_s[:, cols].astype(bf16)
        pool_s[cols, :] = dot(part, high, TN) + dot(part, mid, TN) + dot(part, low, TN)
    pool_store.start()
    for i, ref in (
        (QB, gqb), (VB, gvb), (OB, gob), (G1, gg1), (B1, gb1), (UB, gub), (G2, gg2), (B2, gb2),
    ):
        ref[...] = small_ref[i, :]
    for j in range(4):
        gib[j * WIDTH : (j + 1) * WIDTH] = small_ref[IB + j, :]
    for copy in stores + passed + [pool_store]:
        copy.wait()


def finish(seqs, total, small, head, vecs, pool, lay, grad):
    group, tokens, width = lay.shape
    anywhere = pl.BlockSpec(memory_space=pl.ANY)
    in_vmem = pl.BlockSpec(memory_space=pltpu.VMEM)
    square = ((width, width), f32, anywhere)
    row = ((width,), f32, in_vmem)
    outs = (
        [(lay.shape, bf16, anywhere), ((group,), f32, in_vmem), (grad.shape, bf16, anywhere)]
        + [square] * 4
        + [row] * 5
        + [((width, 4 * width), f32, anywhere), ((4 * width,), f32, in_vmem)]
        + [((4 * width, width), f32, anywhere), row, row, row]
        + [square, row, ((3, width), f32, in_vmem), ((3,), f32, in_vmem)]
    )
    units = total.shape[0]
    return pl.pallas_call(
        functools.partial(finish_kernel, seqs),
        out_shape=tuple(jax.ShapeDtypeStruct(s, t) for s, t, _ in outs),
        in_specs=[anywhere] + [in_vmem] * 4 + [anywhere, anywhere],
        out_specs=tuple(m for _, _, m in outs),
        scratch_shapes=[
            pltpu.VMEM((units, width, width), bf16), pltpu.VMEM((units, width, width), f32),
            pltpu.VMEM((width, width), f32), pltpu.VMEM((2,) + lay.shape, bf16),
            pltpu.VMEM(head.shape, f32), pltpu.VMEM((seqs * head.shape[0], width), f32),
            pltpu.SemaphoreType.DMA((units + 2,)), pltpu.SemaphoreType.DMA((units + 3,)),
        ],
        compiler_params=pltpu.CompilerParams(vmem_limit_bytes=60 * 2**20),
        name="finish",
    )(total, small, head, vecs, pool, lay, grad)


def local(
    states, lengths, labels, cotangent,
    query_proj, key_proj, value_proj, output_proj,
    query_bias, value_bias, output_bias, first_gain, first_bias,
    inner_proj, inner_bias, outer_proj, outer_bias, second_gain, second_bias,
    pool_proj, pool_bias, class_proj, class_bias,
):
    group, tokens, width = states.shape
    seqs = group // lax.axis_size("seq")
    vecs, small, head, x, q, k, v, att, n1, low, hid, slope, stat, y, aux, pg = forward(
        lengths, labels, states, cotangent,
        (query_proj, key_proj, value_proj, output_proj, inner_proj, outer_proj, pool_proj),
        (query_bias, value_bias, output_bias, first_gain, first_bias, inner_bias, outer_bias,
         second_gain, second_bias, pool_bias, class_proj.T, class_bias),
    )
    total, small, head, lay, grad = back(
        seqs, tokens, lengths, vecs, small, head,
        (pg, hid, slope, low, n1, stat, y, q, k, v, att, x, aux),
        (inner_proj, outer_proj, query_proj, key_proj, value_proj, output_proj),
    )
    out = finish(seqs, total, small, head, vecs, pool_proj, lay, grad)
    return out[:20] + (out[20].T,) + out[21:]


def solution(mesh):
    split = P("batch", "seq", None)
    in_specs = (split, P("batch"), P("batch"), split) + (P(),) * 19
    out_specs = (split, P("batch"), split) + (P(),) * 19
    return jax.shard_map(local, mesh=mesh, in_specs=in_specs, out_specs=out_specs, check_vma=False)
```

```python
import functools

import jax
import jax.numpy as jnp
from jax import lax
from jax.experimental import pallas as pl
from jax.experimental.pallas import tpu as pltpu
from jax.sharding import PartitionSpec as P

HEADS = 12
HEAD_DIM = 64
WIDTH = 768
HALF = 384
CHUNK = 256
MESH = pl.DeviceIdType.MESH

bf16 = jnp.bfloat16
f32 = jnp.float32
highest = lax.Precision.HIGHEST
norm_eps = 1e-06
masked_fill = -1e30
inv_root_two = 0.7071067811865476
inv_root_tau = 0.3989422804014327


def pick(code, table):
    out = table[-1]
    for i in range(len(table) - 2, -1, -1):
        out = jnp.where(code == i, table[i], out)
    return out


def flipped(index, bit):
    return index + bit * (1 - 2 * ((index // bit) % 2))


NT = (((1,), (1,)), ((), ()))
NN = (((1,), (0,)), ((), ()))
TN = (((0,), (0,)), ((), ()))
VECS = 24
QB, VB, OB, G1, B1, IB, UB, G2, B2, PB, CP, CB = 0, 1, 2, 3, 4, 5, 9, 10, 11, 12, 13, 16


def dot(left, right, dims=NN):
    return lax.dot_general(left, right, dims, preferred_element_type=f32)


def gelu_parts(u):
    t = 1.0 / (1.0 + (0.3275911 * inv_root_two) * jnp.abs(u))
    bell = jnp.exp(-0.5 * u * u)
    poly = 1.061405429
    for coefficient in (-1.453152027, 1.421413741, -0.284496736, 0.254829592):
        poly = poly * t + coefficient
    tail = (0.5 * t) * poly * bell
    cumulative = jnp.where(u >= 0.0, 1.0 - tail, tail)
    return u * cumulative, cumulative + u * (bell * inv_root_tau)


def norm_rows(z):
    average = jnp.mean(z, axis=-1, keepdims=True)
    centered = z - average
    inv_root = lax.rsqrt(jnp.mean(centered * centered, axis=-1, keepdims=True) + norm_eps)
    return centered * inv_root, inv_root


def norm_rows_back(upstream, normed, inv_root, gain):
    scaled = upstream * gain
    return inv_root * (
        scaled
        - jnp.mean(scaled, axis=-1, keepdims=True)
        - normed * jnp.mean(scaled * normed, axis=-1, keepdims=True)
    )


def tile(i, size):
    return pl.ds(pl.multiple_of(i * size, size), size)


def copies(pairs, sems):
    out = []
    for i, (src, dst) in enumerate(pairs):
        out.append(pltpu.make_async_copy(src, dst, sems.at[i]))
    return out


def head_lanes(which):
    lane = lax.broadcasted_iota(jnp.int32, (1, 128), 1)
    return (lane >= 64) if which else (lane < 64)


def only(mask, block):
    return jnp.where(mask, block, jnp.zeros_like(block))


def attend_pair(q2, k2, v2, length, keys):
    k2 = k2[:keys]
    v2 = v2[:keys]
    place = lax.broadcasted_iota(jnp.int32, (1, keys), 1)
    out = None
    logs = []
    for which in (0, 1):
        lanes = head_lanes(which)
        scores = dot(only(lanes, q2) * bf16(0.125), k2, NT)
        scores = jnp.where(place < length, scores, masked_fill)
        top = jnp.max(scores, axis=-1, keepdims=True)
        weights = jnp.exp(scores - top)
        total = jnp.sum(weights, axis=-1, keepdims=True)
        part = dot(weights.astype(bf16), only(lanes, v2)) * (1.0 / total)
        out = part if out is None else out + part
        logs.append(top + jnp.log(total))
    return out, logs


def three_terms(values):
    high = values.astype(bf16).astype(f32)
    mid = (values - high).astype(bf16).astype(f32)
    return high, mid, values - high - mid


def attend_back_pair(q2, k2, v2, d2, a2, q_aux, key_aux, value_aux):
    lane = lax.broadcasted_iota(jnp.int32, (1, 128), 1)
    product = d2.astype(f32) * a2.astype(f32)
    d_aux = jnp.zeros_like(product)
    for which in (0, 1):
        delta = jnp.sum(only(head_lanes(which), product), axis=-1, keepdims=True)
        for i, piece in enumerate(three_terms(-delta)):
            d_aux = jnp.where(lane == 64 * (1 - which) + i, piece, d_aux)
    d_aux = d_aux.astype(bf16)
    q2 = q2 * bf16(0.125)
    heads = []
    for which in (0, 1):
        lanes = head_lanes(which)
        heads.append(
            [
                jnp.where(lanes, block, other)
                for block, other in ((q2, q_aux), (k2, key_aux), (v2, value_aux), (d2, d_aux))
            ]
        )
    scores = [dot(kh, qh, NT) for qh, kh, _, _ in heads]
    prob_grads = [dot(vh, dh, NT) for _, _, vh, dh in heads]
    probs = [jnp.exp(s) for s in scores]
    score_grads = [(p * g).astype(bf16) for p, g in zip(probs, prob_grads)]
    out = [
        (dot(g, kh, TN), dot(g, qh), dot(p.astype(bf16), dh))
        for g, p, (qh, kh, _, dh) in zip(score_grads, probs, heads)
    ]
    first = head_lanes(0)
    dq, dk, dv = [jnp.where(first, one, two) for one, two in zip(*out)]
    return dq * 0.125, dk, dv


def exit_back(cls_rows, labels, vec_ref, pool_s):
    pooled = jnp.tanh(dot(cls_rows, pool_s[...]) + vec_ref[PB : PB + 1, :])
    class_rows = vec_ref[CP : CP + 3, :]
    logits = [
        jnp.sum(pooled * class_rows[i : i + 1, :], axis=-1, keepdims=True)
        + vec_ref[CB : CB + 1, i : i + 1]
        for i in range(3)
    ]
    top = jnp.maximum(jnp.maximum(logits[0], logits[1]), logits[2])
    raised = [jnp.exp(l - top) for l in logits]
    total = raised[0] + raised[1] + raised[2]
    back = jnp.zeros_like(pooled)
    for i in range(3):
        back = back + (raised[i] / total - (labels == i).astype(f32)) * class_rows[i : i + 1, :]
    pre = back * (1.0 - pooled * pooled)
    high = pre.astype(bf16)
    rest = pre - high.astype(f32)
    mid = rest.astype(bf16)
    low = (rest - mid.astype(f32)).astype(bf16)
    return dot(high, pool_s[...], NT) + dot(mid, pool_s[...], NT) + dot(low, pool_s[...], NT)


def spread(src, dst, seqs, tokens, to_rows, sends, recvs, base, s, ordered=False):
    count = lax.axis_size("seq")
    b = lax.axis_index("batch")
    z = lax.axis_index("seq")
    out = []
    for d in range(1, count):
        if ordered and count == 4:
            d = jnp.where(z % 2 == 0, d % 3 + 1, d)
        other = lax.rem(z + d, count)
        if to_rows:
            source = src.at[other * seqs + s]
            target = dst.at[pl.ds(pl.multiple_of((s * count + z) * tokens, tokens), tokens)]
        else:
            source = src.at[pl.ds(pl.multiple_of((s * count + other) * tokens, tokens), tokens)]
            target = dst.at[z * seqs + s]
        i = base + s * (count - 1) + d - 1
        out.append(
            pltpu.make_async_remote_copy(
                source, target, sends.at[i], recvs.at[i],
                device_id=(b, other), device_id_type=MESH,
            )
        )
    return out


def own_part(src, dst, seqs, tokens, to_rows, sem, s):
    count = lax.axis_size("seq")
    z = lax.axis_index("seq")
    block = z * seqs + s
    rows = pl.ds(pl.multiple_of((s * count + z) * tokens, tokens), tokens)
    if to_rows:
        return pltpu.make_async_copy(src.at[block], dst.at[rows], sem)
    return pltpu.make_async_copy(src.at[rows], dst.at[block], sem)


def greet_line():
    count = lax.axis_size("seq")
    z = lax.axis_index("seq")
    return [(lax.axis_index("batch"), lax.rem(z + d, count)) for d in range(1, count)]


def forward_kernel(
    seqs, len_ref, label_ref, states, cot, wq, wk, wv, wo, w1, w2, pool,
    query_bias, value_bias, output_bias, first_gain, first_bias, inner_bias, outer_bias,
    second_gain, second_bias, pool_bias, class_proj, class_bias,
    vec_ref, small_out, head_out, x_out, q_out, k_out, v_out, att_out, n1_out, low_out, hid_out,
    slope_out, stat_out, y_out, aux_out, pg_out,
    x_s, wq_s, wk_s, wv_s, wo_s, w1_s, w2_s,
    q_s, k_s, v_s, att_s, n1_s, low_s, hid_s, slope_s, stat_s, y_s, aux_s, n2_s, z_s,
    cot_s, pool_s, row_s, in_sem, out_sem, own_sem, sends, recvs,
):
    rows = z_s.shape[0]
    tokens = states.shape[1]
    line = greet_line()
    barrier = pltpu.get_barrier_semaphore()
    for who in line:
        pl.semaphore_signal(barrier, inc=1, device_id=who, device_id_type=MESH)
    weights_in = copies(
        [(wq, wq_s), (wk, wk_s), (wv, wv_s), (wo, wo_s), (w1, w1_s), (w2, w2_s), (pool, pool_s)],
        in_sem,
    )
    z = lax.axis_index("seq")
    own = [own_part(states, x_s, seqs, tokens, True, own_sem.at[s], s) for s in range(seqs)]
    own_cot = [
        own_part(cot, cot_s, seqs, tokens, True, own_sem.at[seqs + s], s) for s in range(seqs)
    ]
    for copy in own + weights_in + own_cot:
        copy.start()
    pl.semaphore_wait(barrier, len(line))

    def move(first, s, ordered):
        src, dst, start = (states, x_s, 0) if first else (cot, cot_s, seqs * len(line))
        return spread(src, dst, seqs, tokens, True, sends, recvs, start, s, ordered)

    moves = [move(True, s, False) for s in range(seqs)]
    late = [move(False, s, False) for s in range(seqs)]
    for copy in move(True, 0, False):
        copy.start()
    vec_ref[...] = jnp.zeros_like(vec_ref)
    for i, ref in (
        (QB, query_bias), (VB, value_bias), (OB, output_bias), (G1, first_gain), (B1, first_bias),
        (UB, outer_bias), (G2, second_gain), (B2, second_bias), (PB, pool_bias),
    ):
        vec_ref[i : i + 1, :] = ref[...].astype(f32).reshape(1, WIDTH)
    for i in range(4):
        vec_ref[IB + i : IB + i + 1, :] = (
            inner_bias[i * WIDTH : (i + 1) * WIDTH].astype(f32).reshape(1, WIDTH)
        )
    vec_ref[CP : CP + 3, :] = class_proj[...].astype(f32)
    vec_ref[CB : CB + 1, 0:3] = class_bias[...].astype(f32).reshape(1, 3)

    waiting = []
    def send_late(s):
        for copy in move(False, s, False):
            copy.start()

    for s in range(seqs):
        for copy in moves[s]:
            copy.wait_recv()
        own[s].wait()
        if s == 0:
            for i in range(1, seqs):
                for copy in move(True, i, False):
                    copy.start()
        part = pl.ds(s * rows, rows)
        waiting += forward_rows(
            s, part, len_ref[z * seqs + s], rows, s == 0, vec_ref, weights_in,
            (lambda: send_late(0)) if s == 0 else None,
            (x_s, wq_s, wk_s, wv_s, wo_s, w1_s, w2_s, q_s, k_s, v_s, att_s, n1_s, low_s, hid_s,
             slope_s, stat_s, y_s, aux_s, n2_s, z_s),
            (x_out, q_out, k_out, v_out, att_out, n1_out, low_out, hid_out, slope_out,
             stat_out, y_out, aux_out),
            out_sem,
        )
        if s == 0:
            for i in range(1, seqs):
                send_late(i)

    place = lax.broadcasted_iota(jnp.int32, (16 * seqs, 1), 0)
    labels = jnp.zeros((16 * seqs, 1), jnp.int32)
    label_row = jnp.zeros((1, 128), f32)
    lane = lax.broadcasted_iota(jnp.int32, (1, 128), 1)
    for s in range(seqs):
        label = label_ref[z * seqs + s]
        labels = jnp.where(place == 16 * s, label, labels)
        label_row = jnp.where(lane == s, label.astype(f32), label_row)
    cls_rows = jnp.concatenate([y_s[s * rows : s * rows + 16, :] for s in range(seqs)])
    weights_in[6].wait()
    cls_grad = exit_back(cls_rows, labels, vec_ref, pool_s)
    row_s[...] = jnp.zeros_like(row_s)
    for s in range(seqs):
        first = y_s[s * rows : s * rows + 16, :].astype(f32)
        for j in range(6):
            row_s[s * 6 + j : s * 6 + j + 1, :] = first[0:1, j * 128 : (j + 1) * 128]
    row_s[6 * seqs : 6 * seqs + 1, :] = label_row
    head_out[...] = row_s[...].astype(bf16)
    small_out[...] = jnp.zeros_like(small_out)

    def add_sum(index, values):
        small_out[index : index + 1, :] += jnp.sum(values, axis=0, keepdims=True)

    for s in range(seqs):
        for copy in late[s]:
            copy.wait_recv()
        own_cot[s].wait()

        @pl.loop(0, rows // 128)
        def _(i):
            r = pl.ds(pl.multiple_of(s * rows + i * 128, 128), 128)
            place = lax.broadcasted_iota(jnp.int32, (128, 1), 0) + i * 128
            upstream = cot_s[r, :].astype(f32) + jnp.where(
                place == 0, cls_grad[16 * s : 16 * s + 1, :], 0.0
            )
            normed = n2_s[r, :].astype(f32)
            add_sum(G2, upstream * normed)
            add_sum(B2, upstream)
            grad = norm_rows_back(upstream, normed, stat_s[r, 13:14], vec_ref[G2 : G2 + 1, :])
            rounded = grad.astype(bf16)
            n2_s[r, :] = rounded
            add_sum(UB, rounded.astype(f32))

        part = pl.ds(s * rows, rows)
        waiting.append(pltpu.make_async_copy(n2_s.at[part], pg_out.at[part], out_sem.at[s, 12]))
        waiting[-1].start()
    for group in moves + late:
        for copy in group:
            copy.wait_send()
    for copy in waiting:
        copy.wait()


def forward_rows(
    s, part, length, rows, first_time, vec_ref, weights_in, halfway, scratch, outs, out_sem
):
    (x_s, wq_s, wk_s, wv_s, wo_s, w1_s, w2_s, q_s, k_s, v_s, att_s, n1_s, low_s, hid_s,
     slope_s, stat_s, y_s, aux_s, n2_s, z_s) = scratch
    start = s * rows
    out = [
        pltpu.make_async_copy(src.at[part], dst.at[part], out_sem.at[s, i])
        for i, (src, dst) in enumerate(
            zip(
                (x_s, q_s, k_s, v_s, att_s, n1_s, low_s, hid_s, slope_s, stat_s, y_s, aux_s), outs
            )
        )
    ]
    out[0].start()
    for i, (w, dst, bias) in enumerate(((wq_s, q_s, QB), (wk_s, k_s, None), (wv_s, v_s, VB))):
        if first_time:
            weights_in[i].wait()

        @pl.loop(0, WIDTH // 256)
        def _(j):
            cols = tile(j, 256)
            grid = dot(x_s[part, :], w[:, cols])
            if bias is not None:
                grid = grid + vec_ref[bias : bias + 1, cols]
            dst[part, cols] = grid.astype(bf16)

        out[1 + i].start()

    stat_s[part, :] = jnp.zeros((rows, 128), f32)
    lane = lax.broadcasted_iota(jnp.int32, (1, 128), 1)

    @pl.loop(0, HEADS // 2)
    def _(p):
        cols = tile(p, 128)
        mix, logs = attend_pair(q_s[part, cols], k_s[part, cols], v_s[part, cols], length, rows)
        att_s[part, cols] = mix.astype(bf16)
        aux = jnp.where((lane == 3) | (lane == 67), 1.0, jnp.zeros((rows, 128), f32))
        for which in (0, 1):
            for i, piece in enumerate(three_terms(-logs[which])):
                aux = jnp.where(lane == 64 * (1 - which) + i, piece, aux)
        aux_s[part, cols] = aux.astype(bf16)

    out[4].start()
    out[11].start()
    if halfway is not None:
        halfway()
    if first_time:
        weights_in[3].wait()

    @pl.loop(0, WIDTH // 256)
    def _(j):
        cols = tile(j, 256)
        z_s[:, cols] = (
            x_s[part, cols].astype(f32)
            + dot(att_s[part, :], wo_s[:, cols])
            + vec_ref[OB : OB + 1, cols]
        )

    @pl.loop(0, rows // 128)
    def _(i):
        r = tile(i, 128)
        q = pl.ds(pl.multiple_of(start + i * 128, 128), 128)
        normed, inv_root = norm_rows(z_s[r, :])
        n1_s[q, :] = normed.astype(bf16)
        first = normed * vec_ref[G1 : G1 + 1, :] + vec_ref[B1 : B1 + 1, :]
        low_s[q, :] = first.astype(bf16)
        z_s[r, :] = first + vec_ref[UB : UB + 1, :]
        stat_s[q, :] = jnp.where(lane == 12, inv_root, stat_s[q, :])

    out[5].start()
    out[6].start()
    if first_time:
        weights_in[4].wait()
        weights_in[5].wait()
    ft = 256

    @pl.loop(0, 4 * WIDTH // ft)
    def _(j):
        cols = tile(j, ft)
        u = dot(low_s[part, :], w1_s[:, cols]) + vec_ref[pl.ds(IB + j // 3, 1), tile(j % 3, ft)]
        h, slope = gelu_parts(u)
        hid_s[part, cols] = h.astype(bf16)
        slope_s[part, cols] = slope.astype(bf16)

    out[7].start()
    out[8].start()

    @pl.loop(0, WIDTH // 256)
    def _(j):
        cols = tile(j, 256)
        z_s[:, cols] += dot(hid_s[part, :], w2_s[:, cols])

    @pl.loop(0, rows // 128)
    def _(i):
        r = tile(i, 128)
        q = pl.ds(pl.multiple_of(start + i * 128, 128), 128)
        normed, inv_root = norm_rows(z_s[r, :])
        n2_s[q, :] = normed.astype(bf16)
        y_s[q, :] = (normed * vec_ref[G2 : G2 + 1, :] + vec_ref[B2 : B2 + 1, :]).astype(bf16)
        stat_s[q, :] = jnp.where(lane == 13, inv_root, stat_s[q, :])

    for i in (9, 10):
        out[i].start()
    return out


def forward(lengths, labels, states, cotangent, weights, small):
    count = lax.axis_size("seq")
    group, tokens, width = states.shape
    seqs = group // count
    one = count * tokens
    rows = seqs * one
    ff = 4 * width
    anywhere = pl.BlockSpec(memory_space=pl.ANY)
    in_vmem = pl.BlockSpec(memory_space=pltpu.VMEM)
    wide = ((rows, width), bf16)
    saved = [wide] * 6 + [((rows, ff), bf16)] * 2 + [((rows, 128), f32), wide, wide, wide]
    outs = [((VECS, width), f32), ((16, width), f32), ((16, 128), bf16), wide] + saved
    moves = 2 * seqs * (count - 1)
    flops = 2 * rows * width * (4 * width + 2 * ff) + 4 * rows * one * width
    dma = pltpu.SemaphoreType.DMA
    return pl.pallas_call(
        functools.partial(forward_kernel, seqs),
        out_shape=tuple(jax.ShapeDtypeStruct(s, t) for s, t in outs),
        in_specs=[pl.BlockSpec(memory_space=pltpu.SMEM)] * 2
        + [anywhere] * 9
        + [in_vmem] * len(small),
        out_specs=(in_vmem,) * 3 + (anywhere,) * (len(outs) - 3),
        scratch_shapes=[pltpu.VMEM((rows, width), bf16)]
        + [pltpu.VMEM(w.shape, bf16) for w in weights[:6]]
        + [pltpu.VMEM(s, t) for s, t in saved]
        + [
            pltpu.VMEM((one, width), f32), pltpu.VMEM((rows, width), bf16),
            pltpu.VMEM((width, width), bf16), pltpu.VMEM((16, 128), f32),
            dma((7,)), dma((seqs, 13)), dma((2 * seqs,)),
            dma((moves,)), dma((moves,)),
        ],
        compiler_params=pltpu.CompilerParams(
            collective_id=1, has_side_effects=True, vmem_limit_bytes=60 * 2**20
        ),
        cost_estimate=pl.CostEstimate(
            flops=flops, bytes_accessed=50 * 2**20, transcendentals=rows * (ff + 12 * one)
        ),
        name="forward",
    )(lengths, labels, states, cotangent, *weights, *small)


def place_of_block():
    return (lax.axis_index("batch") % 8) * 4 + lax.axis_index("seq")


def back_kernel(
    seqs, chunks, pattern, lags, len_ref, vec_ref, small_ref, head_ref,
    pg, hid, slope, low, n1, stat, y, q, k, v, att, x, aux,
    w1, w2, wq, wk, wv, wo,
    out_ref, small_out, head_out, lay_out, grad_out,
    wide, fg_s, stat_s, w1_s, w2_s,
    acc, staged, r0, r1, r2, r3, r4, sgot, own_s,
    in_sem, hid_sem, rs_send, rs_recv, ag_send, ag_recv, loc, sm_send, sm_recv, hd_send, hd_recv,
    tok_send, tok_recv, tok_own,
):
    rows = fg_s.shape[0]
    one = rows // seqs
    tokens = lay_out.shape[1]
    count = lax.axis_size("seq")
    b = lax.axis_index("batch")
    z = lax.axis_index("seq")
    core = b % 2

    got = [r0, r1, r2, r3, r4]
    res = r0
    near_b = [flipped(b, 2), flipped(b, 4), b, b]
    near_z = [z, z, flipped(z, 1), flipped(z, 2)]
    mine = [(b // 2) % 2, (b // 4) % 2, z % 2, (z // 2) % 2]
    orders = {"x": (0, 1, 2, 3), "y": (1, 0, 2, 3)}
    period = len(pattern)

    def direction(c, level):
        code = c % period
        dirs = [orders[p][level] for p in pattern]
        return (
            pick(code, [near_b[d] for d in dirs]),
            pick(code, [near_z[d] for d in dirs]),
            pick(code, [mine[d] for d in dirs]),
        )

    core_partner = (flipped(b, 1), z)
    barrier = pltpu.get_barrier_semaphore()
    partners = [(near_b[2], near_z[2]), (near_b[3], near_z[3]), core_partner]
    partners += [(near_b[0], near_z[0]), (near_b[1], near_z[1])]
    greeted = [core_partner, (near_b[0], near_z[0]), (near_b[1], near_z[1])] + greet_line()
    for who in greeted:
        pl.semaphore_signal(barrier, inc=1, device_id=who, device_id_type=MESH)

    def base(c, level):
        first = 0
        size = CHUNK
        for l in range(level):
            size = size // 2
            first = first + direction(c, l)[2] * size
        return pl.multiple_of(first, 16)

    slots = staged.shape[0]
    my_cols = pl.ds(pl.multiple_of(core * HALF, HALF), HALF)

    def rs_copy(c, s):
        if s == 0:
            return pltpu.make_async_remote_copy(
                staged.at[c % slots], r0.at[c], rs_send.at[0, c], rs_recv.at[0, c],
                device_id=core_partner, device_id_type=MESH,
            )
        size = CHUNK >> s
        nb, nz, m = direction(c, s - 1)
        start = pl.multiple_of(base(c, s - 1) + (1 - m) * size, 16)
        return pltpu.make_async_remote_copy(
            acc.at[c, pl.ds(start, size)], got[s].at[c], rs_send.at[s, c], rs_recv.at[s, c],
            device_id=(nb, nz), device_id_type=MESH,
        )

    def out_rows(c):
        return out_ref.at[pl.ds(pl.multiple_of(c * CHUNK, CHUNK), CHUNK), my_cols]

    def ag_copy(c, s):
        if s == 0:
            return pltpu.make_async_remote_copy(
                res.at[c], out_rows(c), ag_send.at[0, c], ag_recv.at[0, c],
                device_id=core_partner, device_id_type=MESH,
            )
        size = CHUNK >> s
        nb, nz, _ = direction(c, s - 1)
        start = base(c, s)
        return pltpu.make_async_remote_copy(
            res.at[c, pl.ds(start, size)], res.at[c, pl.ds(start, size)],
            ag_send.at[s, c], ag_recv.at[s, c], device_id=(nb, nz), device_id_type=MESH,
        )

    def loc_out(c):
        return pltpu.make_async_copy(res.at[c], out_rows(c), loc.at[c])

    def stage_scatter(s, c):
        rs_copy(c, s - 1).wait_recv()
        half = CHUNK >> s
        start = base(c, s - 1)
        m = direction(c, s - 1)[2]
        for which in (0, 1):
            off = pl.multiple_of(((1 - m) if which == 0 else m) * half, 16)
            part = pl.ds(pl.multiple_of(start + off, 16), half)
            acc[c, part] = acc[c, part] + got[s - 1][c, pl.ds(off, half)]
            if which == 0:
                rs_copy(c, s).start()

    def stage_turn(c):
        rs_copy(c, 4).wait_recv()
        part = pl.ds(base(c, 4), 16)
        res[c, part] = acc[c, part] + r4[c]
        ag_copy(c, 4).start()

    def stage_gather(s, c):
        ag_copy(c, s + 1).wait_recv()
        ag_copy(c, s).start()
        if s == 0:
            loc_out(c).start()

    def stage_last(c):
        ag_copy(c, 0).wait_recv()
        loc_out(c).wait()
        for s in range(1, 5):
            rs_copy(c, s).wait_send()
        for s in range(5):
            ag_copy(c, s).wait_send()

    stages = (
        [functools.partial(stage_scatter, s) for s in (1, 2, 3, 4)]
        + [stage_turn]
        + [functools.partial(stage_gather, s) for s in (3, 2, 1, 0)]
        + [stage_last]
    )

    piece = tokens // 4
    per_seq = 4 * (count - 1)

    def send_piece(src, dst, first_sem, number):
        s = number // per_seq
        part = (number // (count - 1)) % 4
        d = number % (count - 1)
        other = (z + d + 1) % count
        i = first_sem + s * (count - 1) + d
        start = pl.multiple_of((s * count + other) * tokens + part * piece, piece)
        pltpu.make_async_remote_copy(
            src.at[pl.ds(start, piece)],
            dst.at[z * seqs + s, pl.ds(pl.multiple_of(part * piece, piece), piece)],
            tok_send.at[i], tok_recv.at[i], device_id=(b, other), device_id_type=MESH,
        ).start()

    def tick(t):
        @pl.when(t < seqs * per_seq)
        def _():
            send_piece(y, lay_out, 0, t)

        @pl.when((t >= 23) & (t < 23 + seqs * per_seq))
        def _():
            send_piece(wide.at[3], grad_out, seqs * (count - 1), t - 23)

        for stage, lag in reversed(list(zip(stages, lags))):
            c = t - lag

            @pl.when((c >= 0) & (c < chunks))
            def _():
                stage(c)

    def give(c, left, right, fresh=False):
        grad = dot(left, right, TN).astype(bf16)
        first = grad[:, 0:HALF]
        second = grad[:, HALF:]

        @pl.when(c >= slots)
        def _():
            rs_copy(c - slots, 0).wait_send()

        staged[c % slots] = jnp.where(core == 0, second, first)
        acc[c] = jnp.where(core == 0, first, second)
        rs_copy(c, 0).start()

    (low_s, n1_s, pg_s, eg_s) = [wide.at[i] for i in range(2, 6)]
    ag_s = wide.at[10]

    def chunk_load(j):
        cols = pl.ds(pl.multiple_of(j * WIDTH, WIDTH), WIDTH)
        return (
            pltpu.make_async_copy(hid.at[:, cols], wide.at[6 + j % 2], hid_sem.at[0, j]),
            pltpu.make_async_copy(slope.at[:, cols], wide.at[8 + j % 2], hid_sem.at[1, j]),
        )

    pg_load, low_load, n1_load, stat_load = copies(
        [(pg, pg_s), (low, low_s), (n1, n1_s), (stat, stat_s)], in_sem
    )

    def weight_load(j):
        part = pl.ds(pl.multiple_of(j * WIDTH, WIDTH), WIDTH)
        return (
            pltpu.make_async_copy(w2.at[part], w2_s.at[part], hid_sem.at[2, j]),
            pltpu.make_async_copy(w1.at[:, part], w1_s.at[:, part], hid_sem.at[3, j]),
        )

    pg_load.start()
    for copy in chunk_load(0) + weight_load(0)[:1] + (low_load,) + weight_load(0)[1:]:
        copy.start()
    own_in = [
        pltpu.make_async_copy(
            y.at[pl.ds(pl.multiple_of(s * one + z * tokens, tokens), tokens)],
            own_s.at[s], tok_own.at[s],
        )
        for s in range(seqs)
    ]
    own_y = [
        pltpu.make_async_copy(own_s.at[s], lay_out.at[z * seqs + s], tok_own.at[2 * seqs + s])
        for s in range(seqs)
    ]
    for copy in own_in:
        copy.start()
    later = copies(
        [(q, wide.at[0]), (k, wide.at[1]), (aux, wide.at[11])], in_sem.at[pl.ds(7, 3)]
    )
    middle = copies([(v, wide.at[6]), (att, wide.at[8])], in_sem.at[pl.ds(10, 2)])
    (x_load,) = copies([(x, wide.at[7])], in_sem.at[pl.ds(12, 1)])
    attn_weights = [
        pltpu.make_async_copy(w, w2_s.at[pl.ds(i * WIDTH, WIDTH)], in_sem.at[13 + i])
        for i, w in enumerate((wo, wq, wk, wv))
    ]
    block = place_of_block()
    head_out[block] = head_ref[...]
    small_out[...] = small_ref[...]
    y_moves = []
    for s in range(seqs):
        y_moves += spread(y, lay_out, seqs, tokens, False, tok_send, tok_recv, 0, s)
    pl.semaphore_wait(barrier, len(greeted))
    ROW = 128

    def add_sum(index, values):
        small_out[index : index + 1, :] += jnp.sum(values, axis=0, keepdims=True)

    pg_load.wait()

    @pl.loop(0, 4)
    def _(j):
        chunk_load(j)[0].wait()

        @pl.loop(0, 3)
        def _(t):
            give(6 * j + t, wide[6 + j % 2, :, tile(t, 256)], pg_s[...])

            @pl.when(j < 2)
            def _():
                tick(6 * j + t)

        chunk_load(j)[1].wait()
        weight_load(j)[0].wait()

        @pl.when(j < 3)
        def _():
            for copy in chunk_load(j + 1) + weight_load(j + 1):
                copy.start()

        @pl.when(j == 0)
        def _():
            for before, after in zip(own_in, own_y):
                before.wait()
                after.start()
            fg_s[...] = pg_s[...].astype(f32)

        @pl.when(j == 1)
        def _():
            for copy in (n1_load, stat_load):
                copy.start()

        @pl.when(j == 2)
        def _():
            for copy in later:
                copy.start()

        @pl.when(j == 3)
        def _():
            for copy in middle:
                copy.start()

        @pl.loop(0, WIDTH // 256)
        def _(t):
            cols = tile(t, 256)
            ff = pl.ds(pl.multiple_of(j * WIDTH + t * 256, 256), 256)
            grad = dot(pg_s[...], w2_s[ff, :], NT) * wide[8 + j % 2, :, cols].astype(f32)
            rounded = grad.astype(bf16)
            eg_s[:, cols] = rounded
            small_out[pl.ds(IB + j, 1), cols] = jnp.sum(
                rounded.astype(f32), axis=0, keepdims=True
            )

        for i in range(4):

            @pl.when(j == i)
            def _():
                attn_weights[i].start()

        @pl.when(j == 0)
        def _():
            low_load.wait()

        @pl.loop(0, 3)
        def _(t):
            give(6 * j + 3 + t, low_s[:, tile(t, 256)], eg_s[...])

            @pl.when(j < 2)
            def _():
                tick(6 * j + 3 + t)

        @pl.when(j >= 2)
        def _():
            tick(6 + 3 * j)

        weight_load(j)[1].wait()
        ff_cols = pl.ds(pl.multiple_of(j * WIDTH, WIDTH), WIDTH)

        @pl.loop(0, WIDTH // 256)
        def _(t):
            cols = tile(t, 256)
            fg_s[:, cols] += dot(eg_s[...], w1_s[cols, ff_cols], NT)

        @pl.when(j >= 2)
        def _():
            tick(7 + 3 * j)
            tick(8 + 3 * j)

    x_load.start()
    n1_load.wait()
    stat_load.wait()

    @pl.loop(0, rows // ROW)
    def _(i):
        r = tile(i, ROW)
        upstream = fg_s[r, :]
        normed = n1_s[r, :].astype(f32)
        add_sum(G1, upstream * normed)
        add_sum(B1, upstream)
        zg = norm_rows_back(upstream, normed, stat_s[r, 12:13], vec_ref[G1 : G1 + 1, :])
        rounded = zg.astype(bf16)
        ag_s[r, :] = rounded
        add_sum(OB, rounded.astype(f32))

    tick(18)

    (q_s, k_s, dv_s, sg_s, dq_s, dk_s, v_s, x_s, att_s, dat_s) = [wide.at[i] for i in range(10)]
    wo_s, wq_s, wk_s, wv_s = [w2_s.at[pl.ds(i * WIDTH, WIDTH)] for i in range(4)]
    attn_weights[0].wait()

    @pl.loop(0, WIDTH // 256)
    def _(t):
        cols = tile(t, 256)
        dat_s[:, cols] = dot(ag_s[...], wo_s[cols, :], NT).astype(bf16)

    for copy in middle + later:
        copy.wait()

    @pl.loop(0, 3)
    def _(t):
        give(24 + t, att_s[:, tile(t, 256)], ag_s[...])

    tick(19)
    aux_s = wide.at[11]
    for copy in attn_weights[1:]:
        copy.wait()
    x_load.wait()
    lane = lax.broadcasted_iota(jnp.int32, (1, 128), 1)

    def move(s, ordered):
        return spread(
            sg_s, grad_out, seqs, tokens, False, tok_send, tok_recv, seqs * (count - 1), s, ordered
        )

    own_sg = [
        own_part(sg_s, grad_out, seqs, tokens, False, tok_own.at[seqs + s], s) for s in range(seqs)
    ]

    def states_rows(s):
        part = pl.ds(pl.multiple_of(s * one, one), one)

        @pl.loop(0, WIDTH // 256)
        def _(t):
            cols = tile(t, 256)
            total = ag_s[part, cols].astype(f32)
            for d, w in ((dq_s, wq_s), (dk_s, wk_s), (dv_s, wv_s)):
                total = total + dot(d[part, :], w[cols, :], NT)
            sg_s[part, cols] = total.astype(bf16)
            for index, d in ((QB, dq_s), (VB, dv_s)):
                small_out[index : index + 1, cols] += jnp.sum(
                    d[part, cols].astype(f32), axis=0, keepdims=True
                )

        own_sg[s].start()

    @pl.loop(0, seqs)
    def _(s):
        part = pl.ds(pl.multiple_of(s * one, one), one)
        hidden = lax.broadcasted_iota(jnp.int32, (one, 1), 0) >= len_ref[z * seqs + s]
        ones = jnp.where((lane % 64) < 3, 1.0, jnp.zeros((one, 128), f32))
        key_aux = jnp.where((lane % 64 == 3) & hidden, masked_fill, ones).astype(bf16)
        value_aux = ones.astype(bf16)

        @pl.loop(0, 2)
        def _(i):
            for turn in range(3):
                cols = tile(3 * i + turn, 128)
                dq, dk, dv = attend_back_pair(
                    q_s[part, cols], k_s[part, cols], v_s[part, cols], dat_s[part, cols],
                    att_s[part, cols], aux_s[part, cols], key_aux, value_aux,
                )
                dq_s[part, cols] = dq.astype(bf16)
                dk_s[part, cols] = dk.astype(bf16)
                dv_s[part, cols] = dv.astype(bf16)
            tick(20 + 4 * s + 2 * i)

            @pl.when(i == 0)
            def _():
                tick(21 + 4 * s)

        @pl.when(s == 0)
        def _():
            states_rows(0)

        tick(23 + 4 * s)

    moves = []
    for s in range(seqs):
        moves += move(s, False)
    done = 18 + 5 * seqs
    for i, d in enumerate((dq_s, dk_s, dv_s)):

        @pl.loop(0, 3)
        def _(t):
            give(27 + 3 * i + t, x_s[:, tile(t, 256)], d[...])
            tick(done + 3 * i + t)

        if i == 1:
            for s in range(1, seqs):
                states_rows(s)

    done += 9


    def small_copies(i):
        first = block - block % (1 << i)
        part = pl.ds(first, 1 << i)
        return (
            pltpu.make_async_remote_copy(
                small_out, sgot.at[i], sm_send.at[i], sm_recv.at[i],
                device_id=partners[i], device_id_type=MESH,
            ),
            pltpu.make_async_remote_copy(
                head_out.at[part], head_out.at[part], hd_send.at[i], hd_recv.at[i],
                device_id=partners[i], device_id_type=MESH,
            ),
        )


    def late_tick(t, carry):
        for i in range(len(partners) + 1):

            @pl.when(t == done + 3 * i)
            def _():
                if i > 0:
                    for copy in small_copies(i - 1):
                        copy.wait()
                    small_out[...] = small_out[...] + sgot[i - 1]
                if i < len(partners):
                    for copy in small_copies(i):
                        copy.start()

        tick(t)
        return carry

    lax.fori_loop(done, chunks + lags[-1], late_tick, 0)
    for c in range(chunks - slots, chunks):
        rs_copy(c, 0).wait_send()
    for copy in own_sg + own_y + y_moves + moves:
        copy.wait()


def back(seqs, tokens, lengths, vecs, small, head, saved, weights):
    rows, width = saved[0].shape
    ff = 4 * width
    one = rows // seqs
    count = lax.axis_size("seq")
    chunks = 12 * width // CHUNK
    moves = 2 * seqs * (count - 1)
    dma = pltpu.SemaphoreType.DMA
    anywhere = pl.BlockSpec(memory_space=pl.ANY)
    in_vmem = pl.BlockSpec(memory_space=pltpu.VMEM)
    in_smem = pl.BlockSpec(memory_space=pltpu.SMEM)
    block = jax.ShapeDtypeStruct((seqs * count, tokens, width), bf16)
    half = functools.partial(pltpu.VMEM, dtype=bf16)
    total, small, head, lay, grad = pl.pallas_call(
        functools.partial(back_kernel, seqs, chunks, "xy", tuple(1 + 3 * i for i in range(10))),
        out_shape=(
            jax.ShapeDtypeStruct((12 * width, width), bf16),
            jax.ShapeDtypeStruct(small.shape, f32),
            jax.ShapeDtypeStruct((32,) + head.shape, bf16),
            block,
            block,
        ),
        in_specs=[in_smem, in_vmem, in_vmem, in_vmem] + [anywhere] * (len(saved) + len(weights)),
        out_specs=(anywhere, in_vmem, in_vmem, anywhere, anywhere),
        scratch_shapes=[
            pltpu.VMEM((12, rows, width), bf16), pltpu.VMEM((rows, width), f32),
            pltpu.VMEM((rows, 128), f32), pltpu.VMEM((width, ff), bf16),
            pltpu.VMEM((ff, width), bf16),
            pltpu.VMEM((chunks, CHUNK, HALF), bf16),
            pltpu.VMEM((6, CHUNK, HALF), bf16),
            pltpu.VMEM((chunks, CHUNK, HALF), bf16),
            pltpu.VMEM((chunks, CHUNK // 2, HALF), bf16),
            pltpu.VMEM((chunks, CHUNK // 4, HALF), bf16),
            pltpu.VMEM((chunks, CHUNK // 8, HALF), bf16),
            pltpu.VMEM((chunks, CHUNK // 16, HALF), bf16),
            pltpu.VMEM((5,) + small.shape, f32), pltpu.VMEM((seqs, tokens, width), bf16),
            dma((17,)), dma((4, 4)),
            dma((5, chunks)), dma((5, chunks)), dma((5, chunks)), dma((5, chunks)),
            dma((chunks,)), dma((5,)), dma((5,)), dma((5,)), dma((5,)),
            dma((moves,)), dma((moves,)), dma((3 * seqs,)),
        ],
        compiler_params=pltpu.CompilerParams(
            collective_id=0, has_side_effects=True, vmem_limit_bytes=62 * 2**20
        ),
        cost_estimate=pl.CostEstimate(
            flops=8 * rows * width * ff + 16 * rows * width * width + 10 * rows * one * width,
            bytes_accessed=100 * 2**20, transcendentals=12 * rows * one,
        ),
        name="back",
    )(lengths, vecs, small, head, *saved, *weights)
    blocks = lax.axis_size("batch") // 8
    if blocks > 1:
        alike = [[i + 8 * j for j in range(blocks)] for i in range(8)]
        total = lax.psum(total, "batch", axis_index_groups=alike)
        small = lax.psum(small, "batch", axis_index_groups=alike)
        head = lax.all_gather(head, "batch", axis_index_groups=alike, axis=0, tiled=True)
    return total.reshape(12, width, width), small, head, lay, grad


def finish_kernel(
    seqs, total, small_ref, head_ref, vec_ref, pool_ref, lay_in, grad_in,
    lay_out, loss_out, grad_out, gq, gk, gv, go, gqb, gvb, gob, gg1, gb1, gin, gib, gou, gub,
    gg2, gb2, gpool, gpb, gcp, gcb,
    low_s, full_s, pool_s, pass_s, head_s, cls_s, in_sem, out_sem,
):
    units = low_s.shape[0]
    group = loss_out.shape[0]
    places = head_ref.shape[0]
    every = seqs * places
    loads = [pltpu.make_async_copy(total.at[u], low_s.at[u], in_sem.at[u]) for u in range(units)]
    for copy in loads:
        copy.start()
    targets = []
    for j in range(4):
        part = pl.ds(j * WIDTH, WIDTH)
        targets += [gou.at[part], gin.at[:, part]]
    targets += [go, gq, gk, gv]
    stores = [
        pltpu.make_async_copy(full_s.at[u], targets[u], out_sem.at[u]) for u in range(units)
    ]
    passed_in = [
        pltpu.make_async_copy(src, pass_s.at[i], in_sem.at[units + i])
        for i, src in enumerate((lay_in, grad_in))
    ]
    passed = [
        pltpu.make_async_copy(pass_s.at[i], dst, out_sem.at[units + i])
        for i, dst in enumerate((lay_out, grad_out))
    ]
    for copy in passed_in:
        copy.start()
    pool_store = pltpu.make_async_copy(pool_s, gpool, out_sem.at[units + 2])

    def widen(u):
        loads[u].wait()

        @pl.loop(0, WIDTH // 128)
        def _(i):
            r = tile(i, 128)
            full_s[u, r, :] = low_s[u, r, :].astype(f32)

        stores[u].start()

    for u in range(units):
        widen(u)
    for before, after in zip(passed_in, passed):
        before.wait()
        after.start()

    def exact(left, right, dims=NN):
        return lax.dot_general(left, right, dims, precision=highest, preferred_element_type=f32)

    head_s[...] = head_ref[...].astype(f32)
    eye = lax.broadcasted_iota(jnp.int32, (places, places), 0) == lax.broadcasted_iota(
        jnp.int32, (places, places), 1
    )
    label_rows = []
    for s in range(seqs):
        for j in range(6):
            cls_s[s * places : (s + 1) * places, j * 128 : (j + 1) * 128] = head_s[:, s * 6 + j, :]
        column = head_s[:, 6 * seqs, s : s + 1]
        label_rows.append(jnp.sum(jnp.where(eye, column, 0.0), axis=0, keepdims=True))
    cls = cls_s[...].astype(bf16)
    pooled = jnp.tanh(dot(cls, pool_ref[...]) + vec_ref[PB : PB + 1, :])
    row = lax.broadcasted_iota(jnp.int32, (8, 1), 0)
    class_rows = jnp.where(row < 3, vec_ref[CP : CP + 8, :], 0.0)
    picked = jnp.where(
        row == lax.broadcasted_iota(jnp.int32, (8, 128), 1), vec_ref[CB : CB + 1, 0:128], 0.0
    )
    logits = exact(class_rows, pooled, NT) + jnp.sum(picked, axis=-1, keepdims=True)
    logits = jnp.where(row < 3, logits, masked_fill)
    top = jnp.max(logits, axis=0, keepdims=True)
    raised = jnp.exp(logits - top)
    total_row = jnp.sum(raised, axis=0, keepdims=True)
    chosen = jnp.concatenate(
        [(row.astype(f32) == labels).astype(f32) for labels in label_rows], axis=-1
    )
    losses = (top + jnp.log(total_row)) - jnp.sum(
        jnp.where(chosen > 0.0, logits, 0.0), axis=0, keepdims=True
    )
    logit_grad = raised / total_row - chosen
    first = lax.axis_index("batch") * (group // seqs)
    own = lax.broadcasted_iota(jnp.int32, (every, 128), 1)
    pickers = (
        lax.broadcasted_iota(jnp.int32, (every, 128), 0)
        == (own % seqs) * places + first + own // seqs
    ).astype(f32)
    loss_out[...] = exact(losses, pickers)[0, 0:group]
    pre = exact(logit_grad, class_rows, TN) * (1.0 - pooled * pooled)
    ones = jnp.ones((1, every), f32)
    gcb[...] = exact(ones, logit_grad, NT)[0, 0:3]
    gpb[...] = jnp.sum(pre, axis=0)
    gcp[...] = exact(logit_grad, pooled)[0:3, :]
    high = pre.astype(bf16)
    rest = pre - high.astype(f32)
    mid = rest.astype(bf16)
    low = (rest - mid.astype(f32)).astype(bf16)
    for j in range(3):
        cols = pl.ds(j * 256, 256)
        part = cls_s[:, cols].astype(bf16)
        pool_s[cols, :] = dot(part, high, TN) + dot(part, mid, TN) + dot(part, low, TN)
    pool_store.start()
    for i, ref in (
        (QB, gqb), (VB, gvb), (OB, gob), (G1, gg1), (B1, gb1), (UB, gub), (G2, gg2), (B2, gb2),
    ):
        ref[...] = small_ref[i, :]
    for j in range(4):
        gib[j * WIDTH : (j + 1) * WIDTH] = small_ref[IB + j, :]
    for copy in stores + passed + [pool_store]:
        copy.wait()


def finish(seqs, total, small, head, vecs, pool, lay, grad):
    group, tokens, width = lay.shape
    anywhere = pl.BlockSpec(memory_space=pl.ANY)
    in_vmem = pl.BlockSpec(memory_space=pltpu.VMEM)
    square = ((width, width), f32, anywhere)
    row = ((width,), f32, in_vmem)
    outs = (
        [(lay.shape, bf16, anywhere), ((group,), f32, in_vmem), (grad.shape, bf16, anywhere)]
        + [square] * 4
        + [row] * 5
        + [((width, 4 * width), f32, anywhere), ((4 * width,), f32, in_vmem)]
        + [((4 * width, width), f32, anywhere), row, row, row]
        + [square, row, ((3, width), f32, in_vmem), ((3,), f32, in_vmem)]
    )
    units = total.shape[0]
    return pl.pallas_call(
        functools.partial(finish_kernel, seqs),
        out_shape=tuple(jax.ShapeDtypeStruct(s, t) for s, t, _ in outs),
        in_specs=[anywhere] + [in_vmem] * 4 + [anywhere, anywhere],
        out_specs=tuple(m for _, _, m in outs),
        scratch_shapes=[
            pltpu.VMEM((units, width, width), bf16), pltpu.VMEM((units, width, width), f32),
            pltpu.VMEM((width, width), f32), pltpu.VMEM((2,) + lay.shape, bf16),
            pltpu.VMEM(head.shape, f32), pltpu.VMEM((seqs * head.shape[0], width), f32),
            pltpu.SemaphoreType.DMA((units + 2,)), pltpu.SemaphoreType.DMA((units + 3,)),
        ],
        compiler_params=pltpu.CompilerParams(vmem_limit_bytes=60 * 2**20),
        name="finish",
    )(total, small, head, vecs, pool, lay, grad)


def local(
    states, lengths, labels, cotangent,
    query_proj, key_proj, value_proj, output_proj,
    query_bias, value_bias, output_bias, first_gain, first_bias,
    inner_proj, inner_bias, outer_proj, outer_bias, second_gain, second_bias,
    pool_proj, pool_bias, class_proj, class_bias,
):
    group, tokens, width = states.shape
    seqs = group // lax.axis_size("seq")
    vecs, small, head, x, q, k, v, att, n1, low, hid, slope, stat, y, aux, pg = forward(
        lengths, labels, states, cotangent,
        (query_proj, key_proj, value_proj, output_proj, inner_proj, outer_proj, pool_proj),
        (query_bias, value_bias, output_bias, first_gain, first_bias, inner_bias, outer_bias,
         second_gain, second_bias, pool_bias, class_proj.T, class_bias),
    )
    total, small, head, lay, grad = back(
        seqs, tokens, lengths, vecs, small, head,
        (pg, hid, slope, low, n1, stat, y, q, k, v, att, x, aux),
        (inner_proj, outer_proj, query_proj, key_proj, value_proj, output_proj),
    )
    out = finish(seqs, total, small, head, vecs, pool_proj, lay, grad)
    return out[:20] + (out[20].T,) + out[21:]


def solution(mesh):
    split = P("batch", "seq", None)
    in_specs = (split, P("batch"), P("batch"), split) + (P(),) * 19
    out_specs = (split, P("batch"), split) + (P(),) * 19
    return jax.shard_map(local, mesh=mesh, in_specs=in_specs, out_specs=out_specs, check_vma=False)
```
